32 devices in a mesh: dp: 4 (over x, core), fsdp: 8 (over z, y).
Axes of the slice: x: 2, y: 2, z: 4, core: 2. Of those that a mesh axis runs over, the one named last changes fastest.
Arguments:
- tokens: bfloat16 [32768, 768], P(('dp', 'fsdp')), may hold values from -6 to 6
- document_numbers: int32 [64, 512], P(('dp', 'fsdp')), may hold values from 0 to 3, never falling along the last dimension, each value on 1 to 256 neighbouring positions
- query_weight: bfloat16 [768, 768], P(('dp', 'fsdp')), may hold values from -0.21875 to 0.21875
- key_weight: bfloat16 [768, 768], P(('dp', 'fsdp')), may hold values from -0.21875 to 0.21875
- value_weight: bfloat16 [768, 768], P(('dp', 'fsdp')), may hold values from -0.21875 to 0.21875
- output_weight: bfloat16 [768, 768], P(('dp', 'fsdp')), may hold values from -2.5 to 2.5
- inner_weight: bfloat16 [768, 3072], P(('dp', 'fsdp')), may hold values from -0.21875 to 0.21875
- outer_weight: bfloat16 [3072, 768], P(('dp', 'fsdp')), may hold values from -0.109375 to 0.109375
- fixed_projection_bias: bfloat16 [4, 768], P(None, ('dp', 'fsdp')), may hold values from -3 to 3
- feedforward_inner_bias: bfloat16 [3072], P(('dp', 'fsdp')), may hold values from -3 to 3
- layer_norm_gain: bfloat16 [2, 768], P(None, ('dp', 'fsdp')), may hold values from 0.5 to 1.5
- layer_norm_shift: bfloat16 [2, 768], P(None, ('dp', 'fsdp')), may hold values from -2 to 2
- adapter_down_factors: float32 [2, 768, 8], replicated, may hold values from -0.21875 to 0.21875
- adapter_up_factors: float32 [2, 8, 768], replicated, may hold values from -0.6 to 0.6
- down_first_moment: float32 [2, 768, 8], replicated, may hold values from -3 to 3
- down_second_moment: float32 [2, 768, 8], replicated, may hold values from 0.05 to 2
- up_first_moment: float32 [2, 8, 768], replicated, may hold values from -3 to 3
- up_second_moment: float32 [2, 8, 768], replicated, may hold values from 0.005 to 0.2
- rate: float32 [1], replicated, may hold values from 0.001 to 0.01
- step: int32 [1], replicated, may hold values from 10 to 999
- cotangent: bfloat16 [32768, 768], P(('dp', 'fsdp')), may hold values from -6 to 6
Outputs:
- activations: bfloat16 [32768, 768], P(('dp', 'fsdp'))
- input_grad: float32 [32768, 768], P(('dp', 'fsdp'))
- down_gradient: float32 [2, 768, 8], replicated
- up_gradient: float32 [2, 8, 768], replicated
- gain_grad: float32 [2, 768], replicated
- shift_grad: float32 [2, 768], replicated
- updated_down_factors: float32 [2, 768, 8], replicated
- updated_up_factors: float32 [2, 8, 768], replicated
- updated_down_first_moment: float32 [2, 768, 8], replicated
- updated_down_second_moment: float32 [2, 768, 8], replicated
- updated_up_first_moment: float32 [2, 8, 768], replicated
- updated_up_second_moment: float32 [2, 8, 768], replicated
The draws below stay inside these ranges and needn't reach their ends.
Inputs may be any that keep to these rules, and one draw needn't show every extreme that they name: `document_numbers`: within a row of 512 positions the numbers never fall.
All inputs are finite; a program needn't handle non-finite values.
Results may differ from the reference program's by a relative error of at most 0.015.
The reference program's roundings to bfloat16 on the way count: a program that leaves them out, or rounds other values in their place, can miss the bound.
Values may be sent and summed in bfloat16 or wider, within the bound.
No kernel may reach another device: no remote copies, remote signals or barrier semaphores. Data moves between devices by JAX's collectives and lax.ppermute only.
A program may use at most 128 MiB of HBM per device.

```python
import math
import jax
import jax.numpy as jnp
import numpy as np
from jax import lax

MODEL_WIDTH = 768
HEADS = 12
HEAD = 64
FF = 3072
ADAPTER_RANK = 8
PACK = 512
DOCS = 4
SEQS = 64
TOKENS = 32768
N_DP = 4
N_FSDP = 8


def block_scale(own_key, shape, split, smallest, largest):
    loudness, own = 1.0, jax.random.fold_in(own_key, 6)
    for axis_at, shards_of in split:
        heights = jnp.exp(jax.random.uniform(jax.random.fold_in(own, axis_at), (shards_of,), jnp.float32, smallest / len(split), largest / len(split)))
        loudness = loudness * jnp.repeat(heights, shape[axis_at] // shards_of).reshape([-1 if axis == axis_at else 1 for axis in range(len(shape))])
    return loudness


def length_profile(amount, total, bound, skew):
    portions = [(1 << 20) // math.isqrt(standing ** skew) + 1 for standing in range(2, amount + 1)]
    surplus, counts = total - bound - (amount - 1), [1] * (amount - 1)
    while surplus > 0:
        candidates = [i for i in range(amount - 1) if counts[i] < bound]
        whole, budget = sum([portions[i] for i in candidates]), surplus
        for i in candidates:
            more = min(bound - counts[i], max(1, budget * portions[i] // whole), surplus)
            counts[i] = counts[i] + more
            surplus = surplus - more
    return np.array([bound] + counts)


def ragged(rng, amount, total, reach, lean):
    if amount == 2:
        one = jax.random.randint(rng, (), max(1, total - reach), min(reach, total - 1) + 1)
        return jnp.stack([one, total - one])
    sizes = jnp.asarray(length_profile(amount, total, reach, lean), jnp.int32)
    pairs = (amount - 1) // 2
    donor, sink = sizes[1:1 + 2 * pairs:2], sizes[2:2 + 2 * pairs:2]
    room = jnp.minimum(donor - 1, reach - sink)
    shifted = jax.random.randint(jax.random.fold_in(rng, 1), (pairs,), 0, 1 << 20) % (room + 1)
    sizes = sizes.at[1:1 + 2 * pairs:2].set(donor - shifted).at[2:2 + 2 * pairs:2].set(sink + shifted)
    return sizes[jax.random.permutation(jax.random.fold_in(rng, 2), amount)]


def normal_values(stream_key, shape, spread, limit, shards=(), dtype=jnp.bfloat16):
    values = jax.random.normal(stream_key, shape, jnp.float32) * spread
    if len(shards) > 0:
        values = block_scale(stream_key, shape, shards, -0.22, 0.18) * values
    return jnp.clip(values, min=-limit, max=limit).astype(dtype)


def setup_inputs(seed: int = 0) -> dict:
    key_of = jax.random.split(jax.random.key(seed), 22)
    tokens = normal_values(key_of[0], (TOKENS, MODEL_WIDTH), 1.0, 6.0, ((0, 32),))
    document_numbers = jax.vmap(lambda own: jnp.searchsorted(jnp.cumsum(ragged(own, DOCS, PACK, PACK // 2, 1)), jnp.arange(PACK), side="right"))(jax.random.split(key_of[1], SEQS)).reshape((SEQS, PACK)).astype(jnp.int32)
    query_weight = normal_values(key_of[2], (MODEL_WIDTH, MODEL_WIDTH), MODEL_WIDTH ** -0.5, 0.21875, ((0, 32),))
    key_weight = normal_values(key_of[3], (MODEL_WIDTH, MODEL_WIDTH), MODEL_WIDTH ** -0.5, 0.21875, ((0, 32),))
    value_weight = normal_values(key_of[4], (MODEL_WIDTH, MODEL_WIDTH), MODEL_WIDTH ** -0.5, 0.21875, ((0, 32),))
    output_weight = normal_values(key_of[5], (MODEL_WIDTH, MODEL_WIDTH), (MODEL_WIDTH * DOCS // PACK) ** -0.5, 2.5, ((0, 32),))
    inner_weight = normal_values(key_of[6], (MODEL_WIDTH, FF), MODEL_WIDTH ** -0.5, 0.21875, ((0, 32),))
    outer_weight = normal_values(key_of[7], (FF, MODEL_WIDTH), FF ** -0.5, 0.109375, ((0, 32),))
    fixed_projection_bias = normal_values(key_of[8], (4, MODEL_WIDTH), 0.5, 3.0, ((1, 32),))
    feedforward_inner_bias = normal_values(key_of[9], (FF,), 0.5, 3.0, ((0, 32),))
    layer_norm_gain = jnp.clip(1.0 + 0.1 * jax.random.normal(key_of[10], (2, MODEL_WIDTH), jnp.float32), 0.5, 1.5).astype(jnp.bfloat16)
    layer_norm_shift = normal_values(key_of[11], (2, MODEL_WIDTH), 0.3, 2.0, ((1, 32),))
    adapter_down_factors = normal_values(key_of[12], (2, MODEL_WIDTH, ADAPTER_RANK), MODEL_WIDTH ** -0.5, 0.21875, (), jnp.float32)
    adapter_up_factors = normal_values(key_of[13], (2, ADAPTER_RANK, MODEL_WIDTH), 0.1, 0.6, (), jnp.float32)
    down_first_moment = normal_values(key_of[14], (2, MODEL_WIDTH, ADAPTER_RANK), 0.5, 3.0, (), jnp.float32)
    down_second_moment = jnp.clip(jnp.exp(jax.random.uniform(key_of[15], (2, MODEL_WIDTH, ADAPTER_RANK), jnp.float32, math.log(0.05), math.log(2.0))), 0.05, 2.0)
    up_first_moment = normal_values(key_of[16], (2, ADAPTER_RANK, MODEL_WIDTH), 0.5, 3.0, (), jnp.float32)
    up_second_moment = jnp.clip(jnp.exp(jax.random.uniform(key_of[17], (2, ADAPTER_RANK, MODEL_WIDTH), jnp.float32, math.log(0.005), math.log(0.2))), 0.005, 0.2)
    rate = jnp.clip(jnp.exp(jax.random.uniform(key_of[18], (1,), jnp.float32, math.log(0.001), math.log(0.01))), 0.001, 0.01)
    step = jax.random.randint(key_of[19], (1,), 10, 1000).astype(jnp.int32)
    cotangent = normal_values(key_of[20], (TOKENS, MODEL_WIDTH), 1.0, 6.0, ((0, 32),))
    return dict(tokens=tokens, document_numbers=document_numbers, query_weight=query_weight, key_weight=key_weight, value_weight=value_weight, output_weight=output_weight, inner_weight=inner_weight, outer_weight=outer_weight, fixed_projection_bias=fixed_projection_bias, feedforward_inner_bias=feedforward_inner_bias, layer_norm_gain=layer_norm_gain, layer_norm_shift=layer_norm_shift, adapter_down_factors=adapter_down_factors, adapter_up_factors=adapter_up_factors, down_first_moment=down_first_moment, down_second_moment=down_second_moment, up_first_moment=up_first_moment, up_second_moment=up_second_moment, rate=rate, step=step, cotangent=cotangent)


@jax.custom_vjp
def low(v):
    return lax.optimization_barrier(v.astype(jnp.bfloat16)).astype(jnp.float32)

@jax.custom_vjp
def low_back(v):
    return v

def low_keep(v):
    return (low(v), None)

def low_pass(kept, grad):
    return (grad,)

def back_keep(v):
    return (v, None)

def back_low(kept, grad):
    return (low(grad),)
low.defvjp(low_keep, low_pass)
low_back.defvjp(back_keep, back_low)
highest = lax.Precision.HIGHEST
beta_one = 0.9
beta_two = 0.999
adam_epsilon = 1e-08
down_decay_factor = 0.05
up_decay_factor = 0.01
norm_epsilon = 1e-05
masked_score = -1e+30
group_packs = 8

def product(left, right):
    return jnp.dot(left, right, precision=highest, preferred_element_type=jnp.float32)

def layer_norm(value, gain, shift):
    centred = value - lax.optimization_barrier(jnp.mean(value, axis=-1, keepdims=True))
    variance = lax.optimization_barrier(jnp.mean(centred * centred, axis=-1, keepdims=True))
    return centred * lax.rsqrt(variance + norm_epsilon) * gain + shift

def attend_pack(items):
    query, key_rows, value_rows, segment = items
    length = query.shape[0]
    query_heads = query.reshape(length, HEADS, HEAD)
    key_heads = key_rows.reshape(length, HEADS, HEAD)
    value_heads = value_rows.reshape(length, HEADS, HEAD)
    scores = jnp.einsum('qhd,khd->hqk', query_heads, key_heads, precision=highest) * HEAD ** (-0.5)
    scores = low_back(scores)
    same = segment[:, None] == segment[None, :]
    scores = jnp.where(same[None, :, :], scores, masked_score)
    weights = low(jax.nn.softmax(scores, axis=-1))
    context = jnp.einsum('hqk,khd->qhd', weights, value_heads, precision=highest)
    return context.reshape(length, HEADS * HEAD)

def forward(input_rows, down, up, norm_gains, norm_shifts, frozen, segments):
    query_weight, key_weight, value_weight, output_weight, inner_weight, outer_weight, fixed_projection_bias, feedforward_inner_bias = frozen
    down_adapter_factor = low(down)
    up_adapter_factor = low(up)
    joined = jnp.concatenate([down_adapter_factor[0], down_adapter_factor[1]], axis=1)
    reduced = low_back(low(product(input_rows, joined)))
    query = product(input_rows, query_weight) + fixed_projection_bias[0] + 2.0 * product(reduced[:, :ADAPTER_RANK], up_adapter_factor[0])
    query = low_back(low(query))
    key_rows = low_back(low(product(input_rows, key_weight)))
    value_rows = product(input_rows, value_weight) + fixed_projection_bias[1] + 2.0 * product(reduced[:, ADAPTER_RANK:], up_adapter_factor[1])
    value_rows = low_back(low(value_rows))
    packs = input_rows.shape[0] // PACK
    context = lax.map(jax.checkpoint(attend_pack), (query.reshape(packs, PACK, MODEL_WIDTH), key_rows.reshape(packs, PACK, MODEL_WIDTH), value_rows.reshape(packs, PACK, MODEL_WIDTH), segments))
    context = low_back(low(context.reshape(packs * PACK, MODEL_WIDTH)))
    attended = low_back(product(context, output_weight) + fixed_projection_bias[2])
    first = layer_norm(input_rows + attended, norm_gains[0], norm_shifts[0])
    inner = low_back(product(low(first), inner_weight) + feedforward_inner_bias)
    activated = low(jax.nn.gelu(inner, approximate=False))
    outer = low_back(product(activated, outer_weight) + fixed_projection_bias[3])
    return layer_norm(first + outer, norm_gains[1], norm_shifts[1])

def adamw_update(param, grad, first, second, learning_step_rate, decay, step_counter):
    first_new = beta_one * first + (1.0 - beta_one) * grad
    second_new = beta_two * second + (1.0 - beta_two) * grad * grad
    first_hat = first_new / (1.0 - beta_one ** step_counter)
    second_hat = second_new / (1.0 - beta_two ** step_counter)
    param_new = param - learning_step_rate * (first_hat / (jnp.sqrt(second_hat) + adam_epsilon) + decay * param)
    return (param_new, first_new, second_new)

def reference(tokens, document_numbers, query_weight, key_weight, value_weight, output_weight, inner_weight, outer_weight, fixed_projection_bias, feedforward_inner_bias, layer_norm_gain, layer_norm_shift, adapter_down_factors, adapter_up_factors, down_first_moment, down_second_moment, up_first_moment, up_second_moment, rate, step, cotangent):
    frozen = tuple((array.astype(jnp.float32) for array in (query_weight, key_weight, value_weight, output_weight, inner_weight, outer_weight, fixed_projection_bias, feedforward_inner_bias)))
    norm_gains = layer_norm_gain.astype(jnp.float32)
    norm_shifts = layer_norm_shift.astype(jnp.float32)
    groups = SEQS // group_packs
    rows = group_packs * PACK
    token_groups = tokens.astype(jnp.float32).reshape(groups, rows, MODEL_WIDTH)
    cotangent_groups = cotangent.astype(jnp.float32).reshape(groups, rows, MODEL_WIDTH)
    segment_groups = document_numbers.reshape(groups, group_packs, PACK)

    def one_group(totals, items):
        input_rows, segments, cotangents = items

        def execute_layer(group_inputs, down, up, gain_rows, shift_rows):
            return forward(group_inputs, down, up, gain_rows, shift_rows, frozen, segments)
        layer_result, backward_map = jax.vjp(execute_layer, input_rows, adapter_down_factors, adapter_up_factors, norm_gains, norm_shifts)
        grads = backward_map(cotangents)
        totals = tuple((total + grad for total, grad in zip(totals, grads[1:])))
        return (totals, (layer_result.astype(jnp.bfloat16), grads[0]))
    start_offset = (jnp.zeros_like(adapter_down_factors), jnp.zeros_like(adapter_up_factors), jnp.zeros_like(norm_gains), jnp.zeros_like(norm_shifts))
    totals, (results, input_grads) = lax.scan(one_group, start_offset, (token_groups, segment_groups, cotangent_groups))
    count = N_DP * N_FSDP
    down_gradient = totals[0] / count
    up_gradient = totals[1] / count
    gain_grad = totals[2] / count
    shift_grad = totals[3] / count
    step_counter = step[0].astype(jnp.float32)
    updated_down_factors, updated_down_first_moment, updated_down_second_moment = adamw_update(adapter_down_factors, down_gradient, down_first_moment, down_second_moment, rate[0], down_decay_factor, step_counter)
    updated_up_factors, updated_up_first_moment, updated_up_second_moment = adamw_update(adapter_up_factors, up_gradient, up_first_moment, up_second_moment, 16.0 * rate[0], up_decay_factor, step_counter)
    activations = results.reshape(TOKENS, MODEL_WIDTH)
    input_grad = input_grads.reshape(TOKENS, MODEL_WIDTH)
    return (activations, input_grad, down_gradient, up_gradient, gain_grad, shift_grad, updated_down_factors, updated_up_factors, updated_down_first_moment, updated_down_second_moment, updated_up_first_moment, updated_up_second_moment)
```

```python
import functools
import math

import jax
import jax.numpy as jnp
import numpy as np
from jax import lax
from jax.experimental import pallas as pl
from jax.experimental.pallas import tpu as pltpu
from jax.sharding import PartitionSpec as P

HEAD = 64
AXES = ("dp", "fsdp")

beta_one = 0.9
beta_two = 0.999
adam_epsilon = 1e-08
down_decay_factor = 0.05
up_decay_factor = 0.01
norm_epsilon = 1e-05
masked_score = -1e30
root_circle = 1.0 / math.sqrt(2.0 * math.pi)
LANES = 128
MIB = 1 << 20

f32 = jnp.float32
bf16 = jnp.bfloat16


def nn(a, b):
    return lax.dot_general(a, b, (((1,), (0,)), ((), ())), preferred_element_type=f32)


def nt(a, b):
    return lax.dot_general(a, b, (((1,), (1,)), ((), ())), preferred_element_type=f32)


class Layout:
    def __init__(self, mesh):
        n_dp, n_fsdp = mesh.shape["dp"], mesh.shape["fsdp"]
        self.n = n_dp * n_fsdp
        self.core = n_fsdp
        n_x = n_dp // 2
        n_y = n_x
        y_bits = [1 << t for t in range(int(math.log2(n_y)))]
        z_bits = [n_y << t for t in range(int(math.log2(n_fsdp // n_y)))]
        x_bits = [(2 * n_fsdp) << t for t in range(int(math.log2(n_x)))]
        self.orders = (z_bits + x_bits + y_bits, z_bits[::-1] + y_bits + x_bits)
        self.bits = y_bits + z_bits + x_bits + [self.core]

    def order_of(self, i):
        return self.orders[1 if i & self.core else 0]

    def stage_pairs(self, t):
        return [(i, i ^ self.order_of(i)[t]) for i in range(self.n)]

    def core_pairs(self):
        return [(i, i ^ self.core) for i in range(self.n)]

    def block_masks(self, order):
        masks = [0]
        for bit in order:
            masks = masks + [m ^ bit for m in masks]
        return masks


def gather_blocks(block, layout):
    held = block[None]
    stages = len(layout.orders[0])
    for t in range(stages):
        came = lax.ppermute(held, AXES, layout.stage_pairs(t))
        if t < stages - 1:
            held = jnp.concatenate([held, came], axis=0)
    return (
        held,
        came,
        lax.ppermute(held, AXES, layout.core_pairs()),
        lax.ppermute(came, AXES, layout.core_pairs()),
    )


def block_ids(layout):
    me = lax.axis_index(AXES).astype(jnp.int32)
    one, two = (np.array(layout.block_masks(o), np.int32) for o in layout.orders)
    second = (me & layout.core) != 0
    own = me ^ jnp.where(second, two, one)
    other = me ^ layout.core ^ jnp.where(second, one, two)
    return jnp.concatenate([own, other])


def as_blocks(full, count):
    return tuple(
        part for part in full.reshape((4, count // 4) + (full.shape[0] // count,) + full.shape[1:])
    )


def fetch_blocks(ids_ref, parts, stage, sems):
    each = parts[0].shape[0]
    for a, part in enumerate(parts):
        for j in range(each):
            k = a * each + j
            at = ids_ref[k]
            pltpu.make_async_copy(part.at[j], stage.at[at], sems.at[at]).start()


def wait_block(parts, stage, sems, i):
    pltpu.make_async_copy(parts[0].at[0], stage.at[i], sems.at[i]).wait()


def merge_pairs(parts, stage, sems, target, width, extra=None):
    shards, rows = stage.shape[0], stage.shape[1]
    for i in range(0, shards, 2):
        wait_block(parts, stage, sems, i)
        wait_block(parts, stage, sems, i + 1)
        for c in range(0, width, 768):
            low = stage[i, :, c : c + 768].astype(f32)
            high = stage[i + 1, :, c : c + 768].astype(f32)
            target[rows * i : rows * (i + 2), c : c + 768] = jnp.concatenate(
                [low, high], axis=0
            ).astype(bf16)


def spread(piece, width, step, count):
    lane = lax.broadcasted_iota(jnp.int32, (LANES, width), 1).astype(f32)
    slot = lax.broadcasted_iota(jnp.int32, (LANES, width), 0).astype(f32)
    within = lane - step * jnp.floor((lane + 0.5) * (1.0 / step))
    place = (within == slot).astype(bf16)
    wide = nn(piece.astype(bf16), place)
    at = lax.broadcasted_iota(jnp.int32, (8, width), 1)
    total = jnp.zeros((8, width), f32)
    for i in range(count):
        mine = (at >= step * i) & (at < step * (i + 1))
        total = total + jnp.where(mine, wide[8 * i : 8 * (i + 1)], 0.0)
    return total


def project_kernel(ids_ref, x_ref, down_ref, up_ref, p0, p1, p2, p3, qkv_ref, weight_ref, red_ref,
                   small_ref, inner_bias_ref, stage, sems):
    parts = (p0, p1, p2, p3)
    width = x_ref.shape[1]
    rank = down_ref.shape[1]

    @pl.when(pl.program_id(0) == 0)
    def _():
        fetch_blocks(ids_ref, parts, stage, sems)
        merge_pairs(parts, stage, sems, weight_ref, 3 * width)
        shards, rows = stage.shape[0], stage.shape[1]
        tail = stage[:, :, 3 * width :].astype(f32)
        small_ref[...] = spread(tail[:, 0:8].reshape(8 * shards, LANES), width, rows, shards)
        ff = inner_bias_ref.shape[1]
        inner_bias_ref[...] = spread(
            tail[:, 8:16].reshape(8 * shards, LANES), ff, ff // shards, shards
        )

    x = x_ref[...]
    down = down_ref[...].reshape(2 * rank, width).astype(bf16)
    up = (2.0 * up_ref[...].astype(bf16).astype(f32)).astype(bf16)
    zero = jnp.zeros((rank, width), bf16)
    reduced = nt(x, down).astype(bf16)
    red_ref[...] = nt(down, x).astype(bf16)
    up_query = jnp.concatenate([up[0], zero], axis=0)
    up_value = jnp.concatenate([zero, up[1]], axis=0)
    chunk = 256
    for c in range(0, 3 * width, chunk):
        y = nn(x, weight_ref[:, c : c + chunk])
        o = c % width
        if c < width:
            y = y + small_ref[0:1, o : o + chunk] + nn(reduced, up_query[:, o : o + chunk])
        elif c >= 2 * width:
            y = y + small_ref[1:2, o : o + chunk] + nn(reduced, up_value[:, o : o + chunk])
        qkv_ref[:, c : c + chunk] = y.astype(bf16)


def project(ids, tokens, down, up, parts):
    rows, width = tokens.shape
    shards = 4 * parts[0].shape[0]
    shard_rows = parts[0].shape[1]
    ff = 4 * width
    tile = 256
    whole = lambda *shape: pl.BlockSpec(shape, lambda i: (0,) * len(shape))
    return pl.pallas_call(
        project_kernel,
        grid=(rows // tile,),
        in_specs=[
            pl.BlockSpec(memory_space=pltpu.SMEM),
            pl.BlockSpec((tile, width), lambda i: (i, 0)),
            whole(*down.shape),
            whole(*up.shape),
        ]
        + [pl.BlockSpec(memory_space=pl.ANY)] * 4,
        out_specs=[
            pl.BlockSpec((tile, 3 * width), lambda i: (i, 0)),
            whole(width, 3 * width),
            pl.BlockSpec((2 * down.shape[1], tile), lambda i: (0, i)),
            whole(8, width),
            whole(8, ff),
        ],
        out_shape=[
            jax.ShapeDtypeStruct((rows, 3 * width), bf16),
            jax.ShapeDtypeStruct((width, 3 * width), bf16),
            jax.ShapeDtypeStruct((2 * down.shape[1], rows), bf16),
            jax.ShapeDtypeStruct((8, width), f32),
            jax.ShapeDtypeStruct((8, ff), f32),
        ],
        scratch_shapes=[
            pltpu.VMEM((shards, shard_rows, 3 * width + LANES), bf16),
            pltpu.SemaphoreType.DMA((shards,)),
        ],
        compiler_params=pltpu.CompilerParams(vmem_limit_bytes=40 * MIB),
        cost_estimate=pl.CostEstimate(
            flops=2 * rows * width * width * 3, bytes_accessed=14 * MIB, transcendentals=0
        ),
    )(ids, tokens, down, up, *parts)


def attend_kernel(seg_ref, q_ref, k_ref, v_ref, ctx_ref, w_ref, mask):
    pack, rows = seg_ref.shape[1], seg_ref.shape[1]

    @pl.when(pl.program_id(1) == 0)
    def _():
        row = jnp.broadcast_to(seg_ref[pl.ds(pl.program_id(0), 1), :].astype(f32), (8, rows))
        column = row.T[:, 0:1]
        mask[...] = jnp.where(column == row[0:1], 0.0, masked_score)

    lane = lax.broadcasted_iota(jnp.int32, (1, LANES), 1)
    for s in range(q_ref.shape[1] // LANES):
        cols = slice(s * LANES, (s + 1) * LANES)
        q = q_ref[:, cols] * jnp.asarray(HEAD**-0.5, bf16)
        k = k_ref[:, cols]
        v = v_ref[:, cols]
        ctx = None
        for h in range(2):
            mine = (lane < HEAD) if h == 0 else (lane >= HEAD)
            scores = nt(jnp.where(mine, q, jnp.zeros_like(q)), k) + mask[...]
            peak = jnp.max(scores, axis=-1, keepdims=True)
            exponent = jnp.exp(scores - peak)
            total = jnp.sum(exponent, axis=-1, keepdims=True)
            weights = (exponent * (1.0 / total)).astype(bf16)
            w_ref[2 * s + h] = weights
            part = nn(weights, jnp.where(mine, v, jnp.zeros_like(v)))
            ctx = part if ctx is None else ctx + part
        ctx_ref[:, cols] = ctx.astype(bf16)


HEADS_A_STEP = 4


def attend(segments, qkv):
    packs, length = segments.shape
    rows, wide = qkv.shape
    width = wide // 3
    step = HEADS_A_STEP * HEAD
    steps = width // step
    at = lambda which: pl.BlockSpec((length, step), lambda p, s: (p, which * steps + s))
    return pl.pallas_call(
        attend_kernel,
        grid=(packs, steps),
        in_specs=[pl.BlockSpec((packs, length), lambda p, s: (0, 0)), at(0), at(1), at(2)],
        out_specs=[
            pl.BlockSpec((length, step), lambda p, s: (p, s)),
            pl.BlockSpec((HEADS_A_STEP, length, length), lambda p, s: (p * steps + s, 0, 0)),
        ],
        out_shape=[
            jax.ShapeDtypeStruct((rows, width), bf16),
            jax.ShapeDtypeStruct((packs * width // HEAD, length, length), bf16),
        ],
        scratch_shapes=[pltpu.VMEM((length, length), f32)],
        compiler_params=pltpu.CompilerParams(vmem_limit_bytes=40 * MIB),
        cost_estimate=pl.CostEstimate(
            flops=16 * rows * length * width, bytes_accessed=20 * MIB, transcendentals=rows * length * 12
        ),
    )(segments, qkv, qkv, qkv)


def stats(value):
    centred = value - jnp.mean(value, axis=-1, keepdims=True)
    inverse = lax.rsqrt(jnp.mean(centred * centred, axis=-1, keepdims=True) + norm_epsilon)
    return centred * inverse, inverse


def norm_back(grad, normed, inverse, gain):
    scaled = grad * gain
    return inverse * (
        scaled
        - jnp.mean(scaled, axis=-1, keepdims=True)
        - normed * jnp.mean(scaled * normed, axis=-1, keepdims=True)
    )


def gelu_parts(z):
    size = jnp.abs(z)
    t = 1.0 / (1.0 + 0.2316419 * size)
    density = jnp.exp(z * z * -0.5) * root_circle
    poly = t * (
        0.319381530
        + t * (-0.356563782 + t * (1.781477937 + t * (-1.821255978 + t * 1.330274429)))
    )
    tail = density * poly
    cumulative = jnp.where(z >= 0.0, 1.0 - tail, tail)
    return z * cumulative, cumulative + z * density


def rows_kernel(ids_ref, x_ref, cot_ref, ctx_ref, small_ref, inner_bias_ref, b0, b1, b2, b3, d0, d1, d2, d3,
                act_ref, mid_ref, dctx_ref, sums_ref,
                stage, wo, wi, wf, active, slope, sem_b, sem_d):
    parts_b, parts_d = (b0, b1, b2, b3), (d0, d1, d2, d3)
    width = x_ref.shape[1]
    ff = wi.shape[1]
    shard = d0.shape[1]

    @pl.when(pl.program_id(0) == 0)
    def _():
        fetch_blocks(ids_ref, parts_b, stage, sem_b)
        each = d0.shape[0]
        for a, part in enumerate(parts_d):
            for j in range(each):
                at = ids_ref[a * each + j]
                pltpu.make_async_copy(
                    part.at[j], wf.at[pl.ds(pl.multiple_of(at * shard, shard), shard)], sem_d.at[at]
                ).start()
        shards, rows = stage.shape[0], stage.shape[1]
        for i in range(0, shards, 2):
            wait_block(parts_b, stage, sem_b, i)
            wait_block(parts_b, stage, sem_b, i + 1)
            for c in range(0, width + ff, width):
                both = jnp.concatenate(
                    [
                        stage[i, :, c : c + width].astype(f32),
                        stage[i + 1, :, c : c + width].astype(f32),
                    ],
                    axis=0,
                ).astype(bf16)
                where = slice(rows * i, rows * (i + 2))
                if c == 0:
                    wo[where] = both
                else:
                    wi[where, c - width : c] = both
        for i in range(shards):
            pltpu.make_async_copy(d0.at[0], wf.at[pl.ds(i * shard, shard)], sem_d.at[i]).wait()
        sums_ref[...] = jnp.zeros_like(sums_ref)

    bias_out, bias_ff = small_ref[2:3], small_ref[3:4]
    gain_one, gain_two = small_ref[4:5], small_ref[5:6]
    shift_one, shift_two = small_ref[6:7], small_ref[7:8]
    chunk = 512
    normed_one, inverse_one = stats(x_ref[...].astype(f32) + (nn(ctx_ref[...], wo[...]) + bias_out))
    first = normed_one * gain_one + shift_one
    first_b = first.astype(bf16)
    outer = None
    for c in range(0, ff, chunk):
        cols = slice(c, c + chunk)
        inner = nn(first_b, wi[:, cols]) + inner_bias_ref[0:1, cols]
        value, grad = gelu_parts(inner)
        active[:, cols] = value.astype(bf16)
        slope[:, cols] = grad.astype(bf16)
    outer = nn(active[...], wf[...]) + bias_ff
    normed_two, inverse_two = stats(first + outer)
    act_ref[...] = (normed_two * gain_two + shift_two).astype(bf16)
    grad_out = cot_ref[...].astype(f32)
    grad_gain_two = jnp.sum(grad_out * normed_two, axis=0, keepdims=True)
    grad_shift_two = jnp.sum(grad_out, axis=0, keepdims=True)
    grad_res = norm_back(grad_out, normed_two, inverse_two, gain_two)
    grad_outer = grad_res.astype(bf16)
    for c in range(0, ff, chunk):
        cols = slice(c, c + chunk)
        grad_active = nt(grad_outer, wf[cols])
        active[:, cols] = (grad_active * slope[:, cols].astype(f32)).astype(bf16)
    grad_first = grad_res + nt(active[...], wi[...])
    grad_gain_one = jnp.sum(grad_first * normed_one, axis=0, keepdims=True)
    grad_shift_one = jnp.sum(grad_first, axis=0, keepdims=True)
    sums_ref[0:4] += jnp.concatenate(
        [grad_gain_one, grad_gain_two, grad_shift_one, grad_shift_two], axis=0
    )
    grad_mid = norm_back(grad_first, normed_one, inverse_one, gain_one)
    mid_ref[...] = grad_mid
    dctx_ref[...] = nt(grad_mid.astype(bf16), wo[...]).astype(bf16)


def row_local(ids, tokens, cotangent, context, small, inner_bias, parts_b, parts_d):
    rows, width = tokens.shape
    ff = inner_bias.shape[1]
    shards = 4 * parts_b[0].shape[0]
    tile = 256
    whole = lambda *shape: pl.BlockSpec(shape, lambda i: (0,) * len(shape))
    tiled = pl.BlockSpec((tile, width), lambda i: (i, 0))
    return pl.pallas_call(
        rows_kernel,
        grid=(rows // tile,),
        in_specs=[pl.BlockSpec(memory_space=pltpu.SMEM), tiled, tiled, tiled, whole(8, width), whole(8, ff)]
        + [pl.BlockSpec(memory_space=pl.ANY)] * 8,
        out_specs=[tiled, tiled, tiled, whole(8, width)],
        out_shape=[
            jax.ShapeDtypeStruct((rows, width), bf16),
            jax.ShapeDtypeStruct((rows, width), f32),
            jax.ShapeDtypeStruct((rows, width), bf16),
            jax.ShapeDtypeStruct((8, width), f32),
        ],
        scratch_shapes=[
            pltpu.VMEM((shards,) + parts_b[0].shape[1:], bf16),
            pltpu.VMEM((width, width), bf16),
            pltpu.VMEM((width, ff), bf16),
            pltpu.VMEM((ff, width), bf16),
            pltpu.VMEM((tile, ff), bf16),
            pltpu.VMEM((tile, ff), bf16),
            pltpu.SemaphoreType.DMA((shards,)),
            pltpu.SemaphoreType.DMA((shards,)),
        ],
        compiler_params=pltpu.CompilerParams(vmem_limit_bytes=56 * MIB),
        cost_estimate=pl.CostEstimate(
            flops=2 * rows * width * (4 * ff + 2 * width), bytes_accessed=20 * MIB, transcendentals=0
        ),
    )(ids, tokens, cotangent, context, small, inner_bias, *parts_b, *parts_d)


def attend_back_kernel(q_ref, k_ref, v_ref, ctx_ref, dctx_ref, w_ref, dq_ref, dk_ref, dv_ref):
    scale = HEAD**-0.5
    lane = lax.broadcasted_iota(jnp.int32, (1, LANES), 1)
    for s in range(q_ref.shape[1] // LANES):
        cols = slice(s * LANES, (s + 1) * LANES)
        q, k, v = q_ref[:, cols], k_ref[:, cols], v_ref[:, cols]
        dctx = dctx_ref[:, cols]
        flat = dctx.astype(f32) * ctx_ref[:, cols].astype(f32)
        q_t = q.T
        dctx_t = dctx.T
        dq = None
        dk_t, dv_t = [], []
        for h in range(2):
            mine = (lane < HEAD) if h == 0 else (lane >= HEAD)
            zero = jnp.zeros_like(q)
            grad_weights = nt(jnp.where(mine, dctx, zero), v)
            delta = jnp.sum(jnp.where(mine, flat, 0.0), axis=-1, keepdims=True)
            weights = w_ref[2 * s + h]
            grad_scores = (weights.astype(f32) * (grad_weights - delta)).astype(bf16)
            part = nn(grad_scores, jnp.where(mine, k, zero))
            dq = part if dq is None else dq + part
            rows = slice(h * HEAD, (h + 1) * HEAD)
            dk_t.append(nn(q_t[rows], grad_scores))
            dv_t.append(nn(dctx_t[rows], weights))
        dq_ref[:, cols] = (dq * scale).astype(bf16)
        dk_ref[:, cols] = (jnp.concatenate(dk_t, axis=0) * scale).T.astype(bf16)
        dv_ref[:, cols] = jnp.concatenate(dv_t, axis=0).T.astype(bf16)


def attend_back(qkv, context, grad_context, weights):
    rows, width = context.shape
    length = weights.shape[1]
    packs = rows // length
    step = HEADS_A_STEP * HEAD
    steps = width // step
    at = lambda which: pl.BlockSpec((length, step), lambda p, s: (p, which * steps + s))
    flat = pl.BlockSpec((length, step), lambda p, s: (p, s))
    return pl.pallas_call(
        attend_back_kernel,
        grid=(packs, steps),
        in_specs=[
            at(0),
            at(1),
            at(2),
            flat,
            flat,
            pl.BlockSpec((HEADS_A_STEP, length, length), lambda p, s: (p * steps + s, 0, 0)),
        ],
        out_specs=[flat] * 3,
        out_shape=[jax.ShapeDtypeStruct((rows, width), bf16)] * 3,
        compiler_params=pltpu.CompilerParams(vmem_limit_bytes=40 * MIB),
        cost_estimate=pl.CostEstimate(
            flops=32 * rows * length * width, bytes_accessed=24 * MIB, transcendentals=0
        ),
    )(qkv, qkv, qkv, context, grad_context, weights)


def adapter_kernel(x_ref, dq_ref, dv_ref, up_ref, red_ref, sums_ref, dred_ref, grads_ref):
    rank = up_ref.shape[1]
    up = (2.0 * up_ref[...].astype(bf16).astype(f32)).astype(bf16)
    dq, dv = dq_ref[...], dv_ref[...]
    zero = jnp.zeros_like(up[0])
    up_query = jnp.concatenate([up[0], zero], axis=0)
    up_value = jnp.concatenate([zero, up[1]], axis=0)
    dred_ref[...] = (nt(dq, up_query) + nt(dv, up_value)).astype(bf16)
    dred_t = (nt(up_query, dq) + nt(up_value, dv)).astype(bf16)
    red = red_ref[...]
    grads_ref[0 : 2 * rank] = nn(dred_t, x_ref[...])
    grads_ref[2 * rank : 3 * rank] = 2.0 * nn(red, dq)[0:rank]
    grads_ref[3 * rank : 4 * rank] = 2.0 * nn(red, dv)[rank : 2 * rank]
    grads_ref[4 * rank : 5 * rank] = sums_ref[...]


def adapter_grads(tokens, dq, dv, up, red, sums):
    rows, width = tokens.shape
    rank = up.shape[1]
    return pl.pallas_call(
        adapter_kernel,
        out_shape=[
            jax.ShapeDtypeStruct((rows, 2 * rank), bf16),
            jax.ShapeDtypeStruct((5 * rank, width), f32),
        ],
        compiler_params=pltpu.CompilerParams(vmem_limit_bytes=24 * MIB),
        cost_estimate=pl.CostEstimate(flops=1 << 27, bytes_accessed=5 * MIB, transcendentals=0),
    )(tokens, dq, dv, up, red, sums)


def input_kernel(mid_ref, dq_ref, dk_ref, dv_ref, dred_ref, down_ref, w_ref, out_ref):
    width = mid_ref.shape[1]
    rank = down_ref.shape[1]
    down = down_ref[...].reshape(2 * rank, width).astype(bf16)
    out_ref[...] = (
        mid_ref[...]
        + nt(dq_ref[...], w_ref[:, 0:width])
        + nt(dk_ref[...], w_ref[:, width : 2 * width])
        + nt(dv_ref[...], w_ref[:, 2 * width : 3 * width])
        + nn(dred_ref[...], down)
    )


def input_gradient(mid, dq, dk, dv, dred, down, weight):
    rows, width = mid.shape
    tile = 256
    whole = lambda *shape: pl.BlockSpec(shape, lambda i: (0,) * len(shape))
    tiled = pl.BlockSpec((tile, width), lambda i: (i, 0))
    return pl.pallas_call(
        input_kernel,
        grid=(rows // tile,),
        in_specs=[
            tiled,
            tiled,
            tiled,
            tiled,
            pl.BlockSpec((tile, dred.shape[1]), lambda i: (i, 0)),
            whole(*down.shape),
            whole(*weight.shape),
        ],
        out_specs=tiled,
        out_shape=jax.ShapeDtypeStruct((rows, width), f32),
        compiler_params=pltpu.CompilerParams(vmem_limit_bytes=40 * MIB),
        cost_estimate=pl.CostEstimate(
            flops=6 * rows * width * width, bytes_accessed=15 * MIB, transcendentals=0
        ),
    )(mid, dq, dk, dv, dred, down, weight)


def adamw_kernel(count, scal_ref, total_ref, down_ref, up_ref, dm_ref, dv_ref, um_ref, uv_ref,
                 gd_ref, gu_ref, gain_ref, shift_ref, pd_ref, pu_ref, dm2_ref, dv2_ref, um2_ref, uv2_ref):
    rank = up_ref.shape[1]
    width = up_ref.shape[2]
    part = 1.0 / count
    first_scale, second_scale, rate = scal_ref[0], scal_ref[1], scal_ref[2]

    def update(param, grad, first, second, learn, decay):
        first_new = beta_one * first + (1.0 - beta_one) * grad
        second_new = beta_two * second + (1.0 - beta_two) * grad * grad
        first_hat = first_new / first_scale
        second_hat = second_new / second_scale
        new = param - learn * (first_hat / (jnp.sqrt(second_hat) + adam_epsilon) + decay * param)
        return new, first_new, second_new

    total = total_ref[...] * part
    grad_down = total[0 : 2 * rank].reshape(2, rank, width)
    grad_up = total[2 * rank : 4 * rank].reshape(2, rank, width)
    gd_ref[...] = grad_down
    gu_ref[...] = grad_up
    gain_ref[...] = total[4 * rank : 4 * rank + 2]
    shift_ref[...] = total[4 * rank + 2 : 4 * rank + 4]
    pd_ref[...], dm2_ref[...], dv2_ref[...] = update(
        down_ref[...], grad_down, dm_ref[...], dv_ref[...], rate, down_decay_factor
    )
    pu_ref[...], um2_ref[...], uv2_ref[...] = update(
        up_ref[...], grad_up, um_ref[...], uv_ref[...], 16.0 * rate, up_decay_factor
    )


def adamw(count, scalars, total, down, up, dm, dv, um, uv):
    width = total.shape[1]
    like = jax.ShapeDtypeStruct(up.shape, f32)
    pair = jax.ShapeDtypeStruct((2, width), f32)
    vmem = pl.BlockSpec(memory_space=pltpu.VMEM)
    return pl.pallas_call(
        functools.partial(adamw_kernel, count),
        in_specs=[pl.BlockSpec(memory_space=pltpu.SMEM)] + [vmem] * 7,
        out_shape=[like, like, pair, pair] + [like] * 6,
    )(scalars, total, down, up, dm, dv, um, uv)


def per_device(
    layout,
    tokens,
    document_numbers,
    query_weight,
    key_weight,
    value_weight,
    output_weight,
    inner_weight,
    outer_weight,
    fixed_projection_bias,
    feedforward_inner_bias,
    layer_norm_gain,
    layer_norm_shift,
    adapter_down_factors,
    adapter_up_factors,
    down_first_moment,
    down_second_moment,
    up_first_moment,
    up_second_moment,
    rate,
    step,
    cotangent,
):
    width = tokens.shape[1]
    shard = query_weight.shape[0]
    small = jnp.concatenate(
        [
            fixed_projection_bias,
            layer_norm_gain,
            layer_norm_shift,
        ],
        axis=0,
    )
    inner_bias = feedforward_inner_bias[None]
    if shard % 8 == 0 and shard * layout.n == width and layout.n == 32:
        tail = jnp.concatenate(
            [
                jnp.pad(small, ((0, 0), (0, LANES - shard))),
                jnp.pad(inner_bias, ((0, shard - 9), (0, LANES - inner_bias.shape[1]))),
            ],
            axis=0,
        )
        block_a = jnp.concatenate([query_weight, key_weight, value_weight, tail], axis=1)
        block_b = jnp.concatenate([output_weight, inner_weight], axis=1)
        parts_a = gather_blocks(block_a, layout)
        parts_b = gather_blocks(block_b, layout)
        parts_d = gather_blocks(outer_weight, layout)
        ids = block_ids(layout)
    else:
        count = 32
        rows = width // count
        whole = lambda w: lax.all_gather(w, AXES, axis=0, tiled=True)
        small_full = lax.all_gather(small, AXES, axis=1, tiled=True)
        bias_full = lax.all_gather(inner_bias, AXES, axis=1, tiled=True)
        tail = jnp.concatenate(
            [
                jnp.pad(small_full.reshape(8, count, rows), ((0, 0), (0, 0), (0, LANES - rows))),
                jnp.pad(
                    bias_full.reshape(1, count, -1),
                    ((0, rows - 9), (0, 0), (0, LANES - bias_full.shape[1] // count)),
                ),
            ],
            axis=0,
        )
        tail = jnp.swapaxes(tail, 0, 1).reshape(width, LANES)
        parts_a = as_blocks(
            jnp.concatenate([whole(query_weight), whole(key_weight), whole(value_weight), tail], axis=1), count
        )
        parts_b = as_blocks(jnp.concatenate([whole(output_weight), whole(inner_weight)], axis=1), count)
        parts_d = as_blocks(whole(outer_weight), count)
        ids = jnp.arange(count, dtype=jnp.int32)

    turn = lambda v: jnp.swapaxes(v, 1, 2)
    down = turn(adapter_down_factors)
    up = adapter_up_factors
    qkv, weight, red, small_rows, inner_rows = project(ids, tokens, down, up, parts_a)
    context, attention = attend(document_numbers, qkv)
    activations, grad_mid, grad_context, sums = row_local(
        ids, tokens, cotangent, context, small_rows, inner_rows, parts_b, parts_d
    )
    grad_query, grad_keys, grad_values = attend_back(qkv, context, grad_context, attention)
    grad_reduced, grads = adapter_grads(tokens, grad_query, grad_values, up, red, sums)
    input_grad = input_gradient(
        grad_mid, grad_query, grad_keys, grad_values, grad_reduced, down, weight
    )
    total = grads
    for bit in [layout.core] + layout.bits[:-1]:
        total = total + lax.ppermute(total, AXES, [(i, i ^ bit) for i in range(layout.n)])
    step_counter = step[0].astype(f32)
    scalars = jnp.stack([1.0 - beta_one**step_counter, 1.0 - beta_two**step_counter, rate[0]])
    gd, gu, gain_grad, shift_grad, pd, pu, dm, dv, um, uv = adamw(
        layout.n,
        scalars,
        total,
        down,
        up,
        turn(down_first_moment),
        turn(down_second_moment),
        up_first_moment,
        up_second_moment,
    )
    return (
        activations,
        input_grad,
        turn(gd),
        gu,
        gain_grad,
        shift_grad,
        turn(pd),
        pu,
        turn(dm),
        turn(dv),
        um,
        uv,
    )


def solution(mesh):
    rows = P(AXES, None)
    columns = P(None, AXES)
    in_specs = (
        (rows,) * 8
        + (columns, P(AXES), columns, columns)
        + (P(),) * 8
        + (rows,)
    )
    out_specs = (rows, rows) + (P(),) * 10
    return jax.shard_map(
        functools.partial(per_device, Layout(mesh)),
        mesh=mesh,
        in_specs=in_specs,
        out_specs=out_specs,
        check_vma=False,
    )
```

```python
import functools
import math

import jax
import jax.numpy as jnp
import numpy as np
from jax import lax
from jax.experimental import pallas as pl
from jax.experimental.pallas import tpu as pltpu
from jax.sharding import PartitionSpec as P

HEAD = 64
OUTER_ROWS = 64
AXES = ("dp", "fsdp")

beta_one = 0.9
beta_two = 0.999
adam_epsilon = 1e-08
down_decay_factor = 0.05
up_decay_factor = 0.01
norm_epsilon = 1e-05
masked_score = -1e30
root_half = math.sqrt(0.5)
root_circle = 1.0 / math.sqrt(2.0 * math.pi)
half_log = -0.5 * math.log2(math.e)
LANES = 128
MIB = 1 << 20
VMEM_LIMIT = 60 * MIB

f32 = jnp.float32
bf16 = jnp.bfloat16


def nn(a, b):
    return lax.dot_general(a, b, (((1,), (0,)), ((), ())), preferred_element_type=f32)


def nt(a, b):
    return lax.dot_general(a, b, (((1,), (1,)), ((), ())), preferred_element_type=f32)


class Layout:
    def __init__(self, mesh):
        n_dp, n_fsdp = mesh.shape["dp"], mesh.shape["fsdp"]
        self.n = n_dp * n_fsdp
        self.core = n_fsdp
        n_x = n_dp // 2
        n_y = n_x
        y_bits = [1 << t for t in range(int(math.log2(n_y)))]
        z_bits = [n_y << t for t in range(int(math.log2(n_fsdp // n_y)))]
        x_bits = [(2 * n_fsdp) << t for t in range(int(math.log2(n_x)))]
        self.z_first = (z_bits + x_bits + y_bits, z_bits[::-1] + y_bits + x_bits)
        self.z_last = (x_bits + y_bits + z_bits, y_bits + x_bits + z_bits[::-1])
        self.x_bits, self.y_bits, self.z_bits = x_bits, y_bits, z_bits

    def stage_pairs(self, orders, t):
        return [(i, i ^ orders[1 if i & self.core else 0][t]) for i in range(self.n)]

    def pairs(self, bits):
        return [(i, i ^ bits) for i in range(self.n)]

    def core_pairs(self):
        return [(i, i ^ self.core) for i in range(self.n)]

    def block_masks(self, order):
        masks = [0]
        for bit in order:
            masks = masks + [m ^ bit for m in masks]
        return masks


def after(value, *others):
    return lax.optimization_barrier((value,) + others)[0]


def together(*values):
    return lax.optimization_barrier(values)


def stage(held, layout, orders, t):
    return lax.ppermute(held, AXES, layout.stage_pairs(orders, t))


def swap_cores(value, layout):
    return lax.ppermute(value, AXES, layout.core_pairs())


def join(held, came):
    return jnp.concatenate([held, came], axis=0)


def block_ids(layout, orders):
    me = lax.axis_index(AXES).astype(jnp.int32)
    one, two = (np.array(layout.block_masks(o), np.int32) for o in orders)
    second = (me & layout.core) != 0
    own = me ^ jnp.where(second, two, one)
    other = me ^ layout.core ^ jnp.where(second, one, two)
    return jnp.concatenate([own, other])


def exchange(total, layout, kinds, beside=None):
    combos = [0]
    for bit in kinds:
        combos = combos + [c ^ bit for c in combos]
    parts = [total] + [lax.ppermute(total, AXES, layout.pairs(c)) for c in combos[1:]]
    if beside is not None:
        *parts, beside = together(*parts, beside())
    while len(parts) > 1:
        parts = [one + two for one, two in zip(parts[::2], parts[1::2])]
    return parts[0] if beside is None else (parts[0], beside)


def as_blocks(full, count):
    return tuple(
        part for part in full.reshape((4, count // 4) + (full.shape[0] // count,) + full.shape[1:])
    )


def fetch_blocks(ids_ref, parts, stage, sems):
    each = parts[0].shape[0]
    for a, part in enumerate(parts):
        for j in range(each):
            k = a * each + j
            at = ids_ref[k]
            pltpu.make_async_copy(part.at[j], stage.at[at], sems.at[at]).start()


def wait_block(parts, stage, sems, i):
    pltpu.make_async_copy(parts[0].at[0], stage.at[i], sems.at[i]).wait()


def merge_pairs(parts, stage, sems, target, width, extra=None):
    shards, rows = stage.shape[0], stage.shape[1]
    for i in range(0, shards, 2):
        wait_block(parts, stage, sems, i)
        wait_block(parts, stage, sems, i + 1)
        for c in range(0, width, 768):
            low = stage[i, :, c : c + 768].astype(f32)
            high = stage[i + 1, :, c : c + 768].astype(f32)
            target[rows * i : rows * (i + 2), c : c + 768] = jnp.concatenate(
                [low, high], axis=0
            ).astype(bf16)


def spread(piece, width, step, count):
    lane = lax.broadcasted_iota(jnp.int32, (LANES, width), 1).astype(f32)
    slot = lax.broadcasted_iota(jnp.int32, (LANES, width), 0).astype(f32)
    within = lane - step * jnp.floor((lane + 0.5) * (1.0 / step))
    place = (within == slot).astype(bf16)
    wide = nn(piece.astype(bf16), place)
    at = lax.broadcasted_iota(jnp.int32, (8, width), 1)
    total = jnp.zeros((8, width), f32)
    for i in range(count):
        mine = (at >= step * i) & (at < step * (i + 1))
        total = total + jnp.where(mine, wide[8 * i : 8 * (i + 1)], 0.0)
    return total


def project_kernel(ids_ref, x_ref, down_ref, up_ref, p0, p1, p2, p3, qkv_ref, weight_hbm, red_ref,
                   small_ref, inner_bias_ref, stage, weight_ref, sems, sem_w):
    parts = (p0, p1, p2, p3)
    width = x_ref.shape[1]
    rank = down_ref.shape[1]

    @pl.when(pl.program_id(0) == 0)
    def _():
        fetch_blocks(ids_ref, parts, stage, sems)
        merge_pairs(parts, stage, sems, weight_ref, 3 * width)
        pltpu.make_async_copy(weight_ref, weight_hbm, sem_w).start()
        shards, rows = stage.shape[0], stage.shape[1]
        tail = stage[:, :, 3 * width :].astype(f32)
        small_ref[...] = spread(tail[:, 0:8].reshape(8 * shards, LANES), width, rows, shards)
        ff = inner_bias_ref.shape[1]
        inner_bias_ref[...] = spread(
            tail[:, 8:16].reshape(8 * shards, LANES), ff, ff // shards, shards
        )

    x = x_ref[...]
    down = down_ref[...].reshape(2 * rank, width).astype(bf16)
    up = (2.0 * up_ref[...].astype(bf16).astype(f32)).astype(bf16)
    zero = jnp.zeros((rank, width), bf16)
    reduced = nt(x, down).astype(bf16)
    red_ref[...] = nt(down, x).astype(bf16)
    up_query = jnp.concatenate([up[0], zero], axis=0)
    up_value = jnp.concatenate([zero, up[1]], axis=0)
    chunk = 256
    for c in range(0, 3 * width, chunk):
        y = nn(x, weight_ref[:, c : c + chunk])
        o = c % width
        if c < width:
            y = y + small_ref[0:1, o : o + chunk] + nn(reduced, up_query[:, o : o + chunk])
        elif c >= 2 * width:
            y = y + small_ref[1:2, o : o + chunk] + nn(reduced, up_value[:, o : o + chunk])
        qkv_ref[:, c : c + chunk] = y.astype(bf16)

    @pl.when(pl.program_id(0) == pl.num_programs(0) - 1)
    def _():
        pltpu.make_async_copy(weight_ref, weight_hbm, sem_w).wait()


def project(ids, tokens, down, up, parts):
    rows, width = tokens.shape
    shards = 4 * parts[0].shape[0]
    shard_rows = parts[0].shape[1]
    ff = 4 * width
    tile = 256
    whole = lambda *shape: pl.BlockSpec(shape, lambda i: (0,) * len(shape))
    return pl.pallas_call(
        project_kernel,
        grid=(rows // tile,),
        in_specs=[
            pl.BlockSpec(memory_space=pltpu.SMEM),
            pl.BlockSpec((tile, width), lambda i: (i, 0)),
            whole(*down.shape),
            whole(*up.shape),
        ]
        + [pl.BlockSpec(memory_space=pl.ANY)] * 4,
        out_specs=[
            pl.BlockSpec((tile, 3 * width), lambda i: (i, 0)),
            pl.BlockSpec(memory_space=pl.ANY),
            pl.BlockSpec((2 * down.shape[1], tile), lambda i: (0, i)),
            whole(8, width),
            whole(8, ff),
        ],
        out_shape=[
            jax.ShapeDtypeStruct((rows, 3 * width), bf16),
            jax.ShapeDtypeStruct((width, 3 * width), bf16),
            jax.ShapeDtypeStruct((2 * down.shape[1], rows), bf16),
            jax.ShapeDtypeStruct((8, width), f32),
            jax.ShapeDtypeStruct((8, ff), f32),
        ],
        scratch_shapes=[
            pltpu.VMEM((shards, shard_rows, 3 * width + LANES), bf16),
            pltpu.VMEM((width, 3 * width), bf16),
            pltpu.SemaphoreType.DMA((shards,)),
            pltpu.SemaphoreType.DMA(()),
        ],
        compiler_params=pltpu.CompilerParams(vmem_limit_bytes=VMEM_LIMIT),
        cost_estimate=pl.CostEstimate(
            flops=2 * rows * width * width * 3, bytes_accessed=14 * MIB, transcendentals=0
        ),
    )(ids, tokens, down, up, *parts)


def attend_kernel(pack, seg_ref, q_ref, k_ref, v_ref, *rest):
    ctx_ref, w_ref, mask = rest[-3:]
    rows = seg_ref.shape[1]

    @pl.when(pl.program_id(0) == 0)
    def _():
        row = jnp.broadcast_to(seg_ref[pack : pack + 1, :].astype(f32), (8, rows))
        column = row.T[:, 0:1]
        mask[...] = jnp.where(column == row[0:1], 0.0, masked_score)

    lane = lax.broadcasted_iota(jnp.int32, (1, LANES), 1)
    for s in range(q_ref.shape[1] // LANES):
        cols = slice(s * LANES, (s + 1) * LANES)
        q = q_ref[:, cols] * jnp.asarray(HEAD**-0.5, bf16)
        k = k_ref[:, cols]
        v = v_ref[:, cols]
        ctx = None
        for h in range(2):
            mine = (lane < HEAD) if h == 0 else (lane >= HEAD)
            scores = nt(jnp.where(mine, q, jnp.zeros_like(q)), k) + mask[...]
            peak = jnp.max(scores, axis=-1, keepdims=True)
            exponent = jnp.exp(scores - peak)
            total = jnp.sum(exponent, axis=-1, keepdims=True)
            weights = (exponent * (1.0 / total)).astype(bf16)
            w_ref[2 * s + h] = weights
            part = nn(weights, jnp.where(mine, v, jnp.zeros_like(v)))
            ctx = part if ctx is None else ctx + part
        ctx_ref[:, cols] = ctx.astype(bf16)


HEADS_A_STEP = 4


def attend(pack, segments, qkv, before=()):
    packs, length = segments.shape
    width = qkv.shape[1] // 3
    step = HEADS_A_STEP * HEAD
    steps = width // step
    at = lambda which: pl.BlockSpec((length, step), lambda s: (pack, which * steps + s))
    return pl.pallas_call(
        functools.partial(attend_kernel, pack),
        grid=(steps,),
        in_specs=[pl.BlockSpec((packs, length), lambda s: (0, 0)), at(0), at(1), at(2)]
        + [pl.BlockSpec(memory_space=pl.ANY)] * len(before),
        out_specs=[
            pl.BlockSpec((length, step), lambda s: (pack, s)),
            pl.BlockSpec((HEADS_A_STEP, length, length), lambda s: (pack * steps + s, 0, 0)),
        ],
        out_shape=[
            jax.ShapeDtypeStruct((packs * length, width), bf16),
            jax.ShapeDtypeStruct((packs * width // HEAD, length, length), bf16),
        ],
        input_output_aliases={4 + i: i for i in range(len(before))},
        scratch_shapes=[pltpu.VMEM((length, length), f32)],
        compiler_params=pltpu.CompilerParams(vmem_limit_bytes=VMEM_LIMIT),
        cost_estimate=pl.CostEstimate(
            flops=16 * length * length * width, bytes_accessed=10 * MIB, transcendentals=0
        ),
    )(segments, qkv, qkv, qkv, *before)


def stats(value):
    centred = value - jnp.mean(value, axis=-1, keepdims=True)
    inverse = lax.rsqrt(jnp.mean(centred * centred, axis=-1, keepdims=True) + norm_epsilon)
    return centred * inverse, inverse


def norm_back(grad, normed, inverse, gain):
    scaled = grad * gain
    return inverse * (
        scaled
        - jnp.mean(scaled, axis=-1, keepdims=True)
        - normed * jnp.mean(scaled * normed, axis=-1, keepdims=True)
    )


def gelu_parts(z):
    cumulative = 0.5 + 0.5 * lax.erf(z * root_half)
    density = jnp.exp2(z * z * half_log) * root_circle
    return z * cumulative, cumulative + z * density


def rows_kernel(ids_ref, ids_d_ref, x_ref, cot_ref, ctx_ref, small_ref, inner_bias_ref,
                b0, b1, b2, b3, d0, d1, d2, d3,
                act_ref, mid_ref, dctx_ref, sums_ref,
                stage, wo, wi, wf, active, slope, sem_b, sem_d):
    parts_b, parts_d = (b0, b1, b2, b3), (d0, d1, d2, d3)
    width = x_ref.shape[1]
    taken = d0.shape[1]
    ff = wi.shape[1]
    shard = ff // stage.shape[0]

    @pl.when(pl.program_id(0) == 0)
    def _():
        fetch_blocks(ids_ref, parts_b, stage, sem_b)
        for a, part in enumerate(parts_d):
            for j in range(part.shape[0]):
                at = ids_d_ref[a * part.shape[0] + j]
                place = wf.at[pl.ds(pl.multiple_of(at * shard, shard), taken)]
                pltpu.make_async_copy(part.at[j], place, sem_d.at[at]).start()
        shards, rows = stage.shape[0], stage.shape[1]
        for i in range(0, shards, 2):
            wait_block(parts_b, stage, sem_b, i)
            wait_block(parts_b, stage, sem_b, i + 1)
            for c in range(0, width + ff, width):
                both = jnp.concatenate(
                    [
                        stage[i, :, c : c + width].astype(f32),
                        stage[i + 1, :, c : c + width].astype(f32),
                    ],
                    axis=0,
                ).astype(bf16)
                where = slice(rows * i, rows * (i + 2))
                if c == 0:
                    wo[where] = both
                else:
                    wi[where, c - width : c] = both
            for k in (i, i + 1):
                more = stage[k, :, width + ff :].astype(f32)
                third = more[:, width:]
                eight = [third[8 * n : 8 * (n + 1)] for n in range(3)]
                wf[k * shard + taken : (k + 1) * shard] = jnp.concatenate(
                    [more[:, :width], jnp.concatenate(eight, axis=1)], axis=0
                ).astype(bf16)
        for i in range(shards):
            pltpu.make_async_copy(d0.at[0], wf.at[pl.ds(i * shard, taken)], sem_d.at[i]).wait()
        sums_ref[...] = jnp.zeros_like(sums_ref)

    bias_out, bias_ff = small_ref[2:3], small_ref[3:4]
    gain_one, gain_two = small_ref[4:5], small_ref[5:6]
    shift_one, shift_two = small_ref[6:7], small_ref[7:8]
    chunk = 512
    normed_one, inverse_one = stats(x_ref[...].astype(f32) + (nn(ctx_ref[...], wo[...]) + bias_out))
    first = normed_one * gain_one + shift_one
    first_b = first.astype(bf16)
    outer = None
    for c in range(0, ff, chunk):
        cols = slice(c, c + chunk)
        inner = nn(first_b, wi[:, cols]) + inner_bias_ref[0:1, cols]
        value, grad = gelu_parts(inner)
        active[:, cols] = value.astype(bf16)
        slope[:, cols] = grad.astype(bf16)
    outer = nn(active[...], wf[...]) + bias_ff
    normed_two, inverse_two = stats(first + outer)
    act_ref[...] = (normed_two * gain_two + shift_two).astype(bf16)
    grad_out = cot_ref[...].astype(f32)
    grad_gain_two = jnp.sum(grad_out * normed_two, axis=0, keepdims=True)
    grad_shift_two = jnp.sum(grad_out, axis=0, keepdims=True)
    grad_res = norm_back(grad_out, normed_two, inverse_two, gain_two)
    grad_outer = grad_res.astype(bf16)
    for c in range(0, ff, chunk):
        cols = slice(c, c + chunk)
        grad_active = nt(grad_outer, wf[cols])
        active[:, cols] = (grad_active * slope[:, cols].astype(f32)).astype(bf16)
    grad_first = grad_res + nt(active[...], wi[...])
    grad_gain_one = jnp.sum(grad_first * normed_one, axis=0, keepdims=True)
    grad_shift_one = jnp.sum(grad_first, axis=0, keepdims=True)
    sums_ref[0:4] += jnp.concatenate(
        [grad_gain_one, grad_gain_two, grad_shift_one, grad_shift_two], axis=0
    )
    grad_mid = norm_back(grad_first, normed_one, inverse_one, gain_one)
    mid_ref[...] = grad_mid
    dctx_ref[...] = nt(grad_mid.astype(bf16), wo[...]).astype(bf16)


def row_local(ids, ids_d, tokens, cotangent, context, small, inner_bias, parts_b, parts_d):
    rows, width = tokens.shape
    ff = inner_bias.shape[1]
    shards = 4 * parts_b[0].shape[0]
    tile = 256
    whole = lambda *shape: pl.BlockSpec(shape, lambda i: (0,) * len(shape))
    tiled = pl.BlockSpec((tile, width), lambda i: (i, 0))
    return pl.pallas_call(
        rows_kernel,
        grid=(rows // tile,),
        in_specs=[
            pl.BlockSpec(memory_space=pltpu.SMEM),
            pl.BlockSpec(memory_space=pltpu.SMEM),
            tiled,
            tiled,
            tiled,
            whole(8, width),
            whole(8, ff),
        ]
        + [pl.BlockSpec(memory_space=pl.ANY)] * 8,
        out_specs=[tiled, tiled, tiled, whole(8, width)],
        out_shape=[
            jax.ShapeDtypeStruct((rows, width), bf16),
            jax.ShapeDtypeStruct((rows, width), f32),
            jax.ShapeDtypeStruct((rows, width), bf16),
            jax.ShapeDtypeStruct((8, width), f32),
        ],
        scratch_shapes=[
            pltpu.VMEM((shards,) + parts_b[0].shape[1:], bf16),
            pltpu.VMEM((width, width), bf16),
            pltpu.VMEM((width, ff), bf16),
            pltpu.VMEM((ff, width), bf16),
            pltpu.VMEM((tile, ff), bf16),
            pltpu.VMEM((tile, ff), bf16),
            pltpu.SemaphoreType.DMA((shards,)),
            pltpu.SemaphoreType.DMA((shards,)),
        ],
        compiler_params=pltpu.CompilerParams(vmem_limit_bytes=VMEM_LIMIT),
        cost_estimate=pl.CostEstimate(
            flops=2 * rows * width * (4 * ff + 2 * width), bytes_accessed=20 * MIB, transcendentals=0
        ),
    )(ids, ids_d, tokens, cotangent, context, small, inner_bias, *parts_b, *parts_d)


def attend_back_kernel(core_ref, x_ref, q_ref, k_ref, v_ref, ctx_ref, dctx_ref, w_ref, up_ref, red_ref,
                       sums_ref, dq_ref, dk_ref, dv_ref, dred_ref, keep_ref, send_ref, dred, grads):
    scale = HEAD**-0.5
    pack, step = pl.program_id(0), pl.program_id(1)
    rank = red_ref.shape[0] // 2

    @pl.when((pack == 0) & (step == 0))
    def _():
        grads[...] = jnp.zeros_like(grads)
        keep_ref[...] = jnp.zeros_like(keep_ref)
        send_ref[...] = jnp.zeros_like(send_ref)

    @pl.when(step == 0)
    def _():
        dred[...] = jnp.zeros_like(dred)

    lane = lax.broadcasted_iota(jnp.int32, (1, LANES), 1)
    for s in range(q_ref.shape[1] // LANES):
        cols = slice(s * LANES, (s + 1) * LANES)
        q, k, v = q_ref[:, cols], k_ref[:, cols], v_ref[:, cols]
        dctx = dctx_ref[:, cols]
        flat = dctx.astype(f32) * ctx_ref[:, cols].astype(f32)
        q_t = q.T
        dctx_t = dctx.T
        dq = None
        dk_t, dv_t = [], []
        for h in range(2):
            mine = (lane < HEAD) if h == 0 else (lane >= HEAD)
            zero = jnp.zeros_like(q)
            grad_weights = nt(jnp.where(mine, dctx, zero), v)
            delta = jnp.sum(jnp.where(mine, flat, 0.0), axis=-1, keepdims=True)
            weights = w_ref[2 * s + h]
            grad_scores = (weights.astype(f32) * (grad_weights - delta)).astype(bf16)
            part = nn(grad_scores, jnp.where(mine, k, zero))
            dq = part if dq is None else dq + part
            rows = slice(h * HEAD, (h + 1) * HEAD)
            dk_t.append(nn(q_t[rows], grad_scores))
            dv_t.append(nn(dctx_t[rows], weights))
        dq_ref[:, cols] = (dq * scale).astype(bf16)
        dk_ref[:, cols] = (jnp.concatenate(dk_t, axis=0) * scale).T.astype(bf16)
        dv_ref[:, cols] = jnp.concatenate(dv_t, axis=0).T.astype(bf16)
    red = red_ref[...]
    up = (2.0 * up_ref[...].astype(bf16).astype(f32)).astype(bf16)
    none = jnp.zeros_like(up[0])
    dq, dv = dq_ref[...], dv_ref[...]
    dred[...] += nt(jnp.concatenate([up[0], none], axis=0), dq) + nt(jnp.concatenate([none, up[1]], axis=0), dv)
    grads[step, 0:rank] += 2.0 * nn(red, dq)[0:rank]
    grads[step, rank : 2 * rank] += 2.0 * nn(red, dv)[rank : 2 * rank]

    @pl.when(step == pl.num_programs(1) - 1)
    def _():
        rounded = dred[...].astype(bf16)
        dred_ref[...] = rounded
        down = nn(rounded, x_ref[...])
        raised = jnp.concatenate([grads[i] for i in range(grads.shape[0])], axis=1)
        half = down.shape[1] // 2
        low = (core_ref[0] == 0).astype(f32)
        for out, left in ((keep_ref, low), (send_ref, 1.0 - low)):
            pick = lambda a: jnp.where(left > 0.5, a[:, :half], a[:, half:])
            out[0 : 2 * rank] += pick(down)
            out[2 * rank : 4 * rank] = pick(raised)
            out[4 * rank : 5 * rank] = pick(sums_ref[...])


def attend_back(core, tokens, qkv, context, grad_context, weights, up, red, sums):
    rows, width = context.shape
    length = weights.shape[1]
    rank = up.shape[1]
    step = HEADS_A_STEP * HEAD
    steps = width // step
    at = lambda which: pl.BlockSpec((length, step), lambda p, s: (p, which * steps + s))
    own = pl.BlockSpec((length, step), lambda p, s: (p, s))
    whole = lambda *shape: pl.BlockSpec(shape, lambda p, s: (0,) * len(shape))
    along = pl.BlockSpec((2 * rank, length), lambda p, s: (0, p))
    return pl.pallas_call(
        attend_back_kernel,
        grid=(rows // length, steps),
        in_specs=[
            pl.BlockSpec(memory_space=pltpu.SMEM),
            pl.BlockSpec((length, width), lambda p, s: (p, 0)),
            at(0),
            at(1),
            at(2),
            own,
            own,
            pl.BlockSpec((HEADS_A_STEP, length, length), lambda p, s: (p * steps + s, 0, 0)),
            pl.BlockSpec((2, rank, step), lambda p, s: (0, 0, s)),
            along,
            whole(*sums.shape),
        ],
        out_specs=[own, own, own, along, whole(5 * rank, width // 2), whole(5 * rank, width // 2)],
        out_shape=[jax.ShapeDtypeStruct((rows, width), bf16)] * 3
        + [
            jax.ShapeDtypeStruct((2 * rank, rows), bf16),
            jax.ShapeDtypeStruct((5 * rank, width // 2), f32),
            jax.ShapeDtypeStruct((5 * rank, width // 2), f32),
        ],
        scratch_shapes=[pltpu.VMEM((2 * rank, length), f32), pltpu.VMEM((steps, 2 * rank, step), f32)],
        compiler_params=pltpu.CompilerParams(vmem_limit_bytes=VMEM_LIMIT),
        cost_estimate=pl.CostEstimate(
            flops=32 * rows * length * width, bytes_accessed=28 * MIB, transcendentals=0
        ),
    )(core, tokens, qkv, qkv, qkv, context, grad_context, weights, up, red, sums)


def input_kernel(mid_ref, dq_ref, dk_ref, dv_ref, dred_ref, down_ref, w_ref, out_ref):
    width = mid_ref.shape[1]
    rank = down_ref.shape[1]
    down = down_ref[...].reshape(2 * rank, width).astype(bf16)
    low = lax.dot_general(dred_ref[...], down, (((0,), (0,)), ((), ())), preferred_element_type=f32)
    out_ref[...] = (
        mid_ref[...]
        + low
        + nt(dq_ref[...], w_ref[:, 0:width])
        + nt(dk_ref[...], w_ref[:, width : 2 * width])
        + nt(dv_ref[...], w_ref[:, 2 * width : 3 * width])
    )


def input_gradient(mid, dq, dk, dv, dred, down, weight):
    rows, width = mid.shape
    tile = 256
    whole = lambda *shape: pl.BlockSpec(shape, lambda i: (0,) * len(shape))
    tiled = pl.BlockSpec((tile, width), lambda i: (i, 0))
    return pl.pallas_call(
        input_kernel,
        grid=(rows // tile,),
        in_specs=[
            tiled,
            tiled,
            tiled,
            tiled,
            pl.BlockSpec((dred.shape[0], tile), lambda i: (0, i)),
            whole(*down.shape),
            whole(*weight.shape),
        ],
        out_specs=tiled,
        out_shape=jax.ShapeDtypeStruct((rows, width), f32),
        compiler_params=pltpu.CompilerParams(vmem_limit_bytes=VMEM_LIMIT),
        cost_estimate=pl.CostEstimate(
            flops=6 * rows * width * width, bytes_accessed=15 * MIB, transcendentals=0
        ),
    )(mid, dq, dk, dv, dred, down, weight)


def adamw_kernel(count, scal_ref, core_ref, mine_ref, other_ref, down_ref, up_ref, dm_ref, dv_ref, um_ref, uv_ref,
                 gd_ref, gu_ref, gain_ref, shift_ref, pd_ref, pu_ref, dm2_ref, dv2_ref, um2_ref, uv2_ref):
    rank = up_ref.shape[1]
    width = up_ref.shape[2]
    part = 1.0 / count
    first_scale, second_scale, rate = scal_ref[0], scal_ref[1], scal_ref[2]

    def update(param, grad, first, second, learn, decay):
        first_new = beta_one * first + (1.0 - beta_one) * grad
        second_new = beta_two * second + (1.0 - beta_two) * grad * grad
        first_hat = first_new / first_scale
        second_hat = second_new / second_scale
        new = param - learn * (first_hat / (jnp.sqrt(second_hat) + adam_epsilon) + decay * param)
        return new, first_new, second_new

    mine, other = mine_ref[...] * part, other_ref[...] * part
    low = core_ref[0] == 0
    total = jnp.concatenate([jnp.where(low, mine, other), jnp.where(low, other, mine)], axis=1)
    grad_down = total[0 : 2 * rank].reshape(2, rank, width)
    grad_up = total[2 * rank : 4 * rank].reshape(2, rank, width)
    gd_ref[...] = grad_down
    gu_ref[...] = grad_up
    gain_ref[...] = total[4 * rank : 4 * rank + 2]
    shift_ref[...] = total[4 * rank + 2 : 4 * rank + 4]
    pd_ref[...], dm2_ref[...], dv2_ref[...] = update(
        down_ref[...], grad_down, dm_ref[...], dv_ref[...], rate, down_decay_factor
    )
    pu_ref[...], um2_ref[...], uv2_ref[...] = update(
        up_ref[...], grad_up, um_ref[...], uv_ref[...], 16.0 * rate, up_decay_factor
    )


def adamw(count, scalars, core, mine, other, down, up, dm, dv, um, uv):
    width = up.shape[2]
    like = jax.ShapeDtypeStruct(up.shape, f32)
    pair = jax.ShapeDtypeStruct((2, width), f32)
    vmem = pl.BlockSpec(memory_space=pltpu.VMEM)
    smem = pl.BlockSpec(memory_space=pltpu.SMEM)
    return pl.pallas_call(
        functools.partial(adamw_kernel, count),
        in_specs=[smem, smem] + [vmem] * 8,
        out_shape=[like, like, pair, pair] + [like] * 6,
    )(scalars, core, mine, other, down, up, dm, dv, um, uv)


def per_device(
    layout,
    tokens,
    document_numbers,
    query_weight,
    key_weight,
    value_weight,
    output_weight,
    inner_weight,
    outer_weight,
    fixed_projection_bias,
    feedforward_inner_bias,
    layer_norm_gain,
    layer_norm_shift,
    adapter_down_factors,
    adapter_up_factors,
    down_first_moment,
    down_second_moment,
    up_first_moment,
    up_second_moment,
    rate,
    step,
    cotangent,
):
    width = tokens.shape[1]
    shard = query_weight.shape[0]
    small = jnp.concatenate(
        [
            fixed_projection_bias,
            layer_norm_gain,
            layer_norm_shift,
        ],
        axis=0,
    )
    inner_bias = feedforward_inner_bias[None]
    fast = shard % 8 == 0 and shard * layout.n == width and layout.n == 32
    if fast:
        tail = jnp.concatenate(
            [
                jnp.pad(small, ((0, 0), (0, LANES - shard))),
                jnp.pad(inner_bias, ((0, shard - 9), (0, LANES - inner_bias.shape[1]))),
            ],
            axis=0,
        )
        block_a = jnp.concatenate([query_weight, key_weight, value_weight, tail], axis=1)
        extra = outer_weight[OUTER_ROWS:]
        third = extra[shard:].reshape(8, 3, width // 3)
        third = jnp.swapaxes(third, 0, 1).reshape(shard, width // 3)
        block_b = jnp.concatenate([output_weight, inner_weight, extra[:shard], third], axis=1)
        zf, zl = layout.z_first, layout.z_last
        ids = block_ids(layout, zf)
        ids_d = block_ids(layout, zl)
        a, b, d = block_a[None], block_b[None], outer_weight[None, :OUTER_ROWS]
        a1 = stage(a, layout, zf, 0)
        d1 = stage(d, layout, zl, 0)
        a1, d1 = together(a1, d1)
        a, d = join(a, a1), join(d, d1)
        a2 = stage(a, layout, zf, 1)
        d2 = stage(d, layout, zl, 1)
        a2, d2, b = together(a2, d2, b)
        a, d = join(a, a2), join(d, d2)
        a3 = stage(a, layout, zf, 2)
        b1 = stage(b, layout, zf, 0)
        a3, b1 = together(a3, b1)
        a, b = join(a, a3), join(b, b1)
        a4 = stage(a, layout, zf, 3)
        b2 = stage(b, layout, zf, 1)
        a5 = swap_cores(a, layout)
        a4, b2, a5, d = together(a4, b2, a5, d)
        d3 = stage(d, layout, zl, 2)
        a6 = swap_cores(a4, layout)
        b = join(b, b2)
        b3 = stage(b, layout, zf, 2)
        parts_a = (a, a4, a5, a6)
    else:
        count = 32
        rows = width // count
        whole = lambda w: lax.all_gather(w, AXES, axis=0, tiled=True)
        small_full = lax.all_gather(small, AXES, axis=1, tiled=True)
        bias_full = lax.all_gather(inner_bias, AXES, axis=1, tiled=True)
        tail = jnp.concatenate(
            [
                jnp.pad(small_full.reshape(8, count, rows), ((0, 0), (0, 0), (0, LANES - rows))),
                jnp.pad(
                    bias_full.reshape(1, count, -1),
                    ((0, rows - 9), (0, 0), (0, LANES - bias_full.shape[1] // count)),
                ),
            ],
            axis=0,
        )
        tail = jnp.swapaxes(tail, 0, 1).reshape(width, LANES)
        parts_a = as_blocks(
            jnp.concatenate([whole(query_weight), whole(key_weight), whole(value_weight), tail], axis=1), count
        )
        outer = whole(outer_weight).reshape(count, -1, width)
        extra = outer[:, OUTER_ROWS:]
        third = extra[:, rows:].reshape(count, 8, 3, width // 3)
        third = jnp.swapaxes(third, 1, 2).reshape(width, width // 3)
        parts_b = as_blocks(
            jnp.concatenate(
                [whole(output_weight), whole(inner_weight), extra[:, :rows].reshape(width, width), third], axis=1
            ),
            count,
        )
        parts_d = as_blocks(outer[:, :OUTER_ROWS].reshape(-1, width), count)
        ids = ids_d = jnp.arange(count, dtype=jnp.int32)

    turn = lambda v: jnp.swapaxes(v, 1, 2)
    down = turn(adapter_down_factors)
    up = adapter_up_factors
    qkv, weight, red, small_rows, inner_rows = project(ids, tokens, down, up, parts_a)
    if fast:
        b3, d3, qkv = together(b3, d3, qkv)
        b = join(b, b3)
        b4 = stage(b, layout, zf, 3)
        d = join(d, d3)
        d4 = stage(d, layout, zl, 3)
    half = attend(0, document_numbers, qkv)
    if fast:
        b5 = swap_cores(after(b, *half), layout)
        d5 = swap_cores(after(d, *half), layout)
    context, attention = attend(1, document_numbers, qkv, half)
    if fast:
        b4, d4, context = together(b4, d4, context)
        b6 = swap_cores(b4, layout)
        d6 = swap_cores(d4, layout)
        parts_b = (b, b4, b5, b6)
        parts_d = (d, d4, d5, d6)
    activations, grad_mid, grad_context, sums = row_local(
        ids, ids_d, tokens, cotangent, context, small_rows, inner_rows, parts_b, parts_d
    )
    core = jnp.reshape((lax.axis_index(AXES) & layout.core) != 0, (1,)).astype(jnp.int32)
    dq, dk, dv, dred, keep, send = attend_back(
        core, tokens, qkv, context, grad_context, attention, up, red, sums
    )
    total = keep + swap_cores(send, layout)
    gradient = lambda: input_gradient(grad_mid, after(dq, total), dk, dv, dred, down, weight)
    total, input_grad = exchange(total, layout, layout.x_bits + layout.y_bits, gradient)
    total = exchange(total, layout, layout.z_bits)
    other = swap_cores(total, layout)
    step_counter = step[0].astype(f32)
    scalars = jnp.stack([1.0 - beta_one**step_counter, 1.0 - beta_two**step_counter, rate[0]])
    gd, gu, gain_grad, shift_grad, pd, pu, dm, dv, um, uv = adamw(
        layout.n,
        scalars,
        core,
        total,
        other,
        down,
        up,
        turn(down_first_moment),
        turn(down_second_moment),
        up_first_moment,
        up_second_moment,
    )
    return (
        activations,
        input_grad,
        turn(gd),
        gu,
        gain_grad,
        shift_grad,
        turn(pd),
        pu,
        turn(dm),
        turn(dv),
        um,
        uv,
    )


def solution(mesh):
    rows = P(AXES, None)
    columns = P(None, AXES)
    in_specs = (
        (rows,) * 8
        + (columns, P(AXES), columns, columns)
        + (P(),) * 8
        + (rows,)
    )
    out_specs = (rows, rows) + (P(),) * 10
    return jax.shard_map(
        functools.partial(per_device, Layout(mesh)),
        mesh=mesh,
        in_specs=in_specs,
        out_specs=out_specs,
        check_vma=False,
    )
```

```python
import functools
import math

import jax
import jax.numpy as jnp
import numpy as np
from jax import lax
from jax.experimental import pallas as pl
from jax.experimental.pallas import tpu as pltpu
from jax.sharding import PartitionSpec as P

HEAD = 64
OUTER_ROWS = 64
AXES = ("dp", "fsdp")

beta_one = 0.9
beta_two = 0.999
adam_epsilon = 1e-08
down_decay_factor = 0.05
up_decay_factor = 0.01
norm_epsilon = 1e-05
masked_score = -1e30
root_half = math.sqrt(0.5)
root_circle = 1.0 / math.sqrt(2.0 * math.pi)
log_e = math.log2(math.e)
LANES = 128
MIB = 1 << 20
VMEM_LIMIT = 60 * MIB

f32 = jnp.float32
bf16 = jnp.bfloat16


def nn(a, b):
    return lax.dot_general(a, b, (((1,), (0,)), ((), ())), preferred_element_type=f32)


def nt(a, b):
    return lax.dot_general(a, b, (((1,), (1,)), ((), ())), preferred_element_type=f32)


class Layout:
    def __init__(self, mesh):
        n_dp, n_fsdp = mesh.shape["dp"], mesh.shape["fsdp"]
        self.n = n_dp * n_fsdp
        self.core = n_fsdp
        n_x = n_dp // 2
        n_y = n_x
        y_bits = [1 << t for t in range(int(math.log2(n_y)))]
        z_bits = [n_y << t for t in range(int(math.log2(n_fsdp // n_y)))]
        x_bits = [(2 * n_fsdp) << t for t in range(int(math.log2(n_x)))]
        self.z_first = (z_bits + x_bits + y_bits, z_bits[::-1] + y_bits + x_bits)
        self.z_last = (x_bits + y_bits + z_bits, y_bits + x_bits + z_bits[::-1])
        self.x_bits, self.y_bits, self.z_bits = x_bits, y_bits, z_bits

    def stage_pairs(self, orders, t):
        return [(i, i ^ orders[1 if i & self.core else 0][t]) for i in range(self.n)]

    def pairs(self, bits):
        return [(i, i ^ bits) for i in range(self.n)]

    def core_pairs(self):
        return [(i, i ^ self.core) for i in range(self.n)]

    def block_masks(self, order):
        masks = [0]
        for bit in order:
            masks = masks + [m ^ bit for m in masks]
        return masks


def after(value, *others):
    return lax.optimization_barrier((value,) + others)[0]


def together(*values):
    return lax.optimization_barrier(values)


def stage(held, layout, orders, t):
    return lax.ppermute(held, AXES, layout.stage_pairs(orders, t))


def swap_cores(value, layout):
    return lax.ppermute(value, AXES, layout.core_pairs())


def join(held, came):
    return jnp.concatenate([held, came], axis=0)


def block_ids(layout, orders):
    me = lax.axis_index(AXES).astype(jnp.int32)
    one, two = (np.array(layout.block_masks(o), np.int32) for o in orders)
    second = (me & layout.core) != 0
    own = me ^ jnp.where(second, two, one)
    other = me ^ layout.core ^ jnp.where(second, one, two)
    return jnp.concatenate([own, other])


def exchange(total, layout, kinds):
    combos = [0]
    for bit in kinds:
        combos = combos + [c ^ bit for c in combos]
    parts = [total] + [lax.ppermute(total, AXES, layout.pairs(c)) for c in combos[1:]]
    while len(parts) > 1:
        parts = [one + two for one, two in zip(parts[::2], parts[1::2])]
    return parts[0]


def as_blocks(full, count):
    return tuple(
        part for part in full.reshape((4, count // 4) + (full.shape[0] // count,) + full.shape[1:])
    )


def fetch_blocks(ids_ref, parts, stage, sems):
    each = parts[0].shape[0]
    for a, part in enumerate(parts):
        for j in range(each):
            k = a * each + j
            at = ids_ref[k]
            pltpu.make_async_copy(part.at[j], stage.at[at], sems.at[at]).start()


def wait_block(parts, stage, sems, i):
    pltpu.make_async_copy(parts[0].at[0], stage.at[i], sems.at[i]).wait()


def merge_pairs(parts, stage, sems, target, width, extra=None):
    shards, rows = stage.shape[0], stage.shape[1]
    for i in range(0, shards, 2):
        wait_block(parts, stage, sems, i)
        wait_block(parts, stage, sems, i + 1)
        for c in range(0, width, 768):
            low = stage[i, :, c : c + 768].astype(f32)
            high = stage[i + 1, :, c : c + 768].astype(f32)
            target[rows * i : rows * (i + 2), c : c + 768] = jnp.concatenate(
                [low, high], axis=0
            ).astype(bf16)


def spread(piece, width, step, count):
    lane = lax.broadcasted_iota(jnp.int32, (LANES, width), 1).astype(f32)
    slot = lax.broadcasted_iota(jnp.int32, (LANES, width), 0).astype(f32)
    within = lane - step * jnp.floor((lane + 0.5) * (1.0 / step))
    place = (within == slot).astype(bf16)
    wide = nn(piece.astype(bf16), place)
    at = lax.broadcasted_iota(jnp.int32, (8, width), 1)
    total = jnp.zeros((8, width), f32)
    for i in range(count):
        mine = (at >= step * i) & (at < step * (i + 1))
        total = total + jnp.where(mine, wide[8 * i : 8 * (i + 1)], 0.0)
    return total


def project_kernel(ids_ref, x_ref, down_ref, up_ref, p0, p1, p2, p3, qkv_ref, weight_hbm, red_ref,
                   small_ref, inner_bias_ref, stage, weight_ref, sems, sem_w):
    parts = (p0, p1, p2, p3)
    width = x_ref.shape[1]
    rank = down_ref.shape[1]

    @pl.when(pl.program_id(0) == 0)
    def _():
        fetch_blocks(ids_ref, parts, stage, sems)
        merge_pairs(parts, stage, sems, weight_ref, 3 * width)
        pltpu.make_async_copy(weight_ref, weight_hbm, sem_w).start()
        shards, rows = stage.shape[0], stage.shape[1]
        tail = stage[:, :, 3 * width :].astype(f32)
        small_ref[...] = spread(tail[:, 0:8].reshape(8 * shards, LANES), width, rows, shards)
        ff = inner_bias_ref.shape[1]
        inner_bias_ref[...] = spread(
            tail[:, 8:16].reshape(8 * shards, LANES), ff, ff // shards, shards
        )

    x = x_ref[...]
    down = down_ref[...].reshape(2 * rank, width).astype(bf16)
    up = (2.0 * up_ref[...].astype(bf16).astype(f32)).astype(bf16)
    zero = jnp.zeros((rank, width), bf16)
    reduced = nt(x, down).astype(bf16)
    red_ref[...] = nt(down, x).astype(bf16)
    up_query = jnp.concatenate([up[0], zero], axis=0)
    up_value = jnp.concatenate([zero, up[1]], axis=0)
    chunk = 256
    for c in range(0, 3 * width, chunk):
        y = nn(x, weight_ref[:, c : c + chunk])
        o = c % width
        if c < width:
            y = y + small_ref[0:1, o : o + chunk] + nn(reduced, up_query[:, o : o + chunk])
        elif c >= 2 * width:
            y = y + small_ref[1:2, o : o + chunk] + nn(reduced, up_value[:, o : o + chunk])
        qkv_ref[:, c : c + chunk] = y.astype(bf16)

    @pl.when(pl.program_id(0) == pl.num_programs(0) - 1)
    def _():
        pltpu.make_async_copy(weight_ref, weight_hbm, sem_w).wait()


def project(ids, tokens, down, up, parts):
    rows, width = tokens.shape
    shards = 4 * parts[0].shape[0]
    shard_rows = parts[0].shape[1]
    ff = 4 * width
    tile = 256
    whole = lambda *shape: pl.BlockSpec(shape, lambda i: (0,) * len(shape))
    return pl.pallas_call(
        project_kernel,
        grid=(rows // tile,),
        in_specs=[
            pl.BlockSpec(memory_space=pltpu.SMEM),
            pl.BlockSpec((tile, width), lambda i: (i, 0)),
            whole(*down.shape),
            whole(*up.shape),
        ]
        + [pl.BlockSpec(memory_space=pl.ANY)] * 4,
        out_specs=[
            pl.BlockSpec((tile, 3 * width), lambda i: (i, 0)),
            pl.BlockSpec(memory_space=pl.ANY),
            pl.BlockSpec((2 * down.shape[1], tile), lambda i: (0, i)),
            whole(8, width),
            whole(8, ff),
        ],
        out_shape=[
            jax.ShapeDtypeStruct((rows, 3 * width), bf16),
            jax.ShapeDtypeStruct((width, 3 * width), bf16),
            jax.ShapeDtypeStruct((2 * down.shape[1], rows), bf16),
            jax.ShapeDtypeStruct((8, width), f32),
            jax.ShapeDtypeStruct((8, ff), f32),
        ],
        scratch_shapes=[
            pltpu.VMEM((shards, shard_rows, 3 * width + LANES), bf16),
            pltpu.VMEM((width, 3 * width), bf16),
            pltpu.SemaphoreType.DMA((shards,)),
            pltpu.SemaphoreType.DMA(()),
        ],
        compiler_params=pltpu.CompilerParams(vmem_limit_bytes=VMEM_LIMIT),
        cost_estimate=pl.CostEstimate(
            flops=2 * rows * width * width * 3, bytes_accessed=14 * MIB, transcendentals=0
        ),
    )(ids, tokens, down, up, *parts)


def interleave(programs, lag):
    tick, alive = 0, list(enumerate(programs))
    while alive:
        for item in list(alive):
            if tick >= item[0] * lag:
                try:
                    next(item[1])
                except StopIteration:
                    alive.remove(item)
        tick += 1


def attend_kernel(pack, seg_ref, q_ref, k_ref, v_ref, *rest):
    ctx_ref, w_ref, inverse_ref, hot, cold = rest[-5:]
    rows = seg_ref.shape[1]
    lane = lax.broadcasted_iota(jnp.int32, (1, LANES), 1)

    @pl.when(pl.program_id(0) == 0)
    def _():
        row = jnp.broadcast_to(seg_ref[pack : pack + 1, :].astype(f32), (8, rows))
        column = row.T[:, 0:1]
        slot = jnp.where(lane < HEAD, lane, lane - HEAD).astype(f32)
        hot[...] = jnp.where(column == slot, 1.0, 0.0).astype(bf16)
        cold[...] = jnp.where(column == slot, 0.0, masked_score).astype(bf16)

    sums = {}

    def program(s, h):
        cols = slice(s * LANES, (s + 1) * LANES)
        mine = (lane < HEAD) if h == 0 else (lane >= HEAD)
        q = jnp.where(mine, q_ref[:, cols] * jnp.asarray(HEAD**-0.5, bf16), hot[...])
        scores = nt(q, jnp.where(mine, k_ref[:, cols], cold[...]))
        yield
        peak = jnp.max(scores, axis=-1, keepdims=True)
        exponent = jnp.exp2((scores - peak) * log_e).astype(bf16)
        w_ref[2 * s + h] = exponent
        yield
        v = v_ref[:, cols]
        sums[h] = nn(exponent, jnp.where(mine, v, jnp.ones_like(v)))
        if h == 1:
            top = jnp.where(lane < HEAD, sums[0], sums[1])
            total = pltpu.roll(jnp.where(lane < HEAD, sums[1], sums[0]), HEAD, axis=1)
            inverse = 1.0 / total
            inverse_ref[:, cols] = inverse
            ctx_ref[:, cols] = (top * inverse).astype(bf16)

    interleave([program(s, h) for s in range(q_ref.shape[1] // LANES) for h in range(2)], 1)


HEADS_A_STEP = 4


def attend(pack, segments, qkv, before=()):
    packs, length = segments.shape
    width = qkv.shape[1] // 3
    step = HEADS_A_STEP * HEAD
    steps = width // step
    at = lambda which: pl.BlockSpec((length, step), lambda s: (pack, which * steps + s))
    return pl.pallas_call(
        functools.partial(attend_kernel, pack),
        grid=(steps,),
        in_specs=[pl.BlockSpec((packs, length), lambda s: (0, 0)), at(0), at(1), at(2)]
        + [pl.BlockSpec(memory_space=pl.ANY)] * len(before),
        out_specs=[
            pl.BlockSpec((length, step), lambda s: (pack, s)),
            pl.BlockSpec((HEADS_A_STEP, length, length), lambda s: (pack * steps + s, 0, 0)),
            pl.BlockSpec((length, step), lambda s: (pack, s)),
        ],
        out_shape=[
            jax.ShapeDtypeStruct((packs * length, width), bf16),
            jax.ShapeDtypeStruct((packs * width // HEAD, length, length), bf16),
            jax.ShapeDtypeStruct((packs * length, width), f32),
        ],
        input_output_aliases={4 + i: i for i in range(len(before))},
        scratch_shapes=[pltpu.VMEM((length, LANES), bf16), pltpu.VMEM((length, LANES), bf16)],
        compiler_params=pltpu.CompilerParams(vmem_limit_bytes=VMEM_LIMIT),
        cost_estimate=pl.CostEstimate(
            flops=16 * length * length * width, bytes_accessed=10 * MIB, transcendentals=0
        ),
    )(segments, qkv, qkv, qkv, *before)


def stats(value):
    centred = value - jnp.mean(value, axis=-1, keepdims=True)
    inverse = lax.rsqrt(jnp.mean(centred * centred, axis=-1, keepdims=True) + norm_epsilon)
    return centred * inverse, inverse


def norm_back(grad, normed, inverse, gain):
    scaled = grad * gain
    return inverse * (
        scaled
        - jnp.mean(scaled, axis=-1, keepdims=True)
        - normed * jnp.mean(scaled * normed, axis=-1, keepdims=True)
    )


def gelu_parts(z):
    cumulative = 0.5 + 0.5 * lax.erf(z * root_half)
    density = jnp.exp2(z * z * (-0.5 * log_e)) * root_circle
    return z * cumulative, cumulative + z * density


ROW_TILE = 256
ROW_TILES = 2
ROW_LAG = 12
PIECE = 64
SIDE = 256
FF_CHUNK = 512


def fold(value):
    rows, width = value.shape
    return jnp.sum(value.reshape(rows // 8, 8, width), axis=0)


def rows_kernel(ids_ref, ids_d_ref, x_ref, cot_ref, ctx_ref, small_ref, inner_bias_ref,
                b0, b1, b2, b3, d0, d1, d2, d3,
                act_ref, mid_ref, dctx_ref, sums_ref,
                stage, wo, wi, wf, active, slope, normed, inverse, first, first_b, total, grad_res, grad_b, sem_b, sem_d):
    parts_b, parts_d = (b0, b1, b2, b3), (d0, d1, d2, d3)
    width = x_ref.shape[1]
    taken = d0.shape[1]
    ff = wi.shape[1]
    shard = ff // stage.shape[0]

    @pl.when(pl.program_id(0) == 0)
    def _():
        fetch_blocks(ids_ref, parts_b, stage, sem_b)
        for a, part in enumerate(parts_d):
            for j in range(part.shape[0]):
                at = ids_d_ref[a * part.shape[0] + j]
                place = wf.at[pl.ds(pl.multiple_of(at * shard, shard), taken)]
                pltpu.make_async_copy(part.at[j], place, sem_d.at[at]).start()
        shards, rows = stage.shape[0], stage.shape[1]
        for i in range(0, shards, 2):
            wait_block(parts_b, stage, sem_b, i)
            wait_block(parts_b, stage, sem_b, i + 1)
            for c in range(0, width + ff, width):
                both = jnp.concatenate(
                    [
                        stage[i, :, c : c + width].astype(f32),
                        stage[i + 1, :, c : c + width].astype(f32),
                    ],
                    axis=0,
                ).astype(bf16)
                where = slice(rows * i, rows * (i + 2))
                if c == 0:
                    wo[where] = both
                else:
                    wi[where, c - width : c] = both
            for k in (i, i + 1):
                more = stage[k, :, width + ff :].astype(f32)
                third = more[:, width:]
                eight = [third[8 * n : 8 * (n + 1)] for n in range(3)]
                wf[k * shard + taken : (k + 1) * shard] = jnp.concatenate(
                    [more[:, :width], jnp.concatenate(eight, axis=1)], axis=0
                ).astype(bf16)
        for i in range(shards):
            pltpu.make_async_copy(d0.at[0], wf.at[pl.ds(i * shard, taken)], sem_d.at[i]).wait()
        sums_ref[...] = jnp.zeros_like(sums_ref)

    bias_out, bias_ff = small_ref[2:3], small_ref[3:4]
    gain_one, gain_two = small_ref[4:5], small_ref[5:6]
    shift_one, shift_two = small_ref[6:7], small_ref[7:8]
    sums = [jnp.zeros((8, width), f32) for _ in range(4)]

    def program(t):
        every = slice(t * ROW_TILE, (t + 1) * ROW_TILE)
        pieces = [
            (slice(t * ROW_TILE + p, t * ROW_TILE + p + PIECE), slice(p, p + PIECE))
            for p in range(0, ROW_TILE, PIECE)
        ]
        sides = [slice(c, c + SIDE) for c in range(0, width, SIDE)]
        chunks = [slice(c, c + FF_CHUNK) for c in range(0, ff, FF_CHUNK)]
        for c in sides:
            total[t, :, c] = x_ref[every, c].astype(f32) + (nn(ctx_ref[every], wo[:, c]) + bias_out[:, c])
            yield
        for far, near in pieces:
            n, i = stats(total[t, near])
            normed[t, near] = n
            inverse[t, near] = i
            f = n * gain_one + shift_one
            first[t, near] = f
            first_b[t, near] = f.astype(bf16)
            yield
        for c in chunks:
            value, grad = gelu_parts(nn(first_b[t], wi[:, c]) + inner_bias_ref[0:1, c])
            active[t, :, c] = value.astype(bf16)
            slope[t, :, c] = grad.astype(bf16)
            yield
        for c in sides:
            total[t, :, c] = first[t, :, c] + (nn(active[t], wf[:, c]) + bias_ff[:, c])
            yield
        for far, near in pieces:
            n, i = stats(total[t, near])
            act_ref[far] = (n * gain_two + shift_two).astype(bf16)
            g = cot_ref[far].astype(f32)
            sums[1] = sums[1] + fold(g * n)
            sums[3] = sums[3] + fold(g)
            res = norm_back(g, n, i, gain_two)
            grad_res[t, near] = res
            grad_b[t, near] = res.astype(bf16)
            yield
        for c in chunks:
            grad_active = nt(grad_b[t], wf[c])
            active[t, :, c] = (grad_active * slope[t, :, c].astype(f32)).astype(bf16)
            yield
        for c in sides:
            total[t, :, c] = grad_res[t, :, c] + nt(active[t], wi[c])
            yield
        for far, near in pieces:
            g = total[t, near]
            n = normed[t, near]
            sums[0] = sums[0] + fold(g * n)
            sums[2] = sums[2] + fold(g)
            mid = norm_back(g, n, inverse[t, near], gain_one)
            mid_ref[far] = mid
            grad_b[t, near] = mid.astype(bf16)
            yield
        for c in sides:
            dctx_ref[every, c] = nt(grad_b[t], wo[c]).astype(bf16)
            yield

    interleave([program(t) for t in range(x_ref.shape[0] // ROW_TILE)], ROW_LAG)
    for i, value in enumerate(sums):
        sums_ref[i : i + 1] += jnp.sum(value, axis=0, keepdims=True)


def row_local(ids, ids_d, tokens, cotangent, context, small, inner_bias, parts_b, parts_d):
    rows, width = tokens.shape
    ff = inner_bias.shape[1]
    shards = 4 * parts_b[0].shape[0]
    tile = ROW_TILE * ROW_TILES
    two = lambda w, kind: pltpu.VMEM((ROW_TILES, ROW_TILE, w), kind)
    whole = lambda *shape: pl.BlockSpec(shape, lambda i: (0,) * len(shape))
    tiled = pl.BlockSpec((tile, width), lambda i: (i, 0))
    return pl.pallas_call(
        rows_kernel,
        grid=(rows // tile,),
        in_specs=[
            pl.BlockSpec(memory_space=pltpu.SMEM),
            pl.BlockSpec(memory_space=pltpu.SMEM),
            tiled,
            tiled,
            tiled,
            whole(8, width),
            whole(8, ff),
        ]
        + [pl.BlockSpec(memory_space=pl.ANY)] * 8,
        out_specs=[tiled, tiled, tiled, whole(8, width)],
        out_shape=[
            jax.ShapeDtypeStruct((rows, width), bf16),
            jax.ShapeDtypeStruct((rows, width), f32),
            jax.ShapeDtypeStruct((rows, width), bf16),
            jax.ShapeDtypeStruct((8, width), f32),
        ],
        scratch_shapes=[
            pltpu.VMEM((shards,) + parts_b[0].shape[1:], bf16),
            pltpu.VMEM((width, width), bf16),
            pltpu.VMEM((width, ff), bf16),
            pltpu.VMEM((ff, width), bf16),
            two(ff, bf16),
            two(ff, bf16),
            two(width, f32),
            two(1, f32),
            two(width, f32),
            two(width, bf16),
            two(width, f32),
            two(width, f32),
            two(width, bf16),
            pltpu.SemaphoreType.DMA((shards,)),
            pltpu.SemaphoreType.DMA((shards,)),
        ],
        compiler_params=pltpu.CompilerParams(vmem_limit_bytes=VMEM_LIMIT),
        cost_estimate=pl.CostEstimate(
            flops=2 * rows * width * (4 * ff + 2 * width), bytes_accessed=20 * MIB, transcendentals=0
        ),
    )(ids, ids_d, tokens, cotangent, context, small, inner_bias, *parts_b, *parts_d)


BACK_LAG = 3


def attend_back_kernel(core_ref, x_ref, q_ref, k_ref, v_ref, ctx_ref, dctx_ref, inverse_ref, w_ref, up_ref, red_ref,
                       sums_ref, mid_ref, down_ref, wq_ref, wk_ref, wv_ref, out_ref, keep_ref, send_ref,
                       dq_ref, dk_ref, dv_ref, dred, grads):
    scale = HEAD**-0.5
    pack, step = pl.program_id(0), pl.program_id(1)
    rank = red_ref.shape[0] // 2

    @pl.when((pack == 0) & (step == 0))
    def _():
        grads[...] = jnp.zeros_like(grads)
        keep_ref[...] = jnp.zeros_like(keep_ref)
        send_ref[...] = jnp.zeros_like(send_ref)

    @pl.when(step == 0)
    def _():
        dred[...] = jnp.zeros_like(dred)

    lane = lax.broadcasted_iota(jnp.int32, (1, LANES), 1)
    held = {}

    def program(s, h):
        cols = slice(s * LANES, (s + 1) * LANES)
        mine = (lane < HEAD) if h == 0 else (lane >= HEAD)
        rows = slice(h * HEAD, (h + 1) * HEAD)
        q = q_ref[:, cols]
        zero = jnp.zeros_like(q)
        if h == 0:
            dctx = (dctx_ref[:, cols].astype(f32) * inverse_ref[:, cols]).astype(bf16)
            flat = dctx.astype(f32) * ctx_ref[:, cols].astype(f32)
            held[s] = (dctx, flat, q.T, dctx.T, [], [], [])
        dctx, flat, q_t, dctx_t, dq, dk_t, dv_t = held[s]
        grad_weights = nt(jnp.where(mine, dctx, zero), v_ref[:, cols])
        yield
        delta = jnp.sum(jnp.where(mine, flat, 0.0), axis=-1, keepdims=True)
        weights = w_ref[2 * s + h]
        grad_scores = (weights.astype(f32) * (grad_weights - delta)).astype(bf16)
        yield
        dv_t.append(nn(dctx_t[rows], weights))
        dq.append(nn(grad_scores, jnp.where(mine, k_ref[:, cols], zero)))
        dk_t.append(nn(q_t[rows], grad_scores))
        if h == 1:
            dq_ref[:, cols] = ((dq[0] + dq[1]) * scale).astype(bf16)
            dk_ref[:, cols] = (jnp.concatenate(dk_t, axis=0) * scale).T.astype(bf16)
            dv_ref[:, cols] = jnp.concatenate(dv_t, axis=0).T.astype(bf16)
            del held[s]

    interleave([program(s, h) for s in range(q_ref.shape[1] // LANES) for h in range(2)], BACK_LAG)
    red = red_ref[...]
    up = (2.0 * up_ref[...].astype(bf16).astype(f32)).astype(bf16)
    none = jnp.zeros_like(up[0])
    dq, dv = dq_ref[...], dv_ref[...]
    dred[...] += nt(jnp.concatenate([up[0], none], axis=0), dq) + nt(jnp.concatenate([none, up[1]], axis=0), dv)
    grads[step, 0:rank] += 2.0 * nn(red, dq)[0:rank]
    grads[step, rank : 2 * rank] += 2.0 * nn(red, dv)[rank : 2 * rank]

    grad = nt(dq, wq_ref[...]) + nt(dk_ref[...], wk_ref[...]) + nt(dv, wv_ref[...])

    @pl.when(step == 0)
    def _():
        out_ref[...] = mid_ref[...] + grad

    @pl.when(step > 0)
    def _():
        out_ref[...] += grad

    @pl.when(step == pl.num_programs(1) - 1)
    def _():
        rounded = dred[...].astype(bf16)
        joined = down_ref[...].reshape(2 * rank, down_ref.shape[2]).astype(bf16)
        out_ref[...] += lax.dot_general(rounded, joined, (((0,), (0,)), ((), ())), preferred_element_type=f32)
        down = nn(rounded, x_ref[...])
        raised = jnp.concatenate([grads[i] for i in range(grads.shape[0])], axis=1)
        half = down.shape[1] // 2
        low = (core_ref[0] == 0).astype(f32)
        for out, left in ((keep_ref, low), (send_ref, 1.0 - low)):
            pick = lambda a: jnp.where(left > 0.5, a[:, :half], a[:, half:])
            out[0 : 2 * rank] += pick(down)
            out[2 * rank : 4 * rank] = pick(raised)
            out[4 * rank : 5 * rank] = pick(sums_ref[...])


def attend_back(core, tokens, qkv, context, grad_context, inverse, weights, up, red, sums, mid, down, weight):
    rows, width = context.shape
    length = weights.shape[1]
    rank = up.shape[1]
    step = HEADS_A_STEP * HEAD
    steps = width // step
    at = lambda which: pl.BlockSpec((length, step), lambda p, s: (p, which * steps + s))
    from_weight = lambda which: pl.BlockSpec((width, step), lambda p, s: (0, which * steps + s))
    own = pl.BlockSpec((length, step), lambda p, s: (p, s))
    pack = pl.BlockSpec((length, width), lambda p, s: (p, 0))
    whole = lambda *shape: pl.BlockSpec(shape, lambda p, s: (0,) * len(shape))
    half = whole(5 * rank, width // 2)
    return pl.pallas_call(
        attend_back_kernel,
        grid=(rows // length, steps),
        in_specs=[
            pl.BlockSpec(memory_space=pltpu.SMEM),
            pack,
            at(0),
            at(1),
            at(2),
            own,
            own,
            own,
            pl.BlockSpec((HEADS_A_STEP, length, length), lambda p, s: (p * steps + s, 0, 0)),
            pl.BlockSpec((2, rank, step), lambda p, s: (0, 0, s)),
            pl.BlockSpec((2 * rank, length), lambda p, s: (0, p)),
            whole(*sums.shape),
            pack,
            whole(*down.shape),
            from_weight(0),
            from_weight(1),
            from_weight(2),
        ],
        out_specs=[pack, half, half],
        out_shape=[
            jax.ShapeDtypeStruct((rows, width), f32),
            jax.ShapeDtypeStruct((5 * rank, width // 2), f32),
            jax.ShapeDtypeStruct((5 * rank, width // 2), f32),
        ],
        scratch_shapes=[pltpu.VMEM((length, step), bf16)] * 3
        + [pltpu.VMEM((2 * rank, length), f32), pltpu.VMEM((steps, 2 * rank, step), f32)],
        compiler_params=pltpu.CompilerParams(vmem_limit_bytes=VMEM_LIMIT),
        cost_estimate=pl.CostEstimate(
            flops=32 * rows * length * width, bytes_accessed=28 * MIB, transcendentals=0
        ),
    )(core, tokens, qkv, qkv, qkv, context, grad_context, inverse, weights, up, red, sums, mid, down, weight,
      weight, weight)


def adamw_kernel(count, scal_ref, core_ref, mine_ref, other_ref, down_ref, up_ref, dm_ref, dv_ref, um_ref, uv_ref,
                 gd_ref, gu_ref, gain_ref, shift_ref, pd_ref, pu_ref, dm2_ref, dv2_ref, um2_ref, uv2_ref):
    rank = up_ref.shape[1]
    width = up_ref.shape[2]
    part = 1.0 / count
    first_scale, second_scale, rate = scal_ref[0], scal_ref[1], scal_ref[2]

    def update(param, grad, first, second, learn, decay):
        first_new = beta_one * first + (1.0 - beta_one) * grad
        second_new = beta_two * second + (1.0 - beta_two) * grad * grad
        first_hat = first_new / first_scale
        second_hat = second_new / second_scale
        new = param - learn * (first_hat / (jnp.sqrt(second_hat) + adam_epsilon) + decay * param)
        return new, first_new, second_new

    mine, other = mine_ref[...] * part, other_ref[...] * part
    low = core_ref[0] == 0
    total = jnp.concatenate([jnp.where(low, mine, other), jnp.where(low, other, mine)], axis=1)
    grad_down = total[0 : 2 * rank].reshape(2, rank, width)
    grad_up = total[2 * rank : 4 * rank].reshape(2, rank, width)
    gd_ref[...] = grad_down
    gu_ref[...] = grad_up
    gain_ref[...] = total[4 * rank : 4 * rank + 2]
    shift_ref[...] = total[4 * rank + 2 : 4 * rank + 4]
    pd_ref[...], dm2_ref[...], dv2_ref[...] = update(
        down_ref[...], grad_down, dm_ref[...], dv_ref[...], rate, down_decay_factor
    )
    pu_ref[...], um2_ref[...], uv2_ref[...] = update(
        up_ref[...], grad_up, um_ref[...], uv_ref[...], 16.0 * rate, up_decay_factor
    )


def adamw(count, scalars, core, mine, other, down, up, dm, dv, um, uv):
    width = up.shape[2]
    like = jax.ShapeDtypeStruct(up.shape, f32)
    pair = jax.ShapeDtypeStruct((2, width), f32)
    vmem = pl.BlockSpec(memory_space=pltpu.VMEM)
    smem = pl.BlockSpec(memory_space=pltpu.SMEM)
    return pl.pallas_call(
        functools.partial(adamw_kernel, count),
        in_specs=[smem, smem] + [vmem] * 8,
        out_shape=[like, like, pair, pair] + [like] * 6,
    )(scalars, core, mine, other, down, up, dm, dv, um, uv)


def per_device(
    layout,
    tokens,
    document_numbers,
    query_weight,
    key_weight,
    value_weight,
    output_weight,
    inner_weight,
    outer_weight,
    fixed_projection_bias,
    feedforward_inner_bias,
    layer_norm_gain,
    layer_norm_shift,
    adapter_down_factors,
    adapter_up_factors,
    down_first_moment,
    down_second_moment,
    up_first_moment,
    up_second_moment,
    rate,
    step,
    cotangent,
):
    width = tokens.shape[1]
    shard = query_weight.shape[0]
    small = jnp.concatenate(
        [
            fixed_projection_bias,
            layer_norm_gain,
            layer_norm_shift,
        ],
        axis=0,
    )
    inner_bias = feedforward_inner_bias[None]
    fast = shard % 8 == 0 and shard * layout.n == width and layout.n == 32
    if fast:
        tail = jnp.concatenate(
            [
                jnp.pad(small, ((0, 0), (0, LANES - shard))),
                jnp.pad(inner_bias, ((0, shard - 9), (0, LANES - inner_bias.shape[1]))),
            ],
            axis=0,
        )
        block_a = jnp.concatenate([query_weight, key_weight, value_weight, tail], axis=1)
        extra = outer_weight[OUTER_ROWS:]
        third = extra[shard:].reshape(8, 3, width // 3)
        third = jnp.swapaxes(third, 0, 1).reshape(shard, width // 3)
        block_b = jnp.concatenate([output_weight, inner_weight, extra[:shard], third], axis=1)
        zf, zl = layout.z_first, layout.z_last
        ids = block_ids(layout, zf)
        ids_d = block_ids(layout, zl)
        a, b, d = block_a[None], block_b[None], outer_weight[None, :OUTER_ROWS]
        a1 = stage(a, layout, zf, 0)
        d1 = stage(d, layout, zl, 0)
        a1, d1 = together(a1, d1)
        a, d = join(a, a1), join(d, d1)
        a2 = stage(a, layout, zf, 1)
        d2 = stage(d, layout, zl, 1)
        a2, d2, b = together(a2, d2, b)
        a, d = join(a, a2), join(d, d2)
        a3 = stage(a, layout, zf, 2)
        b1 = stage(b, layout, zf, 0)
        a3, b1 = together(a3, b1)
        a, b = join(a, a3), join(b, b1)
        a4 = stage(a, layout, zf, 3)
        b2 = stage(b, layout, zf, 1)
        a5 = swap_cores(a, layout)
        a4, b2, a5, d = together(a4, b2, a5, d)
        d3 = stage(d, layout, zl, 2)
        a6 = swap_cores(a4, layout)
        b = join(b, b2)
        b3 = stage(b, layout, zf, 2)
        parts_a = (a, a4, a5, a6)
    else:
        count = 32
        rows = width // count
        whole = lambda w: lax.all_gather(w, AXES, axis=0, tiled=True)
        small_full = lax.all_gather(small, AXES, axis=1, tiled=True)
        bias_full = lax.all_gather(inner_bias, AXES, axis=1, tiled=True)
        tail = jnp.concatenate(
            [
                jnp.pad(small_full.reshape(8, count, rows), ((0, 0), (0, 0), (0, LANES - rows))),
                jnp.pad(
                    bias_full.reshape(1, count, -1),
                    ((0, rows - 9), (0, 0), (0, LANES - bias_full.shape[1] // count)),
                ),
            ],
            axis=0,
        )
        tail = jnp.swapaxes(tail, 0, 1).reshape(width, LANES)
        parts_a = as_blocks(
            jnp.concatenate([whole(query_weight), whole(key_weight), whole(value_weight), tail], axis=1), count
        )
        outer = whole(outer_weight).reshape(count, -1, width)
        extra = outer[:, OUTER_ROWS:]
        third = extra[:, rows:].reshape(count, 8, 3, width // 3)
        third = jnp.swapaxes(third, 1, 2).reshape(width, width // 3)
        parts_b = as_blocks(
            jnp.concatenate(
                [whole(output_weight), whole(inner_weight), extra[:, :rows].reshape(width, width), third], axis=1
            ),
            count,
        )
        parts_d = as_blocks(outer[:, :OUTER_ROWS].reshape(-1, width), count)
        ids = ids_d = jnp.arange(count, dtype=jnp.int32)

    turn = lambda v: jnp.swapaxes(v, 1, 2)
    down = turn(adapter_down_factors)
    up = adapter_up_factors
    qkv, weight, red, small_rows, inner_rows = project(ids, tokens, down, up, parts_a)
    if fast:
        b3, d3, qkv = together(b3, d3, qkv)
        b = join(b, b3)
        b4 = stage(b, layout, zf, 3)
        d = join(d, d3)
        d4 = stage(d, layout, zl, 3)
    half = attend(0, document_numbers, qkv)
    if fast:
        b5 = swap_cores(after(b, *half), layout)
        d5 = swap_cores(after(d, *half), layout)
    context, attention, inverse = attend(1, document_numbers, qkv, half)
    if fast:
        b4, d4, context = together(b4, d4, context)
        b6 = swap_cores(b4, layout)
        d6 = swap_cores(d4, layout)
        parts_b = (b, b4, b5, b6)
        parts_d = (d, d4, d5, d6)
    activations, grad_mid, grad_context, sums = row_local(
        ids, ids_d, tokens, cotangent, context, small_rows, inner_rows, parts_b, parts_d
    )
    core = jnp.reshape((lax.axis_index(AXES) & layout.core) != 0, (1,)).astype(jnp.int32)
    input_grad, keep, send = attend_back(
        core, tokens, qkv, context, grad_context, inverse, attention, up, red, sums, grad_mid, down, weight
    )
    total = keep + swap_cores(send, layout)
    total = exchange(total, layout, layout.x_bits + layout.y_bits)
    total = exchange(total, layout, layout.z_bits)
    other = swap_cores(total, layout)
    step_counter = step[0].astype(f32)
    scalars = jnp.stack([1.0 - beta_one**step_counter, 1.0 - beta_two**step_counter, rate[0]])
    gd, gu, gain_grad, shift_grad, pd, pu, dm, dv, um, uv = adamw(
        layout.n,
        scalars,
        core,
        total,
        other,
        down,
        up,
        turn(down_first_moment),
        turn(down_second_moment),
        up_first_moment,
        up_second_moment,
    )
    return (
        activations,
        input_grad,
        turn(gd),
        gu,
        gain_grad,
        shift_grad,
        turn(pd),
        pu,
        turn(dm),
        turn(dv),
        um,
        uv,
    )


def solution(mesh):
    rows = P(AXES, None)
    columns = P(None, AXES)
    in_specs = (
        (rows,) * 8
        + (columns, P(AXES), columns, columns)
        + (P(),) * 8
        + (rows,)
    )
    out_specs = (rows, rows) + (P(),) * 10
    return jax.shard_map(
        functools.partial(per_device, Layout(mesh)),
        mesh=mesh,
        in_specs=in_specs,
        out_specs=out_specs,
        check_vma=False,
    )
```

```python
import functools
import math

import jax
import jax.numpy as jnp
import numpy as np
from jax import lax
from jax.experimental import pallas as pl
from jax.experimental.pallas import tpu as pltpu
from jax.sharding import PartitionSpec as P

HEAD = 64
OUTER_ROWS = 64
AXES = ("dp", "fsdp")

beta_one = 0.9
beta_two = 0.999
adam_epsilon = 1e-08
down_decay_factor = 0.05
up_decay_factor = 0.01
norm_epsilon = 1e-05
masked_score = -1e30
root_half = math.sqrt(0.5)
root_circle = 1.0 / math.sqrt(2.0 * math.pi)
log_e = math.log2(math.e)
LANES = 128
MIB = 1 << 20
VMEM_LIMIT = 60 * MIB

f32 = jnp.float32
bf16 = jnp.bfloat16


def nn(a, b):
    return lax.dot_general(a, b, (((1,), (0,)), ((), ())), preferred_element_type=f32)


def nt(a, b):
    return lax.dot_general(a, b, (((1,), (1,)), ((), ())), preferred_element_type=f32)


class Layout:
    def __init__(self, mesh):
        n_dp, n_fsdp = mesh.shape["dp"], mesh.shape["fsdp"]
        self.n = n_dp * n_fsdp
        self.core = n_fsdp
        n_x = n_dp // 2
        n_y = n_x
        y_bits = [1 << t for t in range(int(math.log2(n_y)))]
        z_bits = [n_y << t for t in range(int(math.log2(n_fsdp // n_y)))]
        x_bits = [(2 * n_fsdp) << t for t in range(int(math.log2(n_x)))]
        self.z_first = (z_bits + x_bits + y_bits, z_bits[::-1] + y_bits + x_bits)
        self.z_last = (x_bits + y_bits + z_bits, y_bits + x_bits + z_bits[::-1])
        self.x_bits, self.y_bits, self.z_bits = x_bits, y_bits, z_bits

    def stage_pairs(self, orders, t):
        return [(i, i ^ orders[1 if i & self.core else 0][t]) for i in range(self.n)]

    def pairs(self, bits):
        return [(i, i ^ bits) for i in range(self.n)]

    def core_pairs(self):
        return [(i, i ^ self.core) for i in range(self.n)]

    def block_masks(self, order):
        masks = [0]
        for bit in order:
            masks = masks + [m ^ bit for m in masks]
        return masks


def after(value, *others):
    return lax.optimization_barrier((value,) + others)[0]


def together(*values):
    return lax.optimization_barrier(values)


def stage(held, layout, orders, t):
    return lax.ppermute(held, AXES, layout.stage_pairs(orders, t))


def swap_cores(value, layout):
    return lax.ppermute(value, AXES, layout.core_pairs())


def join(held, came):
    return jnp.concatenate([held, came], axis=0)


def block_ids(layout, orders):
    me = lax.axis_index(AXES).astype(jnp.int32)
    one, two = (np.array(layout.block_masks(o), np.int32) for o in orders)
    second = (me & layout.core) != 0
    own = me ^ jnp.where(second, two, one)
    other = me ^ layout.core ^ jnp.where(second, one, two)
    return jnp.concatenate([own, other])


def exchange(total, layout, kinds):
    combos = [0]
    for bit in kinds:
        combos = combos + [c ^ bit for c in combos]
    parts = [total] + [lax.ppermute(total, AXES, layout.pairs(c)) for c in combos[1:]]
    while len(parts) > 1:
        parts = [one + two for one, two in zip(parts[::2], parts[1::2])]
    return parts[0]


def as_blocks(full, count):
    return tuple(
        part for part in full.reshape((4, count // 4) + (full.shape[0] // count,) + full.shape[1:])
    )


def fetch_blocks(ids_ref, parts, stage, sems):
    each = parts[0].shape[0]
    for a, part in enumerate(parts):
        for j in range(each):
            k = a * each + j
            at = ids_ref[k]
            pltpu.make_async_copy(part.at[j], stage.at[at], sems.at[at]).start()


def wait_block(parts, stage, sems, i):
    pltpu.make_async_copy(parts[0].at[0], stage.at[i], sems.at[i]).wait()


def merge_pairs(parts, stage, sems, target, width, extra=None):
    shards, rows = stage.shape[0], stage.shape[1]
    for i in range(0, shards, 2):
        wait_block(parts, stage, sems, i)
        wait_block(parts, stage, sems, i + 1)
        for c in range(0, width, 768):
            low = stage[i, :, c : c + 768].astype(f32)
            high = stage[i + 1, :, c : c + 768].astype(f32)
            target[rows * i : rows * (i + 2), c : c + 768] = jnp.concatenate(
                [low, high], axis=0
            ).astype(bf16)


def spread(piece, width, step, count):
    lane = lax.broadcasted_iota(jnp.int32, (LANES, width), 1).astype(f32)
    slot = lax.broadcasted_iota(jnp.int32, (LANES, width), 0).astype(f32)
    within = lane - step * jnp.floor((lane + 0.5) * (1.0 / step))
    place = (within == slot).astype(bf16)
    wide = nn(piece.astype(bf16), place)
    at = lax.broadcasted_iota(jnp.int32, (8, width), 1)
    total = jnp.zeros((8, width), f32)
    for i in range(count):
        mine = (at >= step * i) & (at < step * (i + 1))
        total = total + jnp.where(mine, wide[8 * i : 8 * (i + 1)], 0.0)
    return total


def project_kernel(ids_ref, x_ref, down_ref, up_ref, p0, p1, p2, p3, qkv_ref, weight_hbm, red_ref,
                   small_ref, inner_bias_ref, stage, weight_ref, sems, sem_w):
    parts = (p0, p1, p2, p3)
    width = x_ref.shape[1]
    rank = down_ref.shape[1]

    @pl.when(pl.program_id(0) == 0)
    def _():
        fetch_blocks(ids_ref, parts, stage, sems)
        merge_pairs(parts, stage, sems, weight_ref, 3 * width)
        pltpu.make_async_copy(weight_ref, weight_hbm, sem_w).start()
        shards, rows = stage.shape[0], stage.shape[1]
        tail = stage[:, :, 3 * width :].astype(f32)
        small_ref[...] = spread(tail[:, 0:8].reshape(8 * shards, LANES), width, rows, shards)
        ff = inner_bias_ref.shape[1]
        inner_bias_ref[...] = spread(
            tail[:, 8:16].reshape(8 * shards, LANES), ff, ff // shards, shards
        )

    x = x_ref[...]
    down = down_ref[...].reshape(2 * rank, width).astype(bf16)
    up = (2.0 * up_ref[...].astype(bf16).astype(f32)).astype(bf16)
    zero = jnp.zeros((rank, width), bf16)
    reduced = nt(x, down).astype(bf16)
    red_ref[...] = nt(down, x).astype(bf16)
    up_query = jnp.concatenate([up[0], zero], axis=0)
    up_value = jnp.concatenate([zero, up[1]], axis=0)
    chunk = 256
    for c in range(0, 3 * width, chunk):
        y = nn(x, weight_ref[:, c : c + chunk])
        o = c % width
        if c < width:
            y = y + small_ref[0:1, o : o + chunk] + nn(reduced, up_query[:, o : o + chunk])
        elif c >= 2 * width:
            y = y + small_ref[1:2, o : o + chunk] + nn(reduced, up_value[:, o : o + chunk])
        qkv_ref[:, c : c + chunk] = y.astype(bf16)

    @pl.when(pl.program_id(0) == pl.num_programs(0) - 1)
    def _():
        pltpu.make_async_copy(weight_ref, weight_hbm, sem_w).wait()


def project(ids, tokens, down, up, parts):
    rows, width = tokens.shape
    shards = 4 * parts[0].shape[0]
    shard_rows = parts[0].shape[1]
    ff = 4 * width
    tile = 256
    whole = lambda *shape: pl.BlockSpec(shape, lambda i: (0,) * len(shape))
    return pl.pallas_call(
        project_kernel,
        grid=(rows // tile,),
        in_specs=[
            pl.BlockSpec(memory_space=pltpu.SMEM),
            pl.BlockSpec((tile, width), lambda i: (i, 0)),
            whole(*down.shape),
            whole(*up.shape),
        ]
        + [pl.BlockSpec(memory_space=pl.ANY)] * 4,
        out_specs=[
            pl.BlockSpec((tile, 3 * width), lambda i: (i, 0)),
            pl.BlockSpec(memory_space=pl.ANY),
            pl.BlockSpec((2 * down.shape[1], tile), lambda i: (0, i)),
            whole(8, width),
            whole(8, ff),
        ],
        out_shape=[
            jax.ShapeDtypeStruct((rows, 3 * width), bf16),
            jax.ShapeDtypeStruct((width, 3 * width), bf16),
            jax.ShapeDtypeStruct((2 * down.shape[1], rows), bf16),
            jax.ShapeDtypeStruct((8, width), f32),
            jax.ShapeDtypeStruct((8, ff), f32),
        ],
        scratch_shapes=[
            pltpu.VMEM((shards, shard_rows, 3 * width + LANES), bf16),
            pltpu.VMEM((width, 3 * width), bf16),
            pltpu.SemaphoreType.DMA((shards,)),
            pltpu.SemaphoreType.DMA(()),
        ],
        compiler_params=pltpu.CompilerParams(vmem_limit_bytes=58 * MIB),
        cost_estimate=pl.CostEstimate(
            flops=2 * rows * width * width * 3, bytes_accessed=14 * MIB, transcendentals=0
        ),
    )(ids, tokens, down, up, *parts)


def interleave(programs, lag):
    tick, alive = 0, list(enumerate(programs))
    while alive:
        for item in list(alive):
            if tick >= item[0] * lag:
                try:
                    next(item[1])
                except StopIteration:
                    alive.remove(item)
        tick += 1


def attend_kernel(pack, seg_ref, q_ref, k_ref, v_ref, *rest):
    ctx_ref, w_ref, inverse_ref, hot, cold = rest[-5:]
    rows = seg_ref.shape[1]
    lane = lax.broadcasted_iota(jnp.int32, (1, LANES), 1)

    @pl.when(pl.program_id(0) == 0)
    def _():
        row = jnp.broadcast_to(seg_ref[pack : pack + 1, :].astype(f32), (8, rows))
        column = row.T[:, 0:1]
        slot = jnp.where(lane < HEAD, lane, lane - HEAD).astype(f32)
        hot[...] = jnp.where(column == slot, 1.0, 0.0).astype(bf16)
        cold[...] = jnp.where(column == slot, 0.0, masked_score).astype(bf16)

    sums = {}

    def program(s, h):
        cols = slice(s * LANES, (s + 1) * LANES)
        mine = (lane < HEAD) if h == 0 else (lane >= HEAD)
        q = jnp.where(mine, q_ref[:, cols] * jnp.asarray(HEAD**-0.5, bf16), hot[...])
        scores = nt(q, jnp.where(mine, k_ref[:, cols], cold[...]))
        yield
        peak = jnp.max(scores, axis=-1, keepdims=True)
        exponent = jnp.exp2((scores - peak) * log_e).astype(bf16)
        w_ref[2 * s + h] = exponent
        yield
        v = v_ref[:, cols]
        sums[h] = nn(exponent, jnp.where(mine, v, jnp.ones_like(v)))
        if h == 1:
            top = jnp.where(lane < HEAD, sums[0], sums[1])
            total = pltpu.roll(jnp.where(lane < HEAD, sums[1], sums[0]), HEAD, axis=1)
            inverse = 1.0 / total
            inverse_ref[:, cols] = inverse
            ctx_ref[:, cols] = (top * inverse).astype(bf16)

    interleave([program(s, h) for s in range(q_ref.shape[1] // LANES) for h in range(2)], 1)


HEADS_A_STEP = 4


def attend(pack, segments, qkv, before=()):
    packs, length = segments.shape
    width = qkv.shape[1] // 3
    step = HEADS_A_STEP * HEAD
    steps = width // step
    at = lambda which: pl.BlockSpec((length, step), lambda s: (pack, which * steps + s))
    return pl.pallas_call(
        functools.partial(attend_kernel, pack),
        grid=(steps,),
        in_specs=[pl.BlockSpec((packs, length), lambda s: (0, 0)), at(0), at(1), at(2)]
        + [pl.BlockSpec(memory_space=pl.ANY)] * len(before),
        out_specs=[
            pl.BlockSpec((length, step), lambda s: (pack, s)),
            pl.BlockSpec((HEADS_A_STEP, length, length), lambda s: (pack * steps + s, 0, 0)),
            pl.BlockSpec((length, step), lambda s: (pack, s)),
        ],
        out_shape=[
            jax.ShapeDtypeStruct((packs * length, width), bf16),
            jax.ShapeDtypeStruct((packs * width // HEAD, length, length), bf16),
            jax.ShapeDtypeStruct((packs * length, width), f32),
        ],
        input_output_aliases={4 + i: i for i in range(len(before))},
        scratch_shapes=[pltpu.VMEM((length, LANES), bf16), pltpu.VMEM((length, LANES), bf16)],
        compiler_params=pltpu.CompilerParams(vmem_limit_bytes=VMEM_LIMIT),
        cost_estimate=pl.CostEstimate(
            flops=16 * length * length * width, bytes_accessed=10 * MIB, transcendentals=0
        ),
    )(segments, qkv, qkv, qkv, *before)


def stats(value):
    centred = value - jnp.mean(value, axis=-1, keepdims=True)
    inverse = lax.rsqrt(jnp.mean(centred * centred, axis=-1, keepdims=True) + norm_epsilon)
    return centred * inverse, inverse


def norm_back(grad, normed, inverse, gain):
    scaled = grad * gain
    return inverse * (
        scaled
        - jnp.mean(scaled, axis=-1, keepdims=True)
        - normed * jnp.mean(scaled * normed, axis=-1, keepdims=True)
    )


def gelu_parts(z):
    cumulative = 0.5 + 0.5 * lax.erf(z * root_half)
    density = jnp.exp2(z * z * (-0.5 * log_e)) * root_circle
    return z * cumulative, cumulative + z * density


ROW_TILE = 256
ROW_TILES = 2
ROW_LAG = 8
PIECE = 64
SIDE = 256
FF_CHUNK = 1024


def fold(value):
    rows, width = value.shape
    return jnp.sum(value.reshape(rows // 8, 8, width), axis=0)


def rows_kernel(ids_ref, ids_d_ref, x_ref, cot_ref, ctx_ref, small_ref, inner_bias_ref,
                b0, b1, b2, b3, d0, d1, d2, d3,
                act_ref, mid_ref, dctx_ref, sums_ref,
                stage, wo, wi, wf, active, slope, normed, inverse, first, first_b, total, grad_res, grad_b, sem_b, sem_d):
    parts_b, parts_d = (b0, b1, b2, b3), (d0, d1, d2, d3)
    width = x_ref.shape[1]
    taken = d0.shape[1]
    ff = wi.shape[1]
    shard = ff // stage.shape[0]

    @pl.when(pl.program_id(0) == 0)
    def _():
        fetch_blocks(ids_ref, parts_b, stage, sem_b)
        for a, part in enumerate(parts_d):
            for j in range(part.shape[0]):
                at = ids_d_ref[a * part.shape[0] + j]
                place = wf.at[pl.ds(pl.multiple_of(at * shard, shard), taken)]
                pltpu.make_async_copy(part.at[j], place, sem_d.at[at]).start()
        shards, rows = stage.shape[0], stage.shape[1]
        for i in range(0, shards, 2):
            wait_block(parts_b, stage, sem_b, i)
            wait_block(parts_b, stage, sem_b, i + 1)
            for c in range(0, width + ff, width):
                both = jnp.concatenate(
                    [
                        stage[i, :, c : c + width].astype(f32),
                        stage[i + 1, :, c : c + width].astype(f32),
                    ],
                    axis=0,
                ).astype(bf16)
                where = slice(rows * i, rows * (i + 2))
                if c == 0:
                    wo[where] = both
                else:
                    wi[where, c - width : c] = both
            for k in (i, i + 1):
                more = stage[k, :, width + ff :].astype(f32)
                third = more[:, width:]
                eight = [third[8 * n : 8 * (n + 1)] for n in range(3)]
                wf[k * shard + taken : (k + 1) * shard] = jnp.concatenate(
                    [more[:, :width], jnp.concatenate(eight, axis=1)], axis=0
                ).astype(bf16)
        for i in range(shards):
            pltpu.make_async_copy(d0.at[0], wf.at[pl.ds(i * shard, taken)], sem_d.at[i]).wait()
        sums_ref[...] = jnp.zeros_like(sums_ref)

    bias_out, bias_ff = small_ref[2:3], small_ref[3:4]
    gain_one, gain_two = small_ref[4:5], small_ref[5:6]
    shift_one, shift_two = small_ref[6:7], small_ref[7:8]
    sums = [jnp.zeros((8, width), f32) for _ in range(4)]

    def program(t):
        every = slice(t * ROW_TILE, (t + 1) * ROW_TILE)
        pieces = [
            (slice(t * ROW_TILE + p, t * ROW_TILE + p + PIECE), slice(p, p + PIECE))
            for p in range(0, ROW_TILE, PIECE)
        ]
        sides = [slice(c, c + SIDE) for c in range(0, width, SIDE)]
        chunks = [slice(c, c + FF_CHUNK) for c in range(0, ff, FF_CHUNK)]
        for c in sides:
            total[t, :, c] = x_ref[every, c].astype(f32) + (nn(ctx_ref[every], wo[:, c]) + bias_out[:, c])
            yield
        for far, near in pieces:
            n, i = stats(total[t, near])
            normed[t, near] = n
            inverse[t, near] = i
            f = n * gain_one + shift_one
            first[t, near] = f
            first_b[t, near] = f.astype(bf16)
            yield
        for c in chunks:
            value, grad = gelu_parts(nn(first_b[t], wi[:, c]) + inner_bias_ref[0:1, c])
            active[t, :, c] = value.astype(bf16)
            slope[t, :, c] = grad.astype(bf16)
            yield
        for c in sides:
            total[t, :, c] = first[t, :, c] + (nn(active[t], wf[:, c]) + bias_ff[:, c])
            yield
        for far, near in pieces:
            n, i = stats(total[t, near])
            act_ref[far] = (n * gain_two + shift_two).astype(bf16)
            g = cot_ref[far].astype(f32)
            sums[1] = sums[1] + fold(g * n)
            sums[3] = sums[3] + fold(g)
            res = norm_back(g, n, i, gain_two)
            grad_res[t, near] = res
            grad_b[t, near] = res.astype(bf16)
            yield
        for c in chunks:
            grad_active = nt(grad_b[t], wf[c])
            active[t, :, c] = (grad_active * slope[t, :, c].astype(f32)).astype(bf16)
            yield
        for c in sides:
            total[t, :, c] = grad_res[t, :, c] + nt(active[t], wi[c])
            yield
        for far, near in pieces:
            g = total[t, near]
            n = normed[t, near]
            sums[0] = sums[0] + fold(g * n)
            sums[2] = sums[2] + fold(g)
            mid = norm_back(g, n, inverse[t, near], gain_one)
            mid_ref[far] = mid
            grad_b[t, near] = mid.astype(bf16)
            yield
        for c in sides:
            dctx_ref[every, c] = nt(grad_b[t], wo[c]).astype(bf16)
            yield

    interleave([program(t) for t in range(x_ref.shape[0] // ROW_TILE)], ROW_LAG)
    for i, value in enumerate(sums):
        sums_ref[i : i + 1] += jnp.sum(value, axis=0, keepdims=True)


def row_local(ids, ids_d, tokens, cotangent, context, small, inner_bias, parts_b, parts_d):
    rows, width = tokens.shape
    ff = inner_bias.shape[1]
    shards = 4 * parts_b[0].shape[0]
    tile = ROW_TILE * ROW_TILES
    two = lambda w, kind: pltpu.VMEM((ROW_TILES, ROW_TILE, w), kind)
    whole = lambda *shape: pl.BlockSpec(shape, lambda i: (0,) * len(shape))
    tiled = pl.BlockSpec((tile, width), lambda i: (i, 0))
    return pl.pallas_call(
        rows_kernel,
        grid=(rows // tile,),
        in_specs=[
            pl.BlockSpec(memory_space=pltpu.SMEM),
            pl.BlockSpec(memory_space=pltpu.SMEM),
            tiled,
            tiled,
            tiled,
            whole(8, width),
            whole(8, ff),
        ]
        + [pl.BlockSpec(memory_space=pl.ANY)] * 8,
        out_specs=[tiled, tiled, tiled, whole(8, width)],
        out_shape=[
            jax.ShapeDtypeStruct((rows, width), bf16),
            jax.ShapeDtypeStruct((rows, width), f32),
            jax.ShapeDtypeStruct((rows, width), bf16),
            jax.ShapeDtypeStruct((8, width), f32),
        ],
        scratch_shapes=[
            pltpu.VMEM((shards,) + parts_b[0].shape[1:], bf16),
            pltpu.VMEM((width, width), bf16),
            pltpu.VMEM((width, ff), bf16),
            pltpu.VMEM((ff, width), bf16),
            two(ff, bf16),
            two(ff, bf16),
            two(width, f32),
            two(1, f32),
            two(width, f32),
            two(width, bf16),
            two(width, f32),
            two(width, f32),
            two(width, bf16),
            pltpu.SemaphoreType.DMA((shards,)),
            pltpu.SemaphoreType.DMA((shards,)),
        ],
        compiler_params=pltpu.CompilerParams(vmem_limit_bytes=VMEM_LIMIT),
        cost_estimate=pl.CostEstimate(
            flops=2 * rows * width * (4 * ff + 2 * width), bytes_accessed=20 * MIB, transcendentals=0
        ),
    )(ids, ids_d, tokens, cotangent, context, small, inner_bias, *parts_b, *parts_d)


BACK_LAG = 3


def attend_back_kernel(core_ref, x_ref, q_ref, k_ref, v_ref, ctx_ref, dctx_ref, inverse_ref, w_ref, up_ref, red_ref,
                       sums_ref, mid_ref, down_ref, wq_ref, wk_ref, wv_ref, out_ref, keep_ref, send_ref,
                       dq_ref, dk_ref, dv_ref, dred, grads):
    scale = HEAD**-0.5
    pack, step = pl.program_id(0), pl.program_id(1)
    rank = red_ref.shape[0] // 2

    @pl.when((pack == 0) & (step == 0))
    def _():
        grads[...] = jnp.zeros_like(grads)
        keep_ref[...] = jnp.zeros_like(keep_ref)
        send_ref[...] = jnp.zeros_like(send_ref)

    @pl.when(step == 0)
    def _():
        dred[...] = jnp.zeros_like(dred)

    lane = lax.broadcasted_iota(jnp.int32, (1, LANES), 1)
    held = {}

    def program(s, h):
        cols = slice(s * LANES, (s + 1) * LANES)
        mine = (lane < HEAD) if h == 0 else (lane >= HEAD)
        rows = slice(h * HEAD, (h + 1) * HEAD)
        q = q_ref[:, cols]
        zero = jnp.zeros_like(q)
        if h == 0:
            dctx = (dctx_ref[:, cols].astype(f32) * inverse_ref[:, cols]).astype(bf16)
            flat = dctx.astype(f32) * ctx_ref[:, cols].astype(f32)
            held[s] = (dctx, flat, q.T, dctx.T, [], [], [])
        dctx, flat, q_t, dctx_t, dq, dk_t, dv_t = held[s]
        grad_weights = nt(jnp.where(mine, dctx, zero), v_ref[:, cols])
        yield
        delta = jnp.sum(jnp.where(mine, flat, 0.0), axis=-1, keepdims=True)
        weights = w_ref[2 * s + h]
        grad_scores = (weights.astype(f32) * (grad_weights - delta)).astype(bf16)
        yield
        dv_t.append(nn(dctx_t[rows], weights))
        dq.append(nn(grad_scores, jnp.where(mine, k_ref[:, cols], zero)))
        dk_t.append(nn(q_t[rows], grad_scores))
        if h == 1:
            dq_ref[:, cols] = ((dq[0] + dq[1]) * scale).astype(bf16)
            dk_ref[:, cols] = (jnp.concatenate(dk_t, axis=0) * scale).T.astype(bf16)
            dv_ref[:, cols] = jnp.concatenate(dv_t, axis=0).T.astype(bf16)
            del held[s]

    interleave([program(s, h) for s in range(q_ref.shape[1] // LANES) for h in range(2)], BACK_LAG)
    red = red_ref[...]
    up = (2.0 * up_ref[...].astype(bf16).astype(f32)).astype(bf16)
    none = jnp.zeros_like(up[0])
    dq, dv = dq_ref[...], dv_ref[...]
    dred[...] += nt(jnp.concatenate([up[0], none], axis=0), dq) + nt(jnp.concatenate([none, up[1]], axis=0), dv)
    grads[step, 0:rank] += 2.0 * nn(red, dq)[0:rank]
    grads[step, rank : 2 * rank] += 2.0 * nn(red, dv)[rank : 2 * rank]

    grad = nt(dq, wq_ref[...]) + nt(dk_ref[...], wk_ref[...]) + nt(dv, wv_ref[...])

    @pl.when(step == 0)
    def _():
        out_ref[...] = mid_ref[...] + grad

    @pl.when(step > 0)
    def _():
        out_ref[...] += grad

    @pl.when(step == pl.num_programs(1) - 1)
    def _():
        rounded = dred[...].astype(bf16)
        joined = down_ref[...].reshape(2 * rank, down_ref.shape[2]).astype(bf16)
        out_ref[...] += lax.dot_general(rounded, joined, (((0,), (0,)), ((), ())), preferred_element_type=f32)
        down = nn(rounded, x_ref[...])
        raised = jnp.concatenate([grads[i] for i in range(grads.shape[0])], axis=1)
        half = down.shape[1] // 2
        low = (core_ref[0] == 0).astype(f32)
        for out, left in ((keep_ref, low), (send_ref, 1.0 - low)):
            pick = lambda a: jnp.where(left > 0.5, a[:, :half], a[:, half:])
            out[0 : 2 * rank] += pick(down)
            out[2 * rank : 4 * rank] = pick(raised)
            out[4 * rank : 5 * rank] = pick(sums_ref[...])


def attend_back(core, tokens, qkv, context, grad_context, inverse, weights, up, red, sums, mid, down, weight):
    rows, width = context.shape
    length = weights.shape[1]
    rank = up.shape[1]
    step = HEADS_A_STEP * HEAD
    steps = width // step
    at = lambda which: pl.BlockSpec((length, step), lambda p, s: (p, which * steps + s))
    from_weight = lambda which: pl.BlockSpec((width, step), lambda p, s: (0, which * steps + s))
    own = pl.BlockSpec((length, step), lambda p, s: (p, s))
    pack = pl.BlockSpec((length, width), lambda p, s: (p, 0))
    whole = lambda *shape: pl.BlockSpec(shape, lambda p, s: (0,) * len(shape))
    half = whole(5 * rank, width // 2)
    return pl.pallas_call(
        attend_back_kernel,
        grid=(rows // length, steps),
        in_specs=[
            pl.BlockSpec(memory_space=pltpu.SMEM),
            pack,
            at(0),
            at(1),
            at(2),
            own,
            own,
            own,
            pl.BlockSpec((HEADS_A_STEP, length, length), lambda p, s: (p * steps + s, 0, 0)),
            pl.BlockSpec((2, rank, step), lambda p, s: (0, 0, s)),
            pl.BlockSpec((2 * rank, length), lambda p, s: (0, p)),
            whole(*sums.shape),
            pack,
            whole(*down.shape),
            from_weight(0),
            from_weight(1),
            from_weight(2),
        ],
        out_specs=[pack, half, half],
        out_shape=[
            jax.ShapeDtypeStruct((rows, width), f32),
            jax.ShapeDtypeStruct((5 * rank, width // 2), f32),
            jax.ShapeDtypeStruct((5 * rank, width // 2), f32),
        ],
        scratch_shapes=[pltpu.VMEM((length, step), bf16)] * 3
        + [pltpu.VMEM((2 * rank, length), f32), pltpu.VMEM((steps, 2 * rank, step), f32)],
        compiler_params=pltpu.CompilerParams(vmem_limit_bytes=VMEM_LIMIT),
        cost_estimate=pl.CostEstimate(
            flops=32 * rows * length * width, bytes_accessed=28 * MIB, transcendentals=0
        ),
    )(core, tokens, qkv, qkv, qkv, context, grad_context, inverse, weights, up, red, sums, mid, down, weight,
      weight, weight)


def adamw_kernel(count, scal_ref, core_ref, mine_ref, other_ref, down_ref, up_ref, dm_ref, dv_ref, um_ref, uv_ref,
                 gd_ref, gu_ref, gain_ref, shift_ref, pd_ref, pu_ref, dm2_ref, dv2_ref, um2_ref, uv2_ref):
    rank = up_ref.shape[1]
    width = up_ref.shape[2]
    part = 1.0 / count
    first_scale, second_scale, rate = scal_ref[0], scal_ref[1], scal_ref[2]

    def update(param, grad, first, second, learn, decay):
        first_new = beta_one * first + (1.0 - beta_one) * grad
        second_new = beta_two * second + (1.0 - beta_two) * grad * grad
        first_hat = first_new / first_scale
        second_hat = second_new / second_scale
        new = param - learn * (first_hat / (jnp.sqrt(second_hat) + adam_epsilon) + decay * param)
        return new, first_new, second_new

    mine, other = mine_ref[...] * part, other_ref[...] * part
    low = core_ref[0] == 0
    total = jnp.concatenate([jnp.where(low, mine, other), jnp.where(low, other, mine)], axis=1)
    grad_down = total[0 : 2 * rank].reshape(2, rank, width)
    grad_up = total[2 * rank : 4 * rank].reshape(2, rank, width)
    gd_ref[...] = grad_down
    gu_ref[...] = grad_up
    gain_ref[...] = total[4 * rank : 4 * rank + 2]
    shift_ref[...] = total[4 * rank + 2 : 4 * rank + 4]
    pd_ref[...], dm2_ref[...], dv2_ref[...] = update(
        down_ref[...], grad_down, dm_ref[...], dv_ref[...], rate, down_decay_factor
    )
    pu_ref[...], um2_ref[...], uv2_ref[...] = update(
        up_ref[...], grad_up, um_ref[...], uv_ref[...], 16.0 * rate, up_decay_factor
    )


def adamw(count, scalars, core, mine, other, down, up, dm, dv, um, uv):
    width = up.shape[2]
    like = jax.ShapeDtypeStruct(up.shape, f32)
    pair = jax.ShapeDtypeStruct((2, width), f32)
    vmem = pl.BlockSpec(memory_space=pltpu.VMEM)
    smem = pl.BlockSpec(memory_space=pltpu.SMEM)
    return pl.pallas_call(
        functools.partial(adamw_kernel, count),
        in_specs=[smem, smem] + [vmem] * 8,
        out_shape=[like, like, pair, pair] + [like] * 6,
        compiler_params=pltpu.CompilerParams(vmem_limit_bytes=16 * MIB),
    )(scalars, core, mine, other, down, up, dm, dv, um, uv)


def per_device(
    layout,
    tokens,
    document_numbers,
    query_weight,
    key_weight,
    value_weight,
    output_weight,
    inner_weight,
    outer_weight,
    fixed_projection_bias,
    feedforward_inner_bias,
    layer_norm_gain,
    layer_norm_shift,
    adapter_down_factors,
    adapter_up_factors,
    down_first_moment,
    down_second_moment,
    up_first_moment,
    up_second_moment,
    rate,
    step,
    cotangent,
):
    width = tokens.shape[1]
    shard = query_weight.shape[0]
    small = jnp.concatenate(
        [
            fixed_projection_bias,
            layer_norm_gain,
            layer_norm_shift,
        ],
        axis=0,
    )
    inner_bias = feedforward_inner_bias[None]
    fast = shard % 8 == 0 and shard * layout.n == width and layout.n == 32
    if fast:
        tail = jnp.concatenate(
            [
                jnp.pad(small, ((0, 0), (0, LANES - shard))),
                jnp.pad(inner_bias, ((0, shard - 9), (0, LANES - inner_bias.shape[1]))),
            ],
            axis=0,
        )
        block_a = jnp.concatenate([query_weight, key_weight, value_weight, tail], axis=1)
        extra = outer_weight[OUTER_ROWS:]
        third = extra[shard:].reshape(8, 3, width // 3)
        third = jnp.swapaxes(third, 0, 1).reshape(shard, width // 3)
        block_b = jnp.concatenate([output_weight, inner_weight, extra[:shard], third], axis=1)
        zf, zl = layout.z_first, layout.z_last
        ids = block_ids(layout, zf)
        ids_d = block_ids(layout, zl)
        a, b, d = block_a[None], block_b[None], outer_weight[None, :OUTER_ROWS]
        a1 = stage(a, layout, zf, 0)
        d1 = stage(d, layout, zl, 0)
        a1, d1 = together(a1, d1)
        a, d = join(a, a1), join(d, d1)
        a2 = stage(a, layout, zf, 1)
        d2 = stage(d, layout, zl, 1)
        a2, d2, b = together(a2, d2, b)
        a, d = join(a, a2), join(d, d2)
        a3 = stage(a, layout, zf, 2)
        b1 = stage(b, layout, zf, 0)
        a3, b1 = together(a3, b1)
        a, b = join(a, a3), join(b, b1)
        a4 = stage(a, layout, zf, 3)
        b2 = stage(b, layout, zf, 1)
        a5 = swap_cores(a, layout)
        a4, b2, a5, d = together(a4, b2, a5, d)
        d3 = stage(d, layout, zl, 2)
        a6 = swap_cores(a4, layout)
        b = join(b, b2)
        b3 = stage(b, layout, zf, 2)
        parts_a = (a, a4, a5, a6)
    else:
        count = 32
        rows = width // count
        whole = lambda w: lax.all_gather(w, AXES, axis=0, tiled=True)
        small_full = lax.all_gather(small, AXES, axis=1, tiled=True)
        bias_full = lax.all_gather(inner_bias, AXES, axis=1, tiled=True)
        tail = jnp.concatenate(
            [
                jnp.pad(small_full.reshape(8, count, rows), ((0, 0), (0, 0), (0, LANES - rows))),
                jnp.pad(
                    bias_full.reshape(1, count, -1),
                    ((0, rows - 9), (0, 0), (0, LANES - bias_full.shape[1] // count)),
                ),
            ],
            axis=0,
        )
        tail = jnp.swapaxes(tail, 0, 1).reshape(width, LANES)
        parts_a = as_blocks(
            jnp.concatenate([whole(query_weight), whole(key_weight), whole(value_weight), tail], axis=1), count
        )
        outer = whole(outer_weight).reshape(count, -1, width)
        extra = outer[:, OUTER_ROWS:]
        third = extra[:, rows:].reshape(count, 8, 3, width // 3)
        third = jnp.swapaxes(third, 1, 2).reshape(width, width // 3)
        parts_b = as_blocks(
            jnp.concatenate(
                [whole(output_weight), whole(inner_weight), extra[:, :rows].reshape(width, width), third], axis=1
            ),
            count,
        )
        parts_d = as_blocks(outer[:, :OUTER_ROWS].reshape(-1, width), count)
        ids = ids_d = jnp.arange(count, dtype=jnp.int32)

    turn = lambda v: jnp.swapaxes(v, 1, 2)
    down = turn(adapter_down_factors)
    up = adapter_up_factors
    qkv, weight, red, small_rows, inner_rows = project(ids, tokens, down, up, parts_a)
    if fast:
        b3, d3, qkv = together(b3, d3, qkv)
        b = join(b, b3)
        b4 = stage(b, layout, zf, 3)
        d = join(d, d3)
        d4 = stage(d, layout, zl, 3)
    step_counter = step[0].astype(f32)
    scalars = jnp.stack([1.0 - beta_one**step_counter, 1.0 - beta_two**step_counter, rate[0]])
    core = jnp.reshape((lax.axis_index(AXES) & layout.core) != 0, (1,)).astype(jnp.int32)
    half = attend(0, document_numbers, qkv)
    ids_d, scalars, core, *half = together(ids_d, scalars, core, *half)
    if fast:
        b5 = swap_cores(after(b, *half), layout)
        d5 = swap_cores(after(d, *half), layout)
    context, attention, inverse = attend(1, document_numbers, qkv, half)
    if fast:
        b4, d4, context = together(b4, d4, context)
        b6 = swap_cores(b4, layout)
        d6 = swap_cores(d4, layout)
        parts_b = (b, b4, b5, b6)
        parts_d = (d, d4, d5, d6)
    activations, grad_mid, grad_context, sums = row_local(
        ids, ids_d, tokens, cotangent, context, small_rows, inner_rows, parts_b, parts_d
    )
    input_grad, keep, send = attend_back(
        core, tokens, qkv, context, grad_context, inverse, attention, up, red, sums, grad_mid, down, weight
    )
    total = keep + swap_cores(send, layout)
    total = exchange(total, layout, layout.x_bits + layout.y_bits)
    total = exchange(total, layout, layout.z_bits)
    other = swap_cores(total, layout)
    gd, gu, gain_grad, shift_grad, pd, pu, dm, dv, um, uv = adamw(
        layout.n,
        scalars,
        core,
        total,
        other,
        down,
        up,
        turn(down_first_moment),
        turn(down_second_moment),
        up_first_moment,
        up_second_moment,
    )
    return (
        activations,
        input_grad,
        turn(gd),
        gu,
        gain_grad,
        shift_grad,
        turn(pd),
        pu,
        turn(dm),
        turn(dv),
        um,
        uv,
    )


def solution(mesh):
    rows = P(AXES, None)
    columns = P(None, AXES)
    in_specs = (
        (rows,) * 8
        + (columns, P(AXES), columns, columns)
        + (P(),) * 8
        + (rows,)
    )
    out_specs = (rows, rows) + (P(),) * 10
    return jax.shard_map(
        functools.partial(per_device, Layout(mesh)),
        mesh=mesh,
        in_specs=in_specs,
        out_specs=out_specs,
        check_vma=False,
    )
```

```python
import functools
import math

import jax
import jax.numpy as jnp
import numpy as np
from jax import lax
from jax.experimental import pallas as pl
from jax.experimental.pallas import tpu as pltpu
from jax.sharding import PartitionSpec as P

HEAD = 64
OUTER_ROWS = 64
AXES = ("dp", "fsdp")

beta_one = 0.9
beta_two = 0.999
adam_epsilon = 1e-08
down_decay_factor = 0.05
up_decay_factor = 0.01
norm_epsilon = 1e-05
masked_score = -1e30
root_half = math.sqrt(0.5)
root_circle = 1.0 / math.sqrt(2.0 * math.pi)
log_e = math.log2(math.e)
LANES = 128
MIB = 1 << 20
VMEM_LIMIT = 60 * MIB

f32 = jnp.float32
bf16 = jnp.bfloat16


def nn(a, b):
    return lax.dot_general(a, b, (((1,), (0,)), ((), ())), preferred_element_type=f32)


def nt(a, b):
    return lax.dot_general(a, b, (((1,), (1,)), ((), ())), preferred_element_type=f32)


class Layout:
    def __init__(self, mesh):
        n_dp, n_fsdp = mesh.shape["dp"], mesh.shape["fsdp"]
        self.n = n_dp * n_fsdp
        self.core = n_fsdp
        n_x = n_dp // 2
        n_y = n_x
        y_bits = [1 << t for t in range(int(math.log2(n_y)))]
        z_bits = [n_y << t for t in range(int(math.log2(n_fsdp // n_y)))]
        x_bits = [(2 * n_fsdp) << t for t in range(int(math.log2(n_x)))]
        self.z_first = (z_bits + x_bits + y_bits, z_bits[::-1] + y_bits + x_bits)
        self.z_last = (x_bits + y_bits + z_bits, y_bits + x_bits + z_bits[::-1])
        self.x_bits, self.y_bits, self.z_bits = x_bits, y_bits, z_bits

    def stage_pairs(self, orders, t):
        return [(i, i ^ orders[1 if i & self.core else 0][t]) for i in range(self.n)]

    def pairs(self, bits):
        return [(i, i ^ bits) for i in range(self.n)]

    def core_pairs(self):
        return [(i, i ^ self.core) for i in range(self.n)]

    def block_masks(self, order):
        masks = [0]
        for bit in order:
            masks = masks + [m ^ bit for m in masks]
        return masks


def after(value, *others):
    return lax.optimization_barrier((value,) + others)[0]


def together(*values):
    return lax.optimization_barrier(values)


def stage(held, layout, orders, t):
    return lax.ppermute(held, AXES, layout.stage_pairs(orders, t))


def swap_cores(value, layout):
    return lax.ppermute(value, AXES, layout.core_pairs())


def join(held, came):
    return jnp.concatenate([held, came], axis=0)


def block_ids(layout, orders):
    me = lax.axis_index(AXES).astype(jnp.int32)
    one, two = (np.array(layout.block_masks(o), np.int32) for o in orders)
    second = (me & layout.core) != 0
    own = me ^ jnp.where(second, two, one)
    other = me ^ layout.core ^ jnp.where(second, one, two)
    return jnp.concatenate([own, other])


def exchange(total, layout, kinds):
    combos = [0]
    for bit in kinds:
        combos = combos + [c ^ bit for c in combos]
    parts = [total] + [lax.ppermute(total, AXES, layout.pairs(c)) for c in combos[1:]]
    while len(parts) > 1:
        parts = [one + two for one, two in zip(parts[::2], parts[1::2])]
    return parts[0]


def as_blocks(full, count):
    return tuple(
        part for part in full.reshape((4, count // 4) + (full.shape[0] // count,) + full.shape[1:])
    )


def fetch_blocks(ids_ref, parts, stage, sems):
    each = parts[0].shape[0]
    for a, part in enumerate(parts):
        for j in range(each):
            k = a * each + j
            at = ids_ref[k]
            pltpu.make_async_copy(part.at[j], stage.at[at], sems.at[at]).start()


def wait_block(parts, stage, sems, i):
    pltpu.make_async_copy(parts[0].at[0], stage.at[i], sems.at[i]).wait()


def merge_pairs(parts, stage, sems, target, width, extra=None):
    shards, rows = stage.shape[0], stage.shape[1]
    for i in range(0, shards, 2):
        wait_block(parts, stage, sems, i)
        wait_block(parts, stage, sems, i + 1)
        for c in range(0, width, 768):
            low = stage[i, :, c : c + 768].astype(f32)
            high = stage[i + 1, :, c : c + 768].astype(f32)
            target[rows * i : rows * (i + 2), c : c + 768] = jnp.concatenate(
                [low, high], axis=0
            ).astype(bf16)


def spread(piece, width, step, count):
    lane = lax.broadcasted_iota(jnp.int32, (LANES, width), 1).astype(f32)
    slot = lax.broadcasted_iota(jnp.int32, (LANES, width), 0).astype(f32)
    within = lane - step * jnp.floor((lane + 0.5) * (1.0 / step))
    place = (within == slot).astype(bf16)
    wide = nn(piece.astype(bf16), place)
    at = lax.broadcasted_iota(jnp.int32, (8, width), 1)
    total = jnp.zeros((8, width), f32)
    for i in range(count):
        mine = (at >= step * i) & (at < step * (i + 1))
        total = total + jnp.where(mine, wide[8 * i : 8 * (i + 1)], 0.0)
    return total


def project_kernel(ids_ref, x_ref, down_ref, up_ref, p0, p1, p2, p3, qkv_ref, weight_hbm, red_ref,
                   small_ref, inner_bias_ref, stage, weight_ref, sems, sem_w):
    parts = (p0, p1, p2, p3)
    width = x_ref.shape[1]
    rank = down_ref.shape[1]

    @pl.when(pl.program_id(0) == 0)
    def _():
        fetch_blocks(ids_ref, parts, stage, sems)
        merge_pairs(parts, stage, sems, weight_ref, 3 * width)
        pltpu.make_async_copy(weight_ref, weight_hbm, sem_w).start()
        shards, rows = stage.shape[0], stage.shape[1]
        tail = stage[:, :, 3 * width :].astype(f32)
        small_ref[...] = spread(tail[:, 0:8].reshape(8 * shards, LANES), width, rows, shards)
        ff = inner_bias_ref.shape[1]
        inner_bias_ref[...] = spread(
            tail[:, 8:16].reshape(8 * shards, LANES), ff, ff // shards, shards
        )

    x = x_ref[...]
    down = down_ref[...].reshape(2 * rank, width).astype(bf16)
    up = (2.0 * up_ref[...].astype(bf16).astype(f32)).astype(bf16)
    zero = jnp.zeros((rank, width), bf16)
    reduced = nt(x, down).astype(bf16)
    red_ref[...] = nt(down, x).astype(bf16)
    up_query = jnp.concatenate([up[0], zero], axis=0)
    up_value = jnp.concatenate([zero, up[1]], axis=0)
    chunk = 256
    for c in range(0, 3 * width, chunk):
        y = nn(x, weight_ref[:, c : c + chunk])
        o = c % width
        if c < width:
            y = y + small_ref[0:1, o : o + chunk] + nn(reduced, up_query[:, o : o + chunk])
        elif c >= 2 * width:
            y = y + small_ref[1:2, o : o + chunk] + nn(reduced, up_value[:, o : o + chunk])
        qkv_ref[:, c : c + chunk] = y.astype(bf16)

    @pl.when(pl.program_id(0) == pl.num_programs(0) - 1)
    def _():
        pltpu.make_async_copy(weight_ref, weight_hbm, sem_w).wait()


def project(ids, tokens, down, up, parts):
    rows, width = tokens.shape
    shards = 4 * parts[0].shape[0]
    shard_rows = parts[0].shape[1]
    ff = 4 * width
    tile = 256
    whole = lambda *shape: pl.BlockSpec(shape, lambda i: (0,) * len(shape))
    return pl.pallas_call(
        project_kernel,
        grid=(rows // tile,),
        in_specs=[
            pl.BlockSpec(memory_space=pltpu.SMEM),
            pl.BlockSpec((tile, width), lambda i: (i, 0)),
            whole(*down.shape),
            whole(*up.shape),
        ]
        + [pl.BlockSpec(memory_space=pl.ANY)] * 4,
        out_specs=[
            pl.BlockSpec((tile, 3 * width), lambda i: (i, 0)),
            pl.BlockSpec(memory_space=pl.ANY),
            pl.BlockSpec((2 * down.shape[1], tile), lambda i: (0, i)),
            whole(8, width),
            whole(8, ff),
        ],
        out_shape=[
            jax.ShapeDtypeStruct((rows, 3 * width), bf16),
            jax.ShapeDtypeStruct((width, 3 * width), bf16),
            jax.ShapeDtypeStruct((2 * down.shape[1], rows), bf16),
            jax.ShapeDtypeStruct((8, width), f32),
            jax.ShapeDtypeStruct((8, ff), f32),
        ],
        scratch_shapes=[
            pltpu.VMEM((shards, shard_rows, 3 * width + LANES), bf16),
            pltpu.VMEM((width, 3 * width), bf16),
            pltpu.SemaphoreType.DMA((shards,)),
            pltpu.SemaphoreType.DMA(()),
        ],
        compiler_params=pltpu.CompilerParams(vmem_limit_bytes=58 * MIB),
        cost_estimate=pl.CostEstimate(
            flops=2 * rows * width * width * 3, bytes_accessed=14 * MIB, transcendentals=0
        ),
    )(ids, tokens, down, up, *parts)


def interleave(programs, lag):
    tick, alive = 0, list(enumerate(programs))
    while alive:
        for item in list(alive):
            if tick >= item[0] * lag:
                try:
                    next(item[1])
                except StopIteration:
                    alive.remove(item)
        tick += 1


def attend_kernel(pack, seg_ref, q_ref, k_ref, v_ref, *rest):
    ctx_ref, w_ref, inverse_ref, hot, cold = rest[-5:]
    rows = seg_ref.shape[1]
    lane = lax.broadcasted_iota(jnp.int32, (1, LANES), 1)

    @pl.when(pl.program_id(0) == 0)
    def _():
        row = jnp.broadcast_to(seg_ref[pack : pack + 1, :].astype(f32), (8, rows))
        column = row.T[:, 0:1]
        slot = jnp.where(lane < HEAD, lane, lane - HEAD).astype(f32)
        hot[...] = jnp.where(column == slot, 1.0, 0.0).astype(bf16)
        cold[...] = jnp.where(column == slot, 0.0, masked_score).astype(bf16)

    sums = {}

    def program(s, h):
        cols = slice(s * LANES, (s + 1) * LANES)
        mine = (lane < HEAD) if h == 0 else (lane >= HEAD)
        q = jnp.where(mine, q_ref[:, cols] * jnp.asarray(HEAD**-0.5, bf16), hot[...])
        scores = nt(q, jnp.where(mine, k_ref[:, cols], cold[...]))
        yield
        peak = jnp.max(scores, axis=-1, keepdims=True)
        exponent = jnp.exp2((scores - peak) * log_e).astype(bf16)
        w_ref[2 * s + h] = exponent
        yield
        v = v_ref[:, cols]
        sums[h] = nn(exponent, jnp.where(mine, v, jnp.ones_like(v)))
        if h == 1:
            top = jnp.where(lane < HEAD, sums[0], sums[1])
            total = pltpu.roll(jnp.where(lane < HEAD, sums[1], sums[0]), HEAD, axis=1)
            inverse = 1.0 / total
            inverse_ref[:, cols] = inverse
            ctx_ref[:, cols] = (top * inverse).astype(bf16)

    interleave([program(s, h) for s in range(q_ref.shape[1] // LANES) for h in range(2)], 1)


HEADS_A_STEP = 4


def attend(pack, segments, qkv, before=()):
    packs, length = segments.shape
    width = qkv.shape[1] // 3
    step = HEADS_A_STEP * HEAD
    steps = width // step
    at = lambda which: pl.BlockSpec((length, step), lambda s: (pack, which * steps + s))
    return pl.pallas_call(
        functools.partial(attend_kernel, pack),
        grid=(steps,),
        in_specs=[pl.BlockSpec((packs, length), lambda s: (0, 0)), at(0), at(1), at(2)]
        + [pl.BlockSpec(memory_space=pl.ANY)] * len(before),
        out_specs=[
            pl.BlockSpec((length, step), lambda s: (pack, s)),
            pl.BlockSpec((HEADS_A_STEP, length, length), lambda s: (pack * steps + s, 0, 0)),
            pl.BlockSpec((length, step), lambda s: (pack, s)),
        ],
        out_shape=[
            jax.ShapeDtypeStruct((packs * length, width), bf16),
            jax.ShapeDtypeStruct((packs * width // HEAD, length, length), bf16),
            jax.ShapeDtypeStruct((packs * length, width), f32),
        ],
        input_output_aliases={4 + i: i for i in range(len(before))},
        scratch_shapes=[pltpu.VMEM((length, LANES), bf16), pltpu.VMEM((length, LANES), bf16)],
        compiler_params=pltpu.CompilerParams(vmem_limit_bytes=VMEM_LIMIT),
        cost_estimate=pl.CostEstimate(
            flops=16 * length * length * width, bytes_accessed=10 * MIB, transcendentals=0
        ),
    )(segments, qkv, qkv, qkv, *before)


def stats(value):
    centred = value - jnp.mean(value, axis=-1, keepdims=True)
    inverse = lax.rsqrt(jnp.mean(centred * centred, axis=-1, keepdims=True) + norm_epsilon)
    return centred * inverse, inverse


def norm_back(grad, normed, inverse, gain):
    scaled = grad * gain
    return inverse * (
        scaled
        - jnp.mean(scaled, axis=-1, keepdims=True)
        - normed * jnp.mean(scaled * normed, axis=-1, keepdims=True)
    )


def gelu_parts(z):
    cumulative = 0.5 + 0.5 * lax.erf(z * root_half)
    density = jnp.exp2(z * z * (-0.5 * log_e)) * root_circle
    return z * cumulative, cumulative + z * density


ROW_TILE = 256
ROW_TILES = 2
ROW_LAG = 8
PIECE = 64
SIDE = 256
FF_CHUNK = 1024


def fold(value):
    rows, width = value.shape
    return jnp.sum(value.reshape(rows // 8, 8, width), axis=0)


def rows_kernel(ids_ref, ids_d_ref, x_ref, cot_ref, ctx_ref, small_ref, inner_bias_ref,
                b0, b1, b2, b3, d0, d1, d2, d3,
                act_ref, mid_ref, dctx_ref, sums_ref,
                stage, wo, wi, wf, active, slope, normed, inverse, first, first_b, total, grad_res, grad_b, sem_b, sem_d):
    parts_b, parts_d = (b0, b1, b2, b3), (d0, d1, d2, d3)
    width = x_ref.shape[1]
    taken = d0.shape[1]
    ff = wi.shape[1]
    shard = ff // stage.shape[0]

    @pl.when(pl.program_id(0) == 0)
    def _():
        fetch_blocks(ids_ref, parts_b, stage, sem_b)
        for a, part in enumerate(parts_d):
            for j in range(part.shape[0]):
                at = ids_d_ref[a * part.shape[0] + j]
                place = wf.at[pl.ds(pl.multiple_of(at * shard, shard), taken)]
                pltpu.make_async_copy(part.at[j], place, sem_d.at[at]).start()
        shards, rows = stage.shape[0], stage.shape[1]
        for i in range(0, shards, 2):
            wait_block(parts_b, stage, sem_b, i)
            wait_block(parts_b, stage, sem_b, i + 1)
            for c in range(0, width + ff, width):
                both = jnp.concatenate(
                    [
                        stage[i, :, c : c + width].astype(f32),
                        stage[i + 1, :, c : c + width].astype(f32),
                    ],
                    axis=0,
                ).astype(bf16)
                where = slice(rows * i, rows * (i + 2))
                if c == 0:
                    wo[where] = both
                else:
                    wi[where, c - width : c] = both
            for k in (i, i + 1):
                more = stage[k, :, width + ff :].astype(f32)
                third = more[:, width:]
                eight = [third[8 * n : 8 * (n + 1)] for n in range(3)]
                wf[k * shard + taken : (k + 1) * shard] = jnp.concatenate(
                    [more[:, :width], jnp.concatenate(eight, axis=1)], axis=0
                ).astype(bf16)
        for i in range(shards):
            pltpu.make_async_copy(d0.at[0], wf.at[pl.ds(i * shard, taken)], sem_d.at[i]).wait()
        sums_ref[...] = jnp.zeros_like(sums_ref)

    bias_out, bias_ff = small_ref[2:3], small_ref[3:4]
    gain_one, gain_two = small_ref[4:5], small_ref[5:6]
    shift_one, shift_two = small_ref[6:7], small_ref[7:8]
    sums = [jnp.zeros((8, width), f32) for _ in range(4)]

    def program(t):
        every = slice(t * ROW_TILE, (t + 1) * ROW_TILE)
        pieces = [
            (slice(t * ROW_TILE + p, t * ROW_TILE + p + PIECE), slice(p, p + PIECE))
            for p in range(0, ROW_TILE, PIECE)
        ]
        sides = [slice(c, c + SIDE) for c in range(0, width, SIDE)]
        chunks = [slice(c, c + FF_CHUNK) for c in range(0, ff, FF_CHUNK)]
        for c in sides:
            total[t, :, c] = x_ref[every, c].astype(f32) + (nn(ctx_ref[every], wo[:, c]) + bias_out[:, c])
            yield
        for far, near in pieces:
            n, i = stats(total[t, near])
            normed[t, near] = n
            inverse[t, near] = i
            f = n * gain_one + shift_one
            first[t, near] = f
            first_b[t, near] = f.astype(bf16)
            yield
        for c in chunks:
            value, grad = gelu_parts(nn(first_b[t], wi[:, c]) + inner_bias_ref[0:1, c])
            active[t, :, c] = value.astype(bf16)
            slope[t, :, c] = grad.astype(bf16)
            yield
        for c in sides:
            total[t, :, c] = first[t, :, c] + (nn(active[t], wf[:, c]) + bias_ff[:, c])
            yield
        for far, near in pieces:
            n, i = stats(total[t, near])
            act_ref[far] = (n * gain_two + shift_two).astype(bf16)
            g = cot_ref[far].astype(f32)
            sums[1] = sums[1] + fold(g * n)
            sums[3] = sums[3] + fold(g)
            res = norm_back(g, n, i, gain_two)
            grad_res[t, near] = res
            grad_b[t, near] = res.astype(bf16)
            yield
        for c in chunks:
            grad_active = nt(grad_b[t], wf[c])
            active[t, :, c] = (grad_active * slope[t, :, c].astype(f32)).astype(bf16)
            yield
        for c in sides:
            total[t, :, c] = grad_res[t, :, c] + nt(active[t], wi[c])
            yield
        for far, near in pieces:
            g = total[t, near]
            n = normed[t, near]
            sums[0] = sums[0] + fold(g * n)
            sums[2] = sums[2] + fold(g)
            mid = norm_back(g, n, inverse[t, near], gain_one)
            mid_ref[far] = mid
            grad_b[t, near] = mid.astype(bf16)
            yield
        for c in sides:
            dctx_ref[every, c] = nt(grad_b[t], wo[c]).astype(bf16)
            yield

    interleave([program(t) for t in range(x_ref.shape[0] // ROW_TILE)], ROW_LAG)
    for i, value in enumerate(sums):
        sums_ref[i : i + 1] += jnp.sum(value, axis=0, keepdims=True)


def row_local(ids, ids_d, tokens, cotangent, context, small, inner_bias, parts_b, parts_d):
    rows, width = tokens.shape
    ff = inner_bias.shape[1]
    shards = 4 * parts_b[0].shape[0]
    tile = ROW_TILE * ROW_TILES
    two = lambda w, kind: pltpu.VMEM((ROW_TILES, ROW_TILE, w), kind)
    whole = lambda *shape: pl.BlockSpec(shape, lambda i: (0,) * len(shape))
    tiled = pl.BlockSpec((tile, width), lambda i: (i, 0))
    return pl.pallas_call(
        rows_kernel,
        grid=(rows // tile,),
        in_specs=[
            pl.BlockSpec(memory_space=pltpu.SMEM),
            pl.BlockSpec(memory_space=pltpu.SMEM),
            tiled,
            tiled,
            tiled,
            whole(8, width),
            whole(8, ff),
        ]
        + [pl.BlockSpec(memory_space=pl.ANY)] * 8,
        out_specs=[tiled, tiled, tiled, whole(8, width)],
        out_shape=[
            jax.ShapeDtypeStruct((rows, width), bf16),
            jax.ShapeDtypeStruct((rows, width), f32),
            jax.ShapeDtypeStruct((rows, width), bf16),
            jax.ShapeDtypeStruct((8, width), f32),
        ],
        scratch_shapes=[
            pltpu.VMEM((shards,) + parts_b[0].shape[1:], bf16),
            pltpu.VMEM((width, width), bf16),
            pltpu.VMEM((width, ff), bf16),
            pltpu.VMEM((ff, width), bf16),
            two(ff, bf16),
            two(ff, bf16),
            two(width, f32),
            two(1, f32),
            two(width, f32),
            two(width, bf16),
            two(width, f32),
            two(width, f32),
            two(width, bf16),
            pltpu.SemaphoreType.DMA((shards,)),
            pltpu.SemaphoreType.DMA((shards,)),
        ],
        compiler_params=pltpu.CompilerParams(vmem_limit_bytes=VMEM_LIMIT),
        cost_estimate=pl.CostEstimate(
            flops=2 * rows * width * (4 * ff + 2 * width), bytes_accessed=20 * MIB, transcendentals=0
        ),
    )(ids, ids_d, tokens, cotangent, context, small, inner_bias, *parts_b, *parts_d)


BACK_LAG = 1


def attend_back_kernel(core_ref, x_ref, q_ref, k_ref, v_ref, ctx_ref, dctx_ref, inverse_ref, w_ref, up_ref, red_ref,
                       sums_ref, mid_ref, down_ref, wq_ref, wk_ref, wv_ref, out_ref, keep_ref, send_ref,
                       dq_ref, dk_ref, dv_ref, dred, grads):
    scale = HEAD**-0.5
    pack, step = pl.program_id(0), pl.program_id(1)
    rank = red_ref.shape[0] // 2

    @pl.when((pack == 0) & (step == 0))
    def _():
        grads[...] = jnp.zeros_like(grads)
        keep_ref[...] = jnp.zeros_like(keep_ref)
        send_ref[...] = jnp.zeros_like(send_ref)

    @pl.when(step == 0)
    def _():
        dred[...] = jnp.zeros_like(dred)

    lane = lax.broadcasted_iota(jnp.int32, (1, LANES), 1)
    held = {}

    def program(s, h):
        cols = slice(s * LANES, (s + 1) * LANES)
        mine = (lane < HEAD) if h == 0 else (lane >= HEAD)
        rows = slice(h * HEAD, (h + 1) * HEAD)
        q = q_ref[:, cols]
        zero = jnp.zeros_like(q)
        if h == 0:
            dctx = (dctx_ref[:, cols].astype(f32) * inverse_ref[:, cols]).astype(bf16)
            flat = dctx.astype(f32) * ctx_ref[:, cols].astype(f32)
            held[s] = (dctx, flat, q.T, dctx.T, [], [], [])
        dctx, flat, q_t, dctx_t, dq, dk_t, dv_t = held[s]
        grad_weights = nt(jnp.where(mine, dctx, zero), v_ref[:, cols])
        yield
        delta = jnp.sum(jnp.where(mine, flat, 0.0), axis=-1, keepdims=True)
        weights = w_ref[2 * s + h]
        grad_scores = (weights.astype(f32) * (grad_weights - delta)).astype(bf16)
        yield
        dv_t.append(nn(dctx_t[rows], weights))
        dq.append(nn(grad_scores, jnp.where(mine, k_ref[:, cols], zero)))
        dk_t.append(nn(q_t[rows], grad_scores))
        if h == 1:
            dq_ref[:, cols] = ((dq[0] + dq[1]) * scale).astype(bf16)
            dk_ref[:, cols] = (jnp.concatenate(dk_t, axis=0) * scale).T.astype(bf16)
            dv_ref[:, cols] = jnp.concatenate(dv_t, axis=0).T.astype(bf16)
            del held[s]

    interleave([program(s, h) for s in range(q_ref.shape[1] // LANES) for h in range(2)], BACK_LAG)
    red = red_ref[...]
    up = (2.0 * up_ref[...].astype(bf16).astype(f32)).astype(bf16)
    none = jnp.zeros_like(up[0])
    dq, dv = dq_ref[...], dv_ref[...]
    dred[...] += nt(jnp.concatenate([up[0], none], axis=0), dq) + nt(jnp.concatenate([none, up[1]], axis=0), dv)
    grads[step, 0:rank] += 2.0 * nn(red, dq)[0:rank]
    grads[step, rank : 2 * rank] += 2.0 * nn(red, dv)[rank : 2 * rank]

    grad = nt(dq, wq_ref[...]) + nt(dk_ref[...], wk_ref[...]) + nt(dv, wv_ref[...])

    @pl.when(step == 0)
    def _():
        out_ref[...] = mid_ref[...] + grad

    @pl.when(step > 0)
    def _():
        out_ref[...] += grad

    @pl.when(step == pl.num_programs(1) - 1)
    def _():
        rounded = dred[...].astype(bf16)
        joined = down_ref[...].reshape(2 * rank, down_ref.shape[2]).astype(bf16)
        out_ref[...] += lax.dot_general(rounded, joined, (((0,), (0,)), ((), ())), preferred_element_type=f32)
        down = nn(rounded, x_ref[...])
        raised = jnp.concatenate([grads[i] for i in range(grads.shape[0])], axis=1)
        half = down.shape[1] // 2
        low = (core_ref[0] == 0).astype(f32)
        for out, left in ((keep_ref, low), (send_ref, 1.0 - low)):
            pick = lambda a: jnp.where(left > 0.5, a[:, :half], a[:, half:])
            out[0 : 2 * rank] += pick(down)
            out[2 * rank : 4 * rank] = pick(raised)
            out[4 * rank : 5 * rank] = pick(sums_ref[...])


def attend_back(core, tokens, qkv, context, grad_context, inverse, weights, up, red, sums, mid, down, weight):
    rows, width = context.shape
    length = weights.shape[1]
    rank = up.shape[1]
    step = HEADS_A_STEP * HEAD
    steps = width // step
    at = lambda which: pl.BlockSpec((length, step), lambda p, s: (p, which * steps + s))
    from_weight = lambda which: pl.BlockSpec((width, step), lambda p, s: (0, which * steps + s))
    own = pl.BlockSpec((length, step), lambda p, s: (p, s))
    pack = pl.BlockSpec((length, width), lambda p, s: (p, 0))
    whole = lambda *shape: pl.BlockSpec(shape, lambda p, s: (0,) * len(shape))
    half = whole(5 * rank, width // 2)
    return pl.pallas_call(
        attend_back_kernel,
        grid=(rows // length, steps),
        in_specs=[
            pl.BlockSpec(memory_space=pltpu.SMEM),
            pack,
            at(0),
            at(1),
            at(2),
            own,
            own,
            own,
            pl.BlockSpec((HEADS_A_STEP, length, length), lambda p, s: (p * steps + s, 0, 0)),
            pl.BlockSpec((2, rank, step), lambda p, s: (0, 0, s)),
            pl.BlockSpec((2 * rank, length), lambda p, s: (0, p)),
            whole(*sums.shape),
            pack,
            whole(*down.shape),
            from_weight(0),
            from_weight(1),
            from_weight(2),
        ],
        out_specs=[pack, half, half],
        out_shape=[
            jax.ShapeDtypeStruct((rows, width), f32),
            jax.ShapeDtypeStruct((5 * rank, width // 2), f32),
            jax.ShapeDtypeStruct((5 * rank, width // 2), f32),
        ],
        scratch_shapes=[pltpu.VMEM((length, step), bf16)] * 3
        + [pltpu.VMEM((2 * rank, length), f32), pltpu.VMEM((steps, 2 * rank, step), f32)],
        compiler_params=pltpu.CompilerParams(vmem_limit_bytes=VMEM_LIMIT),
        cost_estimate=pl.CostEstimate(
            flops=32 * rows * length * width, bytes_accessed=28 * MIB, transcendentals=0
        ),
    )(core, tokens, qkv, qkv, qkv, context, grad_context, inverse, weights, up, red, sums, mid, down, weight,
      weight, weight)


def adamw_kernel(count, scal_ref, core_ref, mine_ref, other_ref, down_ref, up_ref, dm_ref, dv_ref, um_ref, uv_ref,
                 gd_ref, gu_ref, gain_ref, shift_ref, pd_ref, pu_ref, dm2_ref, dv2_ref, um2_ref, uv2_ref):
    rank = up_ref.shape[1]
    width = up_ref.shape[2]
    part = 1.0 / count
    first_scale, second_scale, rate = scal_ref[0], scal_ref[1], scal_ref[2]

    def update(param, grad, first, second, learn, decay):
        first_new = beta_one * first + (1.0 - beta_one) * grad
        second_new = beta_two * second + (1.0 - beta_two) * grad * grad
        first_hat = first_new / first_scale
        second_hat = second_new / second_scale
        new = param - learn * (first_hat / (jnp.sqrt(second_hat) + adam_epsilon) + decay * param)
        return new, first_new, second_new

    mine, other = mine_ref[...] * part, other_ref[...] * part
    low = core_ref[0] == 0
    total = jnp.concatenate([jnp.where(low, mine, other), jnp.where(low, other, mine)], axis=1)
    grad_down = total[0 : 2 * rank].reshape(2, rank, width)
    grad_up = total[2 * rank : 4 * rank].reshape(2, rank, width)
    gd_ref[...] = grad_down
    gu_ref[...] = grad_up
    gain_ref[...] = total[4 * rank : 4 * rank + 2]
    shift_ref[...] = total[4 * rank + 2 : 4 * rank + 4]
    pd_ref[...], dm2_ref[...], dv2_ref[...] = update(
        down_ref[...], grad_down, dm_ref[...], dv_ref[...], rate, down_decay_factor
    )
    pu_ref[...], um2_ref[...], uv2_ref[...] = update(
        up_ref[...], grad_up, um_ref[...], uv_ref[...], 16.0 * rate, up_decay_factor
    )


def adamw(count, scalars, core, mine, other, down, up, dm, dv, um, uv):
    width = up.shape[2]
    like = jax.ShapeDtypeStruct(up.shape, f32)
    pair = jax.ShapeDtypeStruct((2, width), f32)
    vmem = pl.BlockSpec(memory_space=pltpu.VMEM)
    smem = pl.BlockSpec(memory_space=pltpu.SMEM)
    return pl.pallas_call(
        functools.partial(adamw_kernel, count),
        in_specs=[smem, smem] + [vmem] * 8,
        out_shape=[like, like, pair, pair] + [like] * 6,
        compiler_params=pltpu.CompilerParams(vmem_limit_bytes=16 * MIB),
    )(scalars, core, mine, other, down, up, dm, dv, um, uv)


def per_device(
    layout,
    tokens,
    document_numbers,
    query_weight,
    key_weight,
    value_weight,
    output_weight,
    inner_weight,
    outer_weight,
    fixed_projection_bias,
    feedforward_inner_bias,
    layer_norm_gain,
    layer_norm_shift,
    adapter_down_factors,
    adapter_up_factors,
    down_first_moment,
    down_second_moment,
    up_first_moment,
    up_second_moment,
    rate,
    step,
    cotangent,
):
    width = tokens.shape[1]
    shard = query_weight.shape[0]
    small = jnp.concatenate(
        [
            fixed_projection_bias,
            layer_norm_gain,
            layer_norm_shift,
        ],
        axis=0,
    )
    inner_bias = feedforward_inner_bias[None]
    fast = shard % 8 == 0 and shard * layout.n == width and layout.n == 32
    if fast:
        tail = jnp.concatenate(
            [
                jnp.pad(small, ((0, 0), (0, LANES - shard))),
                jnp.pad(inner_bias, ((0, shard - 9), (0, LANES - inner_bias.shape[1]))),
            ],
            axis=0,
        )
        block_a = jnp.concatenate([query_weight, key_weight, value_weight, tail], axis=1)
        extra = outer_weight[OUTER_ROWS:]
        third = extra[shard:].reshape(8, 3, width // 3)
        third = jnp.swapaxes(third, 0, 1).reshape(shard, width // 3)
        block_b = jnp.concatenate([output_weight, inner_weight, extra[:shard], third], axis=1)
        zf, zl = layout.z_first, layout.z_last
        ids = block_ids(layout, zf)
        ids_d = block_ids(layout, zl)
        a, b, d = block_a[None], block_b[None], outer_weight[None, :OUTER_ROWS]
        a1 = stage(a, layout, zf, 0)
        d1 = stage(d, layout, zl, 0)
        a1, b, d = together(a1, b, d)
        a = join(a, a1)
        a2 = stage(a, layout, zf, 1)
        d = join(d, after(d1, a1))
        d2 = stage(d, layout, zl, 1)
        a2, d2, b = together(a2, d2, b)
        a, d = join(a, a2), join(d, d2)
        a3 = stage(a, layout, zf, 2)
        b1 = stage(b, layout, zf, 0)
        a3, b1 = together(a3, b1)
        a, b = join(a, a3), join(b, b1)
        a4 = stage(a, layout, zf, 3)
        b2 = stage(b, layout, zf, 1)
        a5 = swap_cores(a, layout)
        a4, b2, a5, d = together(a4, b2, a5, d)
        d3 = stage(d, layout, zl, 2)
        a6 = swap_cores(a4, layout)
        b = join(b, b2)
        b3 = stage(b, layout, zf, 2)
        parts_a = (a, a4, a5, a6)
    else:
        count = 32
        rows = width // count
        whole = lambda w: lax.all_gather(w, AXES, axis=0, tiled=True)
        small_full = lax.all_gather(small, AXES, axis=1, tiled=True)
        bias_full = lax.all_gather(inner_bias, AXES, axis=1, tiled=True)
        tail = jnp.concatenate(
            [
                jnp.pad(small_full.reshape(8, count, rows), ((0, 0), (0, 0), (0, LANES - rows))),
                jnp.pad(
                    bias_full.reshape(1, count, -1),
                    ((0, rows - 9), (0, 0), (0, LANES - bias_full.shape[1] // count)),
                ),
            ],
            axis=0,
        )
        tail = jnp.swapaxes(tail, 0, 1).reshape(width, LANES)
        parts_a = as_blocks(
            jnp.concatenate([whole(query_weight), whole(key_weight), whole(value_weight), tail], axis=1), count
        )
        outer = whole(outer_weight).reshape(count, -1, width)
        extra = outer[:, OUTER_ROWS:]
        third = extra[:, rows:].reshape(count, 8, 3, width // 3)
        third = jnp.swapaxes(third, 1, 2).reshape(width, width // 3)
        parts_b = as_blocks(
            jnp.concatenate(
                [whole(output_weight), whole(inner_weight), extra[:, :rows].reshape(width, width), third], axis=1
            ),
            count,
        )
        parts_d = as_blocks(outer[:, :OUTER_ROWS].reshape(-1, width), count)
        ids = ids_d = jnp.arange(count, dtype=jnp.int32)

    turn = lambda v: jnp.swapaxes(v, 1, 2)
    down = turn(adapter_down_factors)
    up = adapter_up_factors
    qkv, weight, red, small_rows, inner_rows = project(ids, tokens, down, up, parts_a)
    if fast:
        b3, d3, qkv = together(b3, d3, qkv)
        b = join(b, b3)
        b4 = stage(b, layout, zf, 3)
        d = join(d, d3)
        d4 = stage(d, layout, zl, 3)
    step_counter = step[0].astype(f32)
    scalars = jnp.stack([1.0 - beta_one**step_counter, 1.0 - beta_two**step_counter, rate[0]])
    core = jnp.reshape((lax.axis_index(AXES) & layout.core) != 0, (1,)).astype(jnp.int32)
    half = attend(0, document_numbers, qkv)
    ids_d, scalars, core, *half = together(ids_d, scalars, core, *half)
    if fast:
        b5 = swap_cores(after(b, *half), layout)
        d5 = swap_cores(after(d, *half), layout)
    context, attention, inverse = attend(1, document_numbers, qkv, half)
    if fast:
        b4, d4, context = together(b4, d4, context)
        b6 = swap_cores(b4, layout)
        d6 = swap_cores(d4, layout)
        parts_b = (b, b4, b5, b6)
        parts_d = (d, d4, d5, d6)
    activations, grad_mid, grad_context, sums = row_local(
        ids, ids_d, tokens, cotangent, context, small_rows, inner_rows, parts_b, parts_d
    )
    input_grad, keep, send = attend_back(
        core, tokens, qkv, context, grad_context, inverse, attention, up, red, sums, grad_mid, down, weight
    )
    total = keep + swap_cores(send, layout)
    total = exchange(total, layout, layout.x_bits + layout.y_bits)
    total = exchange(total, layout, layout.z_bits)
    other = swap_cores(total, layout)
    gd, gu, gain_grad, shift_grad, pd, pu, dm, dv, um, uv = adamw(
        layout.n,
        scalars,
        core,
        total,
        other,
        down,
        up,
        turn(down_first_moment),
        turn(down_second_moment),
        up_first_moment,
        up_second_moment,
    )
    return (
        activations,
        input_grad,
        turn(gd),
        gu,
        gain_grad,
        shift_grad,
        turn(pd),
        pu,
        turn(dm),
        turn(dv),
        um,
        uv,
    )


def solution(mesh):
    rows = P(AXES, None)
    columns = P(None, AXES)
    in_specs = (
        (rows,) * 8
        + (columns, P(AXES), columns, columns)
        + (P(),) * 8
        + (rows,)
    )
    out_specs = (rows, rows) + (P(),) * 10
    return jax.shard_map(
        functools.partial(per_device, Layout(mesh)),
        mesh=mesh,
        in_specs=in_specs,
        out_specs=out_specs,
        check_vma=False,
    )
```

```python
import functools
import math

import jax
import jax.numpy as jnp
import numpy as np
from jax import lax
from jax.experimental import pallas as pl
from jax.experimental.pallas import tpu as pltpu
from jax.sharding import PartitionSpec as P

HEAD = 64
OUTER_ROWS = 64
AXES = ("dp", "fsdp")

beta_one = 0.9
beta_two = 0.999
adam_epsilon = 1e-08
down_decay_factor = 0.05
up_decay_factor = 0.01
norm_epsilon = 1e-05
masked_score = -1e30
root_half = math.sqrt(0.5)
root_circle = 1.0 / math.sqrt(2.0 * math.pi)
log_e = math.log2(math.e)
LANES = 128
MIB = 1 << 20
VMEM_LIMIT = 60 * MIB

f32 = jnp.float32
bf16 = jnp.bfloat16


def nn(a, b):
    return lax.dot_general(a, b, (((1,), (0,)), ((), ())), preferred_element_type=f32)


def nt(a, b):
    return lax.dot_general(a, b, (((1,), (1,)), ((), ())), preferred_element_type=f32)


class Layout:
    def __init__(self, mesh):
        n_dp, n_fsdp = mesh.shape["dp"], mesh.shape["fsdp"]
        self.n = n_dp * n_fsdp
        self.core = n_fsdp
        n_x = n_dp // 2
        n_y = n_x
        y_bits = [1 << t for t in range(int(math.log2(n_y)))]
        z_bits = [n_y << t for t in range(int(math.log2(n_fsdp // n_y)))]
        x_bits = [(2 * n_fsdp) << t for t in range(int(math.log2(n_x)))]
        self.z_first = (z_bits + x_bits + y_bits, z_bits[::-1] + y_bits + x_bits)
        self.z_last = (x_bits + y_bits + z_bits, y_bits + x_bits + z_bits[::-1])
        self.x_bits, self.y_bits, self.z_bits = x_bits, y_bits, z_bits

    def stage_pairs(self, orders, t):
        return [(i, i ^ orders[1 if i & self.core else 0][t]) for i in range(self.n)]

    def pairs(self, bits):
        return [(i, i ^ bits) for i in range(self.n)]

    def core_pairs(self):
        return [(i, i ^ self.core) for i in range(self.n)]

    def block_masks(self, order):
        masks = [0]
        for bit in order:
            masks = masks + [m ^ bit for m in masks]
        return masks


def after(value, *others):
    return lax.optimization_barrier((value,) + others)[0]


def together(*values):
    return lax.optimization_barrier(values)


def stage(held, layout, orders, t):
    return lax.ppermute(held, AXES, layout.stage_pairs(orders, t))


def swap_cores(value, layout):
    return lax.ppermute(value, AXES, layout.core_pairs())


def join(held, came):
    return jnp.concatenate([held, came], axis=0)


def block_ids(layout, orders):
    me = lax.axis_index(AXES).astype(jnp.int32)
    one, two = (np.array(layout.block_masks(o), np.int32) for o in orders)
    second = (me & layout.core) != 0
    own = me ^ jnp.where(second, two, one)
    other = me ^ layout.core ^ jnp.where(second, one, two)
    return jnp.concatenate([own, other])


def exchange(total, layout, kinds):
    combos = [0]
    for bit in kinds:
        combos = combos + [c ^ bit for c in combos]
    parts = [total] + [lax.ppermute(total, AXES, layout.pairs(c)) for c in combos[1:]]
    while len(parts) > 1:
        parts = [one + two for one, two in zip(parts[::2], parts[1::2])]
    return parts[0]


def as_blocks(full, count):
    return tuple(
        part for part in full.reshape((4, count // 4) + (full.shape[0] // count,) + full.shape[1:])
    )


def fetch_blocks(ids_ref, parts, stage, sems):
    each = parts[0].shape[0]
    for a, part in enumerate(parts):
        for j in range(each):
            k = a * each + j
            at = ids_ref[k]
            pltpu.make_async_copy(part.at[j], stage.at[at], sems.at[at]).start()


def wait_block(parts, stage, sems, i):
    pltpu.make_async_copy(parts[0].at[0], stage.at[i], sems.at[i]).wait()


def merge_pairs(parts, stage, sems, target, width, extra=None):
    shards, rows = stage.shape[0], stage.shape[1]
    for i in range(0, shards, 2):
        wait_block(parts, stage, sems, i)
        wait_block(parts, stage, sems, i + 1)
        for c in range(0, width, 768):
            low = stage[i, :, c : c + 768].astype(f32)
            high = stage[i + 1, :, c : c + 768].astype(f32)
            target[rows * i : rows * (i + 2), c : c + 768] = jnp.concatenate(
                [low, high], axis=0
            ).astype(bf16)


def spread(piece, width, step, count):
    lane = lax.broadcasted_iota(jnp.int32, (LANES, width), 1).astype(f32)
    slot = lax.broadcasted_iota(jnp.int32, (LANES, width), 0).astype(f32)
    within = lane - step * jnp.floor((lane + 0.5) * (1.0 / step))
    place = (within == slot).astype(bf16)
    wide = nn(piece.astype(bf16), place)
    at = lax.broadcasted_iota(jnp.int32, (8, width), 1)
    total = jnp.zeros((8, width), f32)
    for i in range(count):
        mine = (at >= step * i) & (at < step * (i + 1))
        total = total + jnp.where(mine, wide[8 * i : 8 * (i + 1)], 0.0)
    return total


def project_kernel(ids_ref, x_ref, down_ref, up_ref, p0, p1, p2, p3, qkv_ref, weight_hbm, red_ref,
                   small_ref, inner_bias_ref, stage, weight_ref, sems, sem_w):
    parts = (p0, p1, p2, p3)
    width = x_ref.shape[1]
    rank = down_ref.shape[1]

    @pl.when(pl.program_id(0) == 0)
    def _():
        fetch_blocks(ids_ref, parts, stage, sems)
        merge_pairs(parts, stage, sems, weight_ref, 3 * width)
        pltpu.make_async_copy(weight_ref, weight_hbm, sem_w).start()
        shards, rows = stage.shape[0], stage.shape[1]
        tail = stage[:, :, 3 * width :].astype(f32)
        small_ref[...] = spread(tail[:, 0:8].reshape(8 * shards, LANES), width, rows, shards)
        ff = inner_bias_ref.shape[1]
        inner_bias_ref[...] = spread(
            tail[:, 8:16].reshape(8 * shards, LANES), ff, ff // shards, shards
        )

    x = x_ref[...]
    down = down_ref[...].reshape(2 * rank, width).astype(bf16)
    up = (2.0 * up_ref[...].astype(bf16).astype(f32)).astype(bf16)
    zero = jnp.zeros((rank, width), bf16)
    wide = nt(x, down)
    reduced = wide.astype(bf16)
    red_ref[...] = wide.T.astype(bf16)
    up_query = jnp.concatenate([up[0], zero], axis=0)
    up_value = jnp.concatenate([zero, up[1]], axis=0)
    chunk = 256
    for c in range(0, 3 * width, chunk):
        y = nn(x, weight_ref[:, c : c + chunk])
        o = c % width
        if c < width:
            y = y + small_ref[0:1, o : o + chunk] + nn(reduced, up_query[:, o : o + chunk])
        elif c >= 2 * width:
            y = y + small_ref[1:2, o : o + chunk] + nn(reduced, up_value[:, o : o + chunk])
        qkv_ref[:, c : c + chunk] = y.astype(bf16)

    @pl.when(pl.program_id(0) == pl.num_programs(0) - 1)
    def _():
        pltpu.make_async_copy(weight_ref, weight_hbm, sem_w).wait()


def project(ids, tokens, down, up, parts):
    rows, width = tokens.shape
    shards = 4 * parts[0].shape[0]
    shard_rows = parts[0].shape[1]
    ff = 4 * width
    tile = 256
    whole = lambda *shape: pl.BlockSpec(shape, lambda i: (0,) * len(shape))
    return pl.pallas_call(
        project_kernel,
        grid=(rows // tile,),
        in_specs=[
            pl.BlockSpec(memory_space=pltpu.SMEM),
            pl.BlockSpec((tile, width), lambda i: (i, 0)),
            whole(*down.shape),
            whole(*up.shape),
        ]
        + [pl.BlockSpec(memory_space=pl.ANY)] * 4,
        out_specs=[
            pl.BlockSpec((tile, 3 * width), lambda i: (i, 0)),
            pl.BlockSpec(memory_space=pl.ANY),
            pl.BlockSpec((2 * down.shape[1], tile), lambda i: (0, i)),
            whole(8, width),
            whole(8, ff),
        ],
        out_shape=[
            jax.ShapeDtypeStruct((rows, 3 * width), bf16),
            jax.ShapeDtypeStruct((width, 3 * width), bf16),
            jax.ShapeDtypeStruct((2 * down.shape[1], rows), bf16),
            jax.ShapeDtypeStruct((8, width), f32),
            jax.ShapeDtypeStruct((8, ff), f32),
        ],
        scratch_shapes=[
            pltpu.VMEM((shards, shard_rows, 3 * width + LANES), bf16),
            pltpu.VMEM((width, 3 * width), bf16),
            pltpu.SemaphoreType.DMA((shards,)),
            pltpu.SemaphoreType.DMA(()),
        ],
        compiler_params=pltpu.CompilerParams(vmem_limit_bytes=58 * MIB),
        cost_estimate=pl.CostEstimate(
            flops=2 * rows * width * width * 3, bytes_accessed=14 * MIB, transcendentals=0
        ),
    )(ids, tokens, down, up, *parts)


def interleave(programs, lag):
    tick, alive = 0, list(enumerate(programs))
    while alive:
        for item in list(alive):
            if tick >= item[0] * lag:
                try:
                    next(item[1])
                except StopIteration:
                    alive.remove(item)
        tick += 1


def attend_kernel(pack, seg_ref, q_ref, k_ref, v_ref, *rest):
    ctx_ref, w_ref, inverse_ref, hot, cold = rest[-5:]
    rows = seg_ref.shape[1]
    lane = lax.broadcasted_iota(jnp.int32, (1, LANES), 1)

    @pl.when(pl.program_id(0) == 0)
    def _():
        row = jnp.broadcast_to(seg_ref[pack : pack + 1, :].astype(f32), (8, rows))
        column = row.T[:, 0:1]
        slot = jnp.where(lane < HEAD, lane, lane - HEAD).astype(f32)
        hot[...] = jnp.where(column == slot, 1.0, 0.0).astype(bf16)
        cold[...] = jnp.where(column == slot, 0.0, masked_score).astype(bf16)

    sums = {}

    def program(s, h):
        cols = slice(s * LANES, (s + 1) * LANES)
        mine = (lane < HEAD) if h == 0 else (lane >= HEAD)
        q = jnp.where(mine, q_ref[:, cols] * jnp.asarray(HEAD**-0.5, bf16), hot[...])
        scores = nt(q, jnp.where(mine, k_ref[:, cols], cold[...]))
        yield
        peak = jnp.max(scores, axis=-1, keepdims=True)
        exponent = jnp.exp2((scores - peak) * log_e).astype(bf16)
        w_ref[2 * s + h] = exponent
        yield
        v = v_ref[:, cols]
        sums[h] = nn(exponent, jnp.where(mine, v, jnp.ones_like(v)))
        if h == 1:
            top = jnp.where(lane < HEAD, sums[0], sums[1])
            total = pltpu.roll(jnp.where(lane < HEAD, sums[1], sums[0]), HEAD, axis=1)
            inverse = 1.0 / total
            inverse_ref[:, cols] = inverse
            ctx_ref[:, cols] = (top * inverse).astype(bf16)

    interleave([program(s, h) for s in range(q_ref.shape[1] // LANES) for h in range(2)], 1)


HEADS_A_STEP = 4


def attend(pack, segments, qkv, before=()):
    packs, length = segments.shape
    width = qkv.shape[1] // 3
    step = HEADS_A_STEP * HEAD
    steps = width // step
    at = lambda which: pl.BlockSpec((length, step), lambda s: (pack, which * steps + s))
    return pl.pallas_call(
        functools.partial(attend_kernel, pack),
        grid=(steps,),
        in_specs=[pl.BlockSpec((packs, length), lambda s: (0, 0)), at(0), at(1), at(2)]
        + [pl.BlockSpec(memory_space=pl.ANY)] * len(before),
        out_specs=[
            pl.BlockSpec((length, step), lambda s: (pack, s)),
            pl.BlockSpec((HEADS_A_STEP, length, length), lambda s: (pack * steps + s, 0, 0)),
            pl.BlockSpec((length, step), lambda s: (pack, s)),
        ],
        out_shape=[
            jax.ShapeDtypeStruct((packs * length, width), bf16),
            jax.ShapeDtypeStruct((packs * width // HEAD, length, length), bf16),
            jax.ShapeDtypeStruct((packs * length, width), f32),
        ],
        input_output_aliases={4 + i: i for i in range(len(before))},
        scratch_shapes=[pltpu.VMEM((length, LANES), bf16), pltpu.VMEM((length, LANES), bf16)],
        compiler_params=pltpu.CompilerParams(vmem_limit_bytes=VMEM_LIMIT),
        cost_estimate=pl.CostEstimate(
            flops=16 * length * length * width, bytes_accessed=10 * MIB, transcendentals=0
        ),
    )(segments, qkv, qkv, qkv, *before)


def stats(value):
    centred = value - jnp.mean(value, axis=-1, keepdims=True)
    inverse = lax.rsqrt(jnp.mean(centred * centred, axis=-1, keepdims=True) + norm_epsilon)
    return centred * inverse, inverse


def norm_back(grad, normed, inverse, gain):
    scaled = grad * gain
    return inverse * (
        scaled
        - jnp.mean(scaled, axis=-1, keepdims=True)
        - normed * jnp.mean(scaled * normed, axis=-1, keepdims=True)
    )


def gelu_parts(z):
    cumulative = 0.5 + 0.5 * lax.erf(z * root_half)
    density = jnp.exp2(z * z * (-0.5 * log_e)) * root_circle
    return z * cumulative, cumulative + z * density


ROW_TILE = 256
ROW_TILES = 2
ROW_LAG = 8
PIECE = 64
SIDE = 256
FF_CHUNK = 1024


def fold(value):
    rows, width = value.shape
    return jnp.sum(value.reshape(rows // 8, 8, width), axis=0)


def rows_kernel(ids_ref, ids_d_ref, x_ref, cot_ref, ctx_ref, small_ref, inner_bias_ref,
                b0, b1, b2, b3, d0, d1, d2, d3,
                act_ref, mid_ref, dctx_ref, sums_ref,
                stage, wo, wi, wf, active, slope, normed, inverse, first, first_b, total, grad_res, grad_b, sem_b, sem_d):
    parts_b, parts_d = (b0, b1, b2, b3), (d0, d1, d2, d3)
    width = x_ref.shape[1]
    taken = d0.shape[1]
    ff = wi.shape[1]
    shard = ff // stage.shape[0]

    @pl.when(pl.program_id(0) == 0)
    def _():
        fetch_blocks(ids_ref, parts_b, stage, sem_b)
        for a, part in enumerate(parts_d):
            for j in range(part.shape[0]):
                at = ids_d_ref[a * part.shape[0] + j]
                place = wf.at[pl.ds(pl.multiple_of(at * shard, shard), taken)]
                pltpu.make_async_copy(part.at[j], place, sem_d.at[at]).start()
        shards, rows = stage.shape[0], stage.shape[1]
        for i in range(0, shards, 2):
            wait_block(parts_b, stage, sem_b, i)
            wait_block(parts_b, stage, sem_b, i + 1)
            for c in range(0, width + ff, width):
                both = jnp.concatenate(
                    [
                        stage[i, :, c : c + width].astype(f32),
                        stage[i + 1, :, c : c + width].astype(f32),
                    ],
                    axis=0,
                ).astype(bf16)
                where = slice(rows * i, rows * (i + 2))
                if c == 0:
                    wo[where] = both
                else:
                    wi[where, c - width : c] = both
            for k in (i, i + 1):
                more = stage[k, :, width + ff :].astype(f32)
                third = more[:, width:]
                eight = [third[8 * n : 8 * (n + 1)] for n in range(3)]
                wf[k * shard + taken : (k + 1) * shard] = jnp.concatenate(
                    [more[:, :width], jnp.concatenate(eight, axis=1)], axis=0
                ).astype(bf16)
        for i in range(shards):
            pltpu.make_async_copy(d0.at[0], wf.at[pl.ds(i * shard, taken)], sem_d.at[i]).wait()
        sums_ref[...] = jnp.zeros_like(sums_ref)

    bias_out, bias_ff = small_ref[2:3], small_ref[3:4]
    gain_one, gain_two = small_ref[4:5], small_ref[5:6]
    shift_one, shift_two = small_ref[6:7], small_ref[7:8]
    sums = [jnp.zeros((8, width), f32) for _ in range(4)]

    def program(t):
        every = slice(t * ROW_TILE, (t + 1) * ROW_TILE)
        pieces = [
            (slice(t * ROW_TILE + p, t * ROW_TILE + p + PIECE), slice(p, p + PIECE))
            for p in range(0, ROW_TILE, PIECE)
        ]
        sides = [slice(c, c + SIDE) for c in range(0, width, SIDE)]
        chunks = [slice(c, c + FF_CHUNK) for c in range(0, ff, FF_CHUNK)]
        for c in sides:
            total[t, :, c] = x_ref[every, c].astype(f32) + (nn(ctx_ref[every], wo[:, c]) + bias_out[:, c])
            yield
        for far, near in pieces:
            n, i = stats(total[t, near])
            normed[t, near] = n
            inverse[t, near] = i
            f = n * gain_one + shift_one
            first[t, near] = f
            first_b[t, near] = f.astype(bf16)
            yield
        for c in chunks:
            value, grad = gelu_parts(nn(first_b[t], wi[:, c]) + inner_bias_ref[0:1, c])
            active[t, :, c] = value.astype(bf16)
            slope[t, :, c] = grad.astype(bf16)
            yield
        for c in sides:
            total[t, :, c] = first[t, :, c] + (nn(active[t], wf[:, c]) + bias_ff[:, c])
            yield
        for far, near in pieces:
            n, i = stats(total[t, near])
            act_ref[far] = (n * gain_two + shift_two).astype(bf16)
            g = cot_ref[far].astype(f32)
            sums[1] = sums[1] + fold(g * n)
            sums[3] = sums[3] + fold(g)
            res = norm_back(g, n, i, gain_two)
            grad_res[t, near] = res
            grad_b[t, near] = res.astype(bf16)
            yield
        for c in chunks:
            grad_active = nt(grad_b[t], wf[c])
            active[t, :, c] = (grad_active * slope[t, :, c].astype(f32)).astype(bf16)
            yield
        for c in sides:
            total[t, :, c] = grad_res[t, :, c] + nt(active[t], wi[c])
            yield
        for far, near in pieces:
            g = total[t, near]
            n = normed[t, near]
            sums[0] = sums[0] + fold(g * n)
            sums[2] = sums[2] + fold(g)
            mid = norm_back(g, n, inverse[t, near], gain_one)
            mid_ref[far] = mid
            grad_b[t, near] = mid.astype(bf16)
            yield
        for c in sides:
            dctx_ref[every, c] = nt(grad_b[t], wo[c]).astype(bf16)
            yield

    interleave([program(t) for t in range(x_ref.shape[0] // ROW_TILE)], ROW_LAG)
    for i, value in enumerate(sums):
        sums_ref[i : i + 1] += jnp.sum(value, axis=0, keepdims=True)


def row_local(ids, ids_d, tokens, cotangent, context, small, inner_bias, parts_b, parts_d):
    rows, width = tokens.shape
    ff = inner_bias.shape[1]
    shards = 4 * parts_b[0].shape[0]
    tile = ROW_TILE * ROW_TILES
    two = lambda w, kind: pltpu.VMEM((ROW_TILES, ROW_TILE, w), kind)
    whole = lambda *shape: pl.BlockSpec(shape, lambda i: (0,) * len(shape))
    tiled = pl.BlockSpec((tile, width), lambda i: (i, 0))
    return pl.pallas_call(
        rows_kernel,
        grid=(rows // tile,),
        in_specs=[
            pl.BlockSpec(memory_space=pltpu.SMEM),
            pl.BlockSpec(memory_space=pltpu.SMEM),
            tiled,
            tiled,
            tiled,
            whole(8, width),
            whole(8, ff),
        ]
        + [pl.BlockSpec(memory_space=pl.ANY)] * 8,
        out_specs=[tiled, tiled, tiled, whole(8, width)],
        out_shape=[
            jax.ShapeDtypeStruct((rows, width), bf16),
            jax.ShapeDtypeStruct((rows, width), f32),
            jax.ShapeDtypeStruct((rows, width), bf16),
            jax.ShapeDtypeStruct((8, width), f32),
        ],
        scratch_shapes=[
            pltpu.VMEM((shards,) + parts_b[0].shape[1:], bf16),
            pltpu.VMEM((width, width), bf16),
            pltpu.VMEM((width, ff), bf16),
            pltpu.VMEM((ff, width), bf16),
            two(ff, bf16),
            two(ff, bf16),
            two(width, f32),
            two(1, f32),
            two(width, f32),
            two(width, bf16),
            two(width, f32),
            two(width, f32),
            two(width, bf16),
            pltpu.SemaphoreType.DMA((shards,)),
            pltpu.SemaphoreType.DMA((shards,)),
        ],
        compiler_params=pltpu.CompilerParams(vmem_limit_bytes=VMEM_LIMIT),
        cost_estimate=pl.CostEstimate(
            flops=2 * rows * width * (4 * ff + 2 * width), bytes_accessed=20 * MIB, transcendentals=0
        ),
    )(ids, ids_d, tokens, cotangent, context, small, inner_bias, *parts_b, *parts_d)


BACK_LAG = 1


def attend_back_kernel(core_ref, x_ref, q_ref, k_ref, v_ref, ctx_ref, dctx_ref, inverse_ref, w_ref, up_ref, red_ref,
                       sums_ref, mid_ref, down_ref, wq_ref, wk_ref, wv_ref, out_ref, keep_ref, send_ref,
                       dq_ref, dk_ref, dv_ref, dred, grads):
    scale = HEAD**-0.5
    pack, step = pl.program_id(0), pl.program_id(1)
    rank = red_ref.shape[0] // 2

    @pl.when((pack == 0) & (step == 0))
    def _():
        grads[...] = jnp.zeros_like(grads)
        keep_ref[...] = jnp.zeros_like(keep_ref)
        send_ref[...] = jnp.zeros_like(send_ref)

    @pl.when(step == 0)
    def _():
        dred[...] = jnp.zeros_like(dred)

    lane = lax.broadcasted_iota(jnp.int32, (1, LANES), 1)
    held = {}

    def program(s, h):
        cols = slice(s * LANES, (s + 1) * LANES)
        mine = (lane < HEAD) if h == 0 else (lane >= HEAD)
        rows = slice(h * HEAD, (h + 1) * HEAD)
        q = q_ref[:, cols]
        zero = jnp.zeros_like(q)
        if h == 0:
            dctx = (dctx_ref[:, cols].astype(f32) * inverse_ref[:, cols]).astype(bf16)
            flat = dctx.astype(f32) * ctx_ref[:, cols].astype(f32)
            held[s] = (dctx, flat, q.T, dctx.T, [], [], [])
        dctx, flat, q_t, dctx_t, dq, dk_t, dv_t = held[s]
        grad_weights = nt(jnp.where(mine, dctx, zero), v_ref[:, cols])
        yield
        delta = jnp.sum(jnp.where(mine, flat, 0.0), axis=-1, keepdims=True)
        weights = w_ref[2 * s + h]
        grad_scores = (weights.astype(f32) * (grad_weights - delta)).astype(bf16)
        yield
        dv_t.append(nn(dctx_t[rows], weights))
        dq.append(nn(grad_scores, jnp.where(mine, k_ref[:, cols], zero)))
        dk_t.append(nn(q_t[rows], grad_scores))
        if h == 1:
            dq_ref[:, cols] = ((dq[0] + dq[1]) * scale).astype(bf16)
            dk_ref[:, cols] = (jnp.concatenate(dk_t, axis=0) * scale).T.astype(bf16)
            dv_ref[:, cols] = jnp.concatenate(dv_t, axis=0).T.astype(bf16)
            del held[s]

    interleave([program(s, h) for s in range(q_ref.shape[1] // LANES) for h in range(2)], BACK_LAG)
    red = red_ref[...]
    up = (2.0 * up_ref[...].astype(bf16).astype(f32)).astype(bf16)
    none = jnp.zeros_like(up[0])
    dq, dv = dq_ref[...], dv_ref[...]
    dred[...] += nt(jnp.concatenate([up[0], none], axis=0), dq) + nt(jnp.concatenate([none, up[1]], axis=0), dv)
    grads[step, 0:rank] += 2.0 * nn(red, dq)[0:rank]
    grads[step, rank : 2 * rank] += 2.0 * nn(red, dv)[rank : 2 * rank]

    grad = nt(dq, wq_ref[...]) + nt(dk_ref[...], wk_ref[...]) + nt(dv, wv_ref[...])

    @pl.when(step == 0)
    def _():
        out_ref[...] = mid_ref[...] + grad

    @pl.when(step > 0)
    def _():
        out_ref[...] += grad

    @pl.when(step == pl.num_programs(1) - 1)
    def _():
        rounded = dred[...].astype(bf16)
        joined = down_ref[...].reshape(2 * rank, down_ref.shape[2]).astype(bf16)
        out_ref[...] += lax.dot_general(rounded, joined, (((0,), (0,)), ((), ())), preferred_element_type=f32)
        down = nn(rounded, x_ref[...])
        raised = jnp.concatenate([grads[i] for i in range(grads.shape[0])], axis=1)
        half = down.shape[1] // 2
        low = (core_ref[0] == 0).astype(f32)
        for out, left in ((keep_ref, low), (send_ref, 1.0 - low)):
            pick = lambda a: jnp.where(left > 0.5, a[:, :half], a[:, half:])
            out[0 : 2 * rank] += pick(down)
            out[2 * rank : 4 * rank] = pick(raised)
            out[4 * rank : 5 * rank] = pick(sums_ref[...])


def attend_back(core, tokens, qkv, context, grad_context, inverse, weights, up, red, sums, mid, down, weight):
    rows, width = context.shape
    length = weights.shape[1]
    rank = up.shape[1]
    step = HEADS_A_STEP * HEAD
    steps = width // step
    at = lambda which: pl.BlockSpec((length, step), lambda p, s: (p, which * steps + s))
    from_weight = lambda which: pl.BlockSpec((width, step), lambda p, s: (0, which * steps + s))
    own = pl.BlockSpec((length, step), lambda p, s: (p, s))
    pack = pl.BlockSpec((length, width), lambda p, s: (p, 0))
    whole = lambda *shape: pl.BlockSpec(shape, lambda p, s: (0,) * len(shape))
    half = whole(5 * rank, width // 2)
    return pl.pallas_call(
        attend_back_kernel,
        grid=(rows // length, steps),
        in_specs=[
            pl.BlockSpec(memory_space=pltpu.SMEM),
            pack,
            at(0),
            at(1),
            at(2),
            own,
            own,
            own,
            pl.BlockSpec((HEADS_A_STEP, length, length), lambda p, s: (p * steps + s, 0, 0)),
            pl.BlockSpec((2, rank, step), lambda p, s: (0, 0, s)),
            pl.BlockSpec((2 * rank, length), lambda p, s: (0, p)),
            whole(*sums.shape),
            pack,
            whole(*down.shape),
            from_weight(0),
            from_weight(1),
            from_weight(2),
        ],
        out_specs=[pack, half, half],
        out_shape=[
            jax.ShapeDtypeStruct((rows, width), f32),
            jax.ShapeDtypeStruct((5 * rank, width // 2), f32),
            jax.ShapeDtypeStruct((5 * rank, width // 2), f32),
        ],
        scratch_shapes=[pltpu.VMEM((length, step), bf16)] * 3
        + [pltpu.VMEM((2 * rank, length), f32), pltpu.VMEM((steps, 2 * rank, step), f32)],
        compiler_params=pltpu.CompilerParams(vmem_limit_bytes=VMEM_LIMIT),
        cost_estimate=pl.CostEstimate(
            flops=32 * rows * length * width, bytes_accessed=28 * MIB, transcendentals=0
        ),
    )(core, tokens, qkv, qkv, qkv, context, grad_context, inverse, weights, up, red, sums, mid, down, weight,
      weight, weight)


def adamw_kernel(count, scal_ref, core_ref, mine_ref, other_ref, down_ref, up_ref, dm_ref, dv_ref, um_ref, uv_ref,
                 gd_ref, gu_ref, gain_ref, shift_ref, pd_ref, pu_ref, dm2_ref, dv2_ref, um2_ref, uv2_ref):
    rank = up_ref.shape[1]
    width = up_ref.shape[2]
    part = 1.0 / count
    first_scale, second_scale, rate = scal_ref[0], scal_ref[1], scal_ref[2]

    def update(param, grad, first, second, learn, decay):
        first_new = beta_one * first + (1.0 - beta_one) * grad
        second_new = beta_two * second + (1.0 - beta_two) * grad * grad
        first_hat = first_new / first_scale
        second_hat = second_new / second_scale
        new = param - learn * (first_hat / (jnp.sqrt(second_hat) + adam_epsilon) + decay * param)
        return new, first_new, second_new

    mine, other = mine_ref[...] * part, other_ref[...] * part
    low = core_ref[0] == 0
    total = jnp.concatenate([jnp.where(low, mine, other), jnp.where(low, other, mine)], axis=1)
    grad_down = total[0 : 2 * rank].reshape(2, rank, width)
    grad_up = total[2 * rank : 4 * rank].reshape(2, rank, width)
    gd_ref[...] = grad_down
    gu_ref[...] = grad_up
    gain_ref[...] = total[4 * rank : 4 * rank + 2]
    shift_ref[...] = total[4 * rank + 2 : 4 * rank + 4]
    pd_ref[...], dm2_ref[...], dv2_ref[...] = update(
        down_ref[...], grad_down, dm_ref[...], dv_ref[...], rate, down_decay_factor
    )
    pu_ref[...], um2_ref[...], uv2_ref[...] = update(
        up_ref[...], grad_up, um_ref[...], uv_ref[...], 16.0 * rate, up_decay_factor
    )


def adamw(count, scalars, core, mine, other, down, up, dm, dv, um, uv):
    width = up.shape[2]
    like = jax.ShapeDtypeStruct(up.shape, f32)
    pair = jax.ShapeDtypeStruct((2, width), f32)
    vmem = pl.BlockSpec(memory_space=pltpu.VMEM)
    smem = pl.BlockSpec(memory_space=pltpu.SMEM)
    return pl.pallas_call(
        functools.partial(adamw_kernel, count),
        in_specs=[smem, smem] + [vmem] * 8,
        out_shape=[like, like, pair, pair] + [like] * 6,
        compiler_params=pltpu.CompilerParams(vmem_limit_bytes=16 * MIB),
    )(scalars, core, mine, other, down, up, dm, dv, um, uv)


def per_device(
    layout,
    tokens,
    document_numbers,
    query_weight,
    key_weight,
    value_weight,
    output_weight,
    inner_weight,
    outer_weight,
    fixed_projection_bias,
    feedforward_inner_bias,
    layer_norm_gain,
    layer_norm_shift,
    adapter_down_factors,
    adapter_up_factors,
    down_first_moment,
    down_second_moment,
    up_first_moment,
    up_second_moment,
    rate,
    step,
    cotangent,
):
    width = tokens.shape[1]
    shard = query_weight.shape[0]
    small = jnp.concatenate(
        [
            fixed_projection_bias,
            layer_norm_gain,
            layer_norm_shift,
        ],
        axis=0,
    )
    inner_bias = feedforward_inner_bias[None]
    fast = shard % 8 == 0 and shard * layout.n == width and layout.n == 32
    if fast:
        tail = jnp.concatenate(
            [
                jnp.pad(small, ((0, 0), (0, LANES - shard))),
                jnp.pad(inner_bias, ((0, shard - 9), (0, LANES - inner_bias.shape[1]))),
            ],
            axis=0,
        )
        block_a = jnp.concatenate([query_weight, key_weight, value_weight, tail], axis=1)
        extra = outer_weight[OUTER_ROWS:]
        third = extra[shard:].reshape(8, 3, width // 3)
        third = jnp.swapaxes(third, 0, 1).reshape(shard, width // 3)
        block_b = jnp.concatenate([output_weight, inner_weight, extra[:shard], third], axis=1)
        zf, zl = layout.z_first, layout.z_last
        ids = block_ids(layout, zf)
        ids_d = block_ids(layout, zl)
        a, b, d = block_a[None], block_b[None], outer_weight[None, :OUTER_ROWS]
        a1 = stage(a, layout, zf, 0)
        d1 = stage(d, layout, zl, 0)
        a1, b, d = together(a1, b, d)
        a = join(a, a1)
        a2 = stage(a, layout, zf, 1)
        d = join(d, after(d1, a1))
        d2 = stage(d, layout, zl, 1)
        a2, d2, b = together(a2, d2, b)
        a, d = join(a, a2), join(d, d2)
        a3 = stage(a, layout, zf, 2)
        b1 = stage(b, layout, zf, 0)
        a3, b1 = together(a3, b1)
        a, b = join(a, a3), join(b, b1)
        a4 = stage(a, layout, zf, 3)
        b2 = stage(b, layout, zf, 1)
        a5 = swap_cores(a, layout)
        a4, b2, a5, d = together(a4, b2, a5, d)
        d3 = stage(d, layout, zl, 2)
        a6 = swap_cores(a4, layout)
        b = join(b, b2)
        b3 = stage(b, layout, zf, 2)
        parts_a = (a, a4, a5, a6)
    else:
        count = 32
        rows = width // count
        whole = lambda w: lax.all_gather(w, AXES, axis=0, tiled=True)
        small_full = lax.all_gather(small, AXES, axis=1, tiled=True)
        bias_full = lax.all_gather(inner_bias, AXES, axis=1, tiled=True)
        tail = jnp.concatenate(
            [
                jnp.pad(small_full.reshape(8, count, rows), ((0, 0), (0, 0), (0, LANES - rows))),
                jnp.pad(
                    bias_full.reshape(1, count, -1),
                    ((0, rows - 9), (0, 0), (0, LANES - bias_full.shape[1] // count)),
                ),
            ],
            axis=0,
        )
        tail = jnp.swapaxes(tail, 0, 1).reshape(width, LANES)
        parts_a = as_blocks(
            jnp.concatenate([whole(query_weight), whole(key_weight), whole(value_weight), tail], axis=1), count
        )
        outer = whole(outer_weight).reshape(count, -1, width)
        extra = outer[:, OUTER_ROWS:]
        third = extra[:, rows:].reshape(count, 8, 3, width // 3)
        third = jnp.swapaxes(third, 1, 2).reshape(width, width // 3)
        parts_b = as_blocks(
            jnp.concatenate(
                [whole(output_weight), whole(inner_weight), extra[:, :rows].reshape(width, width), third], axis=1
            ),
            count,
        )
        parts_d = as_blocks(outer[:, :OUTER_ROWS].reshape(-1, width), count)
        ids = ids_d = jnp.arange(count, dtype=jnp.int32)

    turn = lambda v: jnp.swapaxes(v, 1, 2)
    down = turn(adapter_down_factors)
    up = adapter_up_factors
    qkv, weight, red, small_rows, inner_rows = project(ids, tokens, down, up, parts_a)
    if fast:
        b3, d3, qkv = together(b3, d3, qkv)
        b = join(b, b3)
        b4 = stage(b, layout, zf, 3)
        d = join(d, d3)
        d4 = stage(d, layout, zl, 3)
    step_counter = step[0].astype(f32)
    scalars = jnp.stack([1.0 - beta_one**step_counter, 1.0 - beta_two**step_counter, rate[0]])
    core = jnp.reshape((lax.axis_index(AXES) & layout.core) != 0, (1,)).astype(jnp.int32)
    half = attend(0, document_numbers, qkv)
    ids_d, scalars, core, *half = together(ids_d, scalars, core, *half)
    if fast:
        b5 = swap_cores(after(b, *half), layout)
        d5 = swap_cores(after(d, *half), layout)
    context, attention, inverse = attend(1, document_numbers, qkv, half)
    if fast:
        b4, d4, context = together(b4, d4, context)
        b6 = swap_cores(b4, layout)
        d6 = swap_cores(d4, layout)
        parts_b = (b, b4, b5, b6)
        parts_d = (d, d4, d5, d6)
    activations, grad_mid, grad_context, sums = row_local(
        ids, ids_d, tokens, cotangent, context, small_rows, inner_rows, parts_b, parts_d
    )
    input_grad, keep, send = attend_back(
        core, tokens, qkv, context, grad_context, inverse, attention, up, red, sums, grad_mid, down, weight
    )
    total = keep + swap_cores(send, layout)
    total = exchange(total, layout, layout.x_bits + layout.y_bits)
    total = exchange(total, layout, layout.z_bits)
    other = swap_cores(total, layout)
    gd, gu, gain_grad, shift_grad, pd, pu, dm, dv, um, uv = adamw(
        layout.n,
        scalars,
        core,
        total,
        other,
        down,
        up,
        turn(down_first_moment),
        turn(down_second_moment),
        up_first_moment,
        up_second_moment,
    )
    return (
        activations,
        input_grad,
        turn(gd),
        gu,
        gain_grad,
        shift_grad,
        turn(pd),
        pu,
        turn(dm),
        turn(dv),
        um,
        uv,
    )


def solution(mesh):
    rows = P(AXES, None)
    columns = P(None, AXES)
    in_specs = (
        (rows,) * 8
        + (columns, P(AXES), columns, columns)
        + (P(),) * 8
        + (rows,)
    )
    out_specs = (rows, rows) + (P(),) * 10
    return jax.shard_map(
        functools.partial(per_device, Layout(mesh)),
        mesh=mesh,
        in_specs=in_specs,
        out_specs=out_specs,
        check_vma=False,
    )
```
